32 devices in a mesh: dp: 8 (over y, x, core), seq: 4 (over z).
Axes of the slice: x: 2, y: 2, z: 4, core: 2. Of those that a mesh axis runs over, the one named last changes fastest.
Arguments:
- inputs: bfloat16 [16, 2048, 1024], P('dp', 'seq'), may hold values from -8 to 8
- w_qkv: bfloat16 [1024, 3072], replicated, may hold values from -0.1875 to 0.1875
- w_out: bfloat16 [1024, 1024], replicated, may hold values from -0.75 to 0.75
- w_gate_up: bfloat16 [1024, 5504], replicated, may hold values from -0.1875 to 0.1875
- w_down: bfloat16 [1024, 2752], replicated, may hold values from -0.15625 to 0.15625
- gain_attn: float32 [1024], replicated, may hold values from 0.5 to 1.5
- gain_mlp: float32 [1024], replicated, may hold values from 0.5 to 1.5
- doc_start: int32 [16, 2048], P('dp', 'seq'), may hold values from 0 to 2047, as said below
- cotangent: bfloat16 [16, 2048, 1024], P('dp', 'seq'), may hold values from -8 to 8
Outputs:
- outputs: bfloat16 [16, 2048, 1024], P('dp', 'seq')
- grad_inputs: float32 [16, 2048, 1024], P('dp', 'seq')
- grad_qkv: float32 [1024, 3072], P('seq')
- grad_out: float32 [1024, 1024], P('seq')
- grad_gate_up: float32 [1024, 5504], P('seq')
- grad_down: float32 [1024, 2752], P('seq')
- grad_gain_attn: float32 [1024], P('seq')
- grad_gain_mlp: float32 [1024], P('seq')
The draws below stay inside these ranges and needn't reach their ends.
Inputs may be any that keep to these rules, and one draw needn't show every extreme that they name: doc_start[r, 0] = 0, and doc_start[r, i] is either i or doc_start[r, i - 1]. Of the 2 rows of each index of dp, one holds a single document from some position below 512 to the row's end.
All inputs are finite; a program needn't handle non-finite values.
Results may differ from the reference program's by a relative error of at most 0.019.
Values may be sent and summed in bfloat16 or wider, within the bound.
No kernel may reach another device: no remote copies, remote signals or barrier semaphores. Data moves between devices by JAX's collectives and lax.ppermute only.
A program may use at most 320 MiB of HBM per device.

```python
import jax
import jax.numpy as jnp
from jax import lax

D = 1024
HEADS = 16
HEAD_DIM = 64
FF = 2752
WINDOW = 64
SEQLEN = 2048
GROUP = 512
ROWS = 2
ALLROWS = 16
N_DP = 8


def draw_doc_start(key, part):
    key = jax.random.fold_in(key, 7)
    mark_key, row_key = jax.random.split(key)
    marks = jax.random.randint(mark_key, (ALLROWS, SEQLEN), 0, 4 * WINDOW) == 0
    chosen = jax.random.randint(row_key, (N_DP,), 0, ROWS)
    row_ids = jnp.arange(ALLROWS, dtype=jnp.int32)
    whole = row_ids % ROWS == chosen[row_ids // ROWS]
    positions = jnp.arange(SEQLEN, dtype=jnp.int32)
    kept = marks & (~whole[:, None] | (positions[None, :] < GROUP))
    kept = kept | (positions[None, :] == 0)
    starts = jnp.where(kept, positions[None, :], 0)
    return lax.cummax(starts, axis=1).astype(jnp.int32)


def spiked(array, stream_key, source, target, parts, factor):
    def block_of(dim):
        return (jnp.arange(array.shape[dim]) // (array.shape[dim] // parts)).reshape((-1,) + (1,) * (array.ndim - 1 - dim))

    one_side = jax.random.permutation(stream_key, parts)[block_of(target)]
    far = (block_of(target) + parts // 2) % parts
    return jnp.where((block_of(source) == one_side) | (block_of(source) == far), factor * array, array)


def block_scale(key, extent, cuts, least, top_value):
    loudness, own = 1.0, jax.random.fold_in(key, 6)
    for dim, parts in cuts:
        draws = jnp.exp(jax.random.uniform(jax.random.fold_in(own, dim), (parts,), jnp.float32, least / len(cuts), top_value / len(cuts)))
        loudness = loudness * jnp.repeat(draws, extent[dim] // parts).reshape([-1 if axis == dim else 1 for axis in range(len(extent))])
    return loudness


def normal_values(own_key, extent, spread, most, pieces=(), kind=jnp.bfloat16):
    values = spread * jax.random.normal(own_key, extent, jnp.float32)
    if pieces:
        values = values * block_scale(own_key, extent, pieces, -0.22, 0.18)
    return jnp.clip(values, -most, most).astype(kind)


def gaussian_with(stream_key, dims, scale, reach, cuts, heavy, kind=jnp.bfloat16):
    values = scale * jax.random.normal(stream_key, dims, jnp.float32)
    if cuts:
        values = values * block_scale(stream_key, dims, cuts, -0.22, 0.18)
    return jnp.clip(spiked(values, jax.random.fold_in(stream_key, 3), *heavy), -reach, reach).astype(kind)


def setup_inputs(seed: int = 0) -> dict:
    splits = jax.random.split(jax.random.key(seed), 10)
    return {
        "inputs": gaussian_with(splits[0], (ALLROWS, SEQLEN, D), 1.0, 8.0, ((0, 8), (1, 4)), (1, 2, 4, 2.0)),
        "w_qkv": normal_values(splits[1], (D, 3 * D), D ** -0.5, 0.1875),
        "w_out": normal_values(splits[2], (D, D), (D // 16) ** -0.5, 0.75),
        "w_gate_up": normal_values(splits[3], (D, 2 * FF), D ** -0.5, 0.1875),
        "w_down": normal_values(splits[4], (D, FF), (FF // 2) ** -0.5, 0.15625),
        "gain_attn": jnp.clip(1.0 + 0.1 * jax.random.normal(splits[5], (D,), jnp.float32), 0.5, 1.5),
        "gain_mlp": jnp.clip(1.0 + 0.1 * jax.random.normal(splits[6], (D,), jnp.float32), 0.5, 1.5),
        "doc_start": draw_doc_start(jax.random.fold_in(splits[9], 71), 0),
        "cotangent": gaussian_with(splits[8], (ALLROWS, SEQLEN, D), 1.0, 8.0, ((0, 8), (1, 4)), (1, 2, 4, 2.0)),
    }


@jax.custom_vjp
def low(v):
    return lax.optimization_barrier(v.astype(jnp.bfloat16)).astype(jnp.float32)

@jax.custom_vjp
def low_back(v):
    return v

def low_keep(v):
    return (low(v), None)

def low_pass(kept, grad):
    return (grad,)

def back_keep(v):
    return (v, None)

def back_low(kept, grad):
    return (low(grad),)
low.defvjp(low_keep, low_pass)
low_back.defvjp(back_keep, back_low)
epsilon = 1e-05
masked_value = -1e+30

def product(left, right):
    return jnp.dot(left, right, precision=lax.Precision.HIGHEST, preferred_element_type=jnp.float32)

def rms_norm(values, gain):
    return values * lax.rsqrt(lax.optimization_barrier(jnp.mean(values * values, axis=-1, keepdims=True)) + epsilon) * gain

def with_previous(blocks):
    empty = jnp.zeros_like(blocks[:1])
    earlier = jnp.concatenate([empty, blocks[:-1]], axis=0)
    return jnp.concatenate([earlier, blocks], axis=1)

def attention(queries, keys, values, starts):
    blocks = SEQLEN // WINDOW
    shape = (blocks, WINDOW, HEADS, HEAD_DIM)
    query_blocks = queries.reshape(shape)
    key_blocks = with_previous(keys.reshape(shape))
    value_blocks = with_previous(values.reshape(shape))
    scores = jnp.einsum('bqhe,bkhe->bhqk', query_blocks, key_blocks, precision=lax.Precision.HIGHEST) * HEAD_DIM ** (-0.5)
    scores = low_back(scores)
    positions = jnp.arange(SEQLEN, dtype=jnp.int32).reshape(blocks, WINDOW)
    key_pos = positions[:, :1] - WINDOW + jnp.arange(2 * WINDOW, dtype=jnp.int32)[None, :]
    start_blocks = starts.reshape(blocks, WINDOW)
    allowed = (key_pos[:, None, :] >= start_blocks[:, :, None]) & (key_pos[:, None, :] <= positions[:, :, None])
    allowed = allowed & (positions[:, :, None] - key_pos[:, None, :] <= WINDOW)
    scores = jnp.where(allowed[:, None], scores, masked_value)
    weights = low(jax.nn.softmax(scores, axis=-1))
    mixed = jnp.einsum('bhqk,bkhe->bqhe', weights, value_blocks, precision=lax.Precision.HIGHEST)
    return mixed.reshape(SEQLEN, HEADS * HEAD_DIM)

def layer(row, w_qkv, w_out, w_gate_up, w_down, gain_attn, gain_mlp, starts):
    width = HEADS * HEAD_DIM
    normed_one = low(rms_norm(row, gain_attn))
    qkv_all = low(low_back(product(normed_one, w_qkv)))
    attended = attention(qkv_all[:, :width], qkv_all[:, width:2 * width], qkv_all[:, 2 * width:], starts)
    attended = low(low_back(attended))
    resid = row + low_back(product(attended, w_out))
    normed_two = low(rms_norm(resid, gain_mlp))
    gate_up = low_back(product(normed_two, w_gate_up))
    hidden = low(jax.nn.silu(gate_up[:, :FF]) * gate_up[:, FF:])
    return resid + low_back(product(hidden, w_down.T))

def reference(inputs, w_qkv, w_out, w_gate_up, w_down, gain_attn, gain_mlp, doc_start, cotangent):
    params = tuple((matrix.astype(jnp.float32) for matrix in (w_qkv, w_out, w_gate_up, w_down, gain_attn, gain_mlp)))

    def one_row(totals, item):
        row, starts, row_grad = item

        def forward(row_in, p_qkv, p_out, p_gate_up, p_down, p_gain_one, p_gain_two):
            return layer(row_in, p_qkv, p_out, p_gate_up, p_down, p_gain_one, p_gain_two, starts)
        result, pull = jax.vjp(forward, row.astype(jnp.float32), *params)
        grads = pull(row_grad.astype(jnp.float32))
        totals = tuple((total + grad_part for total, grad_part in zip(totals, grads[1:])))
        return (totals, (result.astype(jnp.bfloat16), grads[0]))
    zeros = tuple((jnp.zeros_like(matrix) for matrix in params))
    totals, (outputs, grad_inputs) = lax.scan(one_row, zeros, (inputs, doc_start, cotangent))
    return (outputs, grad_inputs, totals[0], totals[1], totals[2], totals[3], totals[4], totals[5])
```

```python
import jax
import jax.numpy as jnp
from jax import lax
from jax.sharding import PartitionSpec as P

HEADS = 16
HEAD_DIM = 64
FF = 2752
WINDOW = 64


epsilon = 1e-05
masked_value = -1e30


def shifted(value, axis, steps):
    count = lax.axis_size(axis)
    leading, last = (max(0, -steps), min(count, count - steps))
    return lax.ppermute(value, axis, [(source, source + steps) for source in range(leading, last)])


def contract(left, right, left_dim, right_dim):
    return lax.dot_general(
        left, right, (((left_dim,), (right_dim,)), ((), ())), preferred_element_type=jnp.float32
    )


def masked_scores(queries, keys, allowed, scale):
    scores = (
        jnp.einsum("rqhe,rkhe->rhqk", queries, keys, preferred_element_type=jnp.float32) * scale
    )
    return jnp.where(allowed[:, None], scores, masked_value)


def norm_back(grad_norm, values, inv_rms, gain):
    scaled = grad_norm * gain
    input_grad = inv_rms * scaled - values * inv_rms**3 * jnp.mean(
        scaled * values, axis=-1, keepdims=True
    )
    return input_grad


def log2(count):
    return count.bit_length() - 1


def stage_orders(n_dp, n_seq):
    dp = [("dp", bit) for bit in range(1, log2(n_dp))]
    seq = [("seq", bit) for bit in range(log2(n_seq))]
    return dp + seq, seq[:1] + dp[::-1] + seq[1:]


def swap_pairs(n_dp, n_seq, steps):
    pairs = []
    for d in range(n_dp):
        for s in range(n_seq):
            axis, bit = steps[d % 2]
            there = (d ^ (1 << bit), s) if axis == "dp" else (d, s ^ (1 << bit))
            pairs.append((d * n_seq + s, there[0] * n_seq + there[1]))
    return pairs


def swap(value, steps):
    n_dp, n_seq = lax.axis_size("dp"), lax.axis_size("seq")
    return lax.ppermute(value, ("dp", "seq"), swap_pairs(n_dp, n_seq, steps))


def bit_of(step):
    axis, bit = step
    return (lax.axis_index(axis) >> bit) & 1


def own_bit(steps):
    core = lax.axis_index("dp") & 1
    return jnp.where(core == 0, bit_of(steps[0]), bit_of(steps[1]))


CORE = (("dp", 0), ("dp", 0))


def pick(value, index):
    return lax.dynamic_index_in_dim(value, index, axis=0, keepdims=False)


def scatter_sum(grad):
    n_dp, n_seq = lax.axis_size("dp"), lax.axis_size("seq")
    orders = stage_orders(n_dp, n_seq)
    dims = [("seq", bit) for bit in reversed(range(log2(n_seq)))]
    dims += [("dp", bit) for bit in reversed(range(1, log2(n_dp)))]
    rows, columns = grad.shape
    part = rows // (n_dp * n_seq)
    cut = grad.reshape((2,) * len(dims) + (2, part, columns))
    core = lax.axis_index("dp") & 1
    halves = []
    for which in range(2):
        half = lax.index_in_dim(cut, which, axis=len(dims), keepdims=False)
        order = [dims.index(step) for step in orders[which]]
        halves.append(half.transpose(order + [len(dims), len(dims) + 1]))
    first = jnp.where(core == 0, halves[1], halves[0])
    kept = jnp.where(core == 0, halves[0], halves[1])
    value = add(kept, swap(first, CORE))
    for steps in zip(*orders):
        bit = own_bit(steps)
        got = swap(pick(value, 1 - bit), steps)
        value = add(pick(value, bit), got)
    return value


def add(left, right):
    return (left.astype(jnp.float32) + right.astype(jnp.float32)).astype(jnp.bfloat16)


def gather_share(value):
    n_dp, n_seq = lax.axis_size("dp"), lax.axis_size("seq")
    orders = stage_orders(n_dp, n_seq)
    dp_orders = [[step for step in order if step[0] == "dp"] for order in orders]
    part, columns = value.shape
    for steps in zip(*(order[::-1] for order in dp_orders)):
        bit = own_bit(steps)
        got = swap(value, steps)
        value = jnp.stack([jnp.where(bit == 0, value, got), jnp.where(bit == 0, got, value)])
    got = swap(value, CORE)
    core = lax.axis_index("dp") & 1
    halves = []
    for which in range(2):
        half = jnp.where(core == which, value, got)
        dims = [("dp", bit) for bit in reversed(range(1, log2(n_dp)))]
        order = [dp_orders[which].index(step) for step in dims]
        halves.append(half.transpose(order + [len(dims), len(dims) + 1]))
    whole = jnp.stack(halves, axis=len(dp_orders[0]))
    return whole.reshape(n_dp * part, columns).astype(jnp.float32)


def per_device(inputs, w_qkv, w_out, w_gate_up, w_down, gain_attn, gain_mlp, doc_start, cotangent):
    rows, group, width = inputs.shape
    tokens = rows * group
    scale = HEAD_DIM ** (-0.5)
    first_pos = lax.axis_index("seq") * group
    query_pos = first_pos + jnp.arange(group, dtype=jnp.int32)
    key_pos = first_pos - WINDOW + jnp.arange(WINDOW + group, dtype=jnp.int32)
    allowed = (key_pos[None, None, :] >= doc_start[:, :, None]) & (
        key_pos[None, None, :] <= query_pos[None, :, None]
    )
    allowed = allowed & (query_pos[None, :, None] - key_pos[None, None, :] <= WINDOW)
    flat = inputs.reshape(tokens, width).astype(jnp.float32)
    inv_one = lax.rsqrt(jnp.mean(flat * flat, axis=-1, keepdims=True) + epsilon)
    normed_one = (flat * inv_one * gain_attn).astype(jnp.bfloat16)
    qkv_all = jnp.dot(normed_one, w_qkv, preferred_element_type=jnp.float32).astype(jnp.bfloat16)
    queries = qkv_all[:, :width].reshape(rows, group, HEADS, HEAD_DIM)
    own_kv = qkv_all[:, width:].reshape(rows, group, 2 * width)
    rim_kv = shifted(own_kv[:, group - WINDOW :], "seq", 1)
    both_kv = jnp.concatenate([rim_kv, own_kv], axis=1)
    keys = both_kv[..., :width].reshape(rows, WINDOW + group, HEADS, HEAD_DIM)
    values = both_kv[..., width:].reshape(rows, WINDOW + group, HEADS, HEAD_DIM)
    scores = masked_scores(queries, keys, allowed, scale)
    row_top = jnp.max(scores, axis=-1, keepdims=True)
    log_total = row_top + jnp.log(jnp.sum(jnp.exp(scores - row_top), axis=-1, keepdims=True))
    probs = jnp.exp(scores - log_total).astype(jnp.bfloat16)
    attended = jnp.einsum("rhqk,rkhe->rqhe", probs, values, preferred_element_type=jnp.float32)
    attended = attended.reshape(tokens, width).astype(jnp.bfloat16)
    resid = flat + jnp.dot(attended, w_out, preferred_element_type=jnp.float32)
    inv_two = lax.rsqrt(jnp.mean(resid * resid, axis=-1, keepdims=True) + epsilon)
    normed_two = (resid * inv_two * gain_mlp).astype(jnp.bfloat16)
    gate_up = jnp.dot(normed_two, w_gate_up, preferred_element_type=jnp.float32)
    gate_act = gate_up[:, :FF]
    up_act = gate_up[:, FF:]
    sigma = jax.nn.sigmoid(gate_act)
    silu_gate = gate_act * sigma
    hidden = (silu_gate * up_act).astype(jnp.bfloat16)
    outputs = (
        (resid + contract(hidden, w_down, 1, 1)).astype(jnp.bfloat16).reshape(rows, group, width)
    )
    grad_rows = cotangent.reshape(tokens, width)
    grad_down = contract(grad_rows, hidden, 0, 0)
    grad_hidden = jnp.dot(grad_rows, w_down, preferred_element_type=jnp.float32)
    grad_gate = grad_hidden * up_act * sigma * (1.0 + gate_act * (1.0 - sigma))
    grad_up = grad_hidden * silu_gate
    grad_gu = jnp.concatenate([grad_gate, grad_up], axis=1).astype(jnp.bfloat16)
    grad_gate = contract(normed_two, grad_gu[:, :FF], 0, 0)
    grad_up = contract(normed_two, grad_gu[:, FF:], 0, 0)
    grad_resid_in = norm_back(
        contract(grad_gu, w_gate_up, 1, 1), resid, inv_two, gain_mlp
    )
    grad_resid = grad_rows.astype(jnp.float32) + grad_resid_in
    grad_branch = grad_resid.astype(jnp.bfloat16)
    grad_out = contract(attended, grad_branch, 0, 0)
    grad_attended = (
        contract(grad_branch, w_out, 1, 1)
        .astype(jnp.bfloat16)
        .reshape(rows, group, HEADS, HEAD_DIM)
    )
    prob_full = jnp.exp(masked_scores(queries, keys, allowed, scale) - log_total)
    grad_probs = jnp.einsum(
        "rqhe,rkhe->rhqk", grad_attended, values, preferred_element_type=jnp.float32
    )
    weighted = jnp.sum(prob_full * grad_probs, axis=-1, keepdims=True)
    grad_scores = (prob_full * (grad_probs - weighted)).astype(jnp.bfloat16)
    grad_queries = (
        jnp.einsum("rhqk,rkhe->rqhe", grad_scores, keys, preferred_element_type=jnp.float32) * scale
    )
    grad_keys = (
        jnp.einsum("rhqk,rqhe->rkhe", grad_scores, queries, preferred_element_type=jnp.float32)
        * scale
    )
    grad_values = jnp.einsum(
        "rhqk,rqhe->rkhe", probs, grad_attended, preferred_element_type=jnp.float32
    )
    grad_kv = jnp.concatenate(
        [
            grad_keys.reshape(rows, WINDOW + group, width),
            grad_values.reshape(rows, WINDOW + group, width),
        ],
        axis=-1,
    )
    returned = shifted(grad_kv[:, :WINDOW].astype(jnp.bfloat16), "seq", -1).astype(jnp.float32)
    own_grad = grad_kv[:, WINDOW:]
    own_grad = jnp.concatenate(
        [own_grad[:, : group - WINDOW], own_grad[:, group - WINDOW :] + returned], axis=1
    )
    grad_qkv_rows = jnp.concatenate(
        [grad_queries.reshape(tokens, width), own_grad.reshape(tokens, 2 * width)], axis=1
    ).astype(jnp.bfloat16)
    grad_qkv = contract(normed_one, grad_qkv_rows, 0, 0)
    grad_flat = norm_back(
        contract(grad_qkv_rows, w_qkv, 1, 1), flat, inv_one, gain_attn
    )
    grad_inputs = (grad_resid + grad_flat).reshape(rows, group, width)
    shares = [
        scatter_sum(grad.astype(jnp.bfloat16))
        for grad in (grad_down, grad_gate, grad_up, jnp.concatenate([grad_out, grad_qkv], axis=1))
    ]
    total_down, total_gate, total_up, total_rest = [gather_share(share) for share in shares]
    total_out, total_qkv = total_rest[:, :width], total_rest[:, width:]
    total_gate_up = jnp.concatenate([total_gate, total_up], axis=1)
    kept = total_qkv.shape[0]
    first_row = lax.axis_index("seq") * kept

    def gain_total(total, weight, gain):
        mine = lax.dynamic_slice_in_dim(weight, first_row, kept, axis=0).astype(jnp.float32)
        return jnp.sum(total * mine, axis=1) / lax.dynamic_slice_in_dim(gain, first_row, kept)

    return (
        outputs,
        grad_inputs,
        total_qkv,
        total_out,
        total_gate_up,
        total_down,
        gain_total(total_qkv, w_qkv, gain_attn),
        gain_total(total_gate_up, w_gate_up, gain_mlp),
    )


def solution(mesh):
    in_specs = (
        P("dp", "seq", None),
        P(),
        P(),
        P(),
        P(),
        P(),
        P(),
        P("dp", "seq"),
        P("dp", "seq", None),
    )
    out_specs = (
        P("dp", "seq", None),
        P("dp", "seq", None),
        P("seq", None),
        P("seq", None),
        P("seq", None),
        P("seq", None),
        P("seq"),
        P("seq"),
    )
    return jax.shard_map(
        per_device, mesh=mesh, in_specs=in_specs, out_specs=out_specs, check_vma=False
    )
```

```python
import functools
import jax
import jax.numpy as jnp
import numpy as np
from jax import lax
from jax.experimental import pallas as pl
from jax.experimental.pallas import tpu as pltpu
from jax.sharding import PartitionSpec as P

HEADS = 16
HEAD_DIM = 64
FF = 2752
WINDOW = 64
LANES = 128
epsilon = 1e-05
masked_value = -1e30
F32 = jnp.float32
BF16 = jnp.bfloat16
VMEM_LIMIT = 56 * 1024 * 1024


def dot(left, right, left_dim=1, right_dim=0):
    return lax.dot_general(
        left, right, (((left_dim,), (right_dim,)), ((), ())), preferred_element_type=F32
    )


def params():
    return pltpu.CompilerParams(vmem_limit_bytes=VMEM_LIMIT)


def cost(flops, nbytes):
    return pl.CostEstimate(flops=int(flops), bytes_accessed=int(nbytes), transcendentals=0)


def store_slabs(out_ref, value, places_ref, first, slab, columns=slice(None)):
    for k in range(value.shape[0] // slab):
        row = pl.multiple_of(places_ref[first + k] * slab, slab)
        out_ref[pl.ds(row, slab), columns] = value[k * slab : (k + 1) * slab]


def head_masks(rows):
    lane = lax.broadcasted_iota(jnp.int32, (rows, LANES), 1)
    return lane < HEAD_DIM


def two_heads(value, low):
    zero = jnp.zeros_like(value)
    return jnp.concatenate([jnp.where(low, value, zero), jnp.where(low, zero, value)], axis=0)


def key_window(own_ref, rim_ref, row, block, group, size):
    if block == 0:
        rim = rim_ref[row * WINDOW : (row + 1) * WINDOW, :]
        return jnp.concatenate([rim, own_ref[row * group : row * group + size, :]], axis=0)
    start = row * group + block * size - WINDOW
    return own_ref[start : start + size + WINDOW, :]


def attend_kernel(places_ref, first_ref, starts_ref, q_ref, k_ref, v_ref, kr_ref, vr_ref,
                  att_ref, attT_ref, probs_ref, bias_ref, *, rows, group, size, slab):
    pair = pl.program_id(0)
    blocks = group // size

    @pl.when(pair == 0)
    def _():
        for row in range(rows):
            for block in range(blocks):
                key = lax.broadcasted_iota(jnp.int32, (size + WINDOW, size), 0) - WINDOW
                query = lax.broadcasted_iota(jnp.int32, (size + WINDOW, size), 1)
                begin = starts_ref[row : row + 1, block * size : (block + 1) * size]
                begin = begin - first_ref[0] - block * size
                allowed = (key >= begin) & (key <= query) & (query - key <= WINDOW)
                bias = jnp.where(allowed, 0.0, masked_value).astype(F32)
                at = row * blocks + block
                bias_ref[at, :, :size] = bias
                bias_ref[at, :, size:] = bias

    low = head_masks(size)
    for row in range(rows):
        for block in range(blocks):
            at = row * blocks + block
            here = slice(row * group + block * size, row * group + (block + 1) * size)
            queries = q_ref[here, :] * jnp.asarray(HEAD_DIM ** (-0.5), BF16)
            keys = key_window(k_ref, kr_ref, row, block, group, size)
            values = key_window(v_ref, vr_ref, row, block, group, size)
            scores = dot(keys, two_heads(queries, low), 1, 1) + bias_ref[at]
            top = jnp.max(scores, axis=0, keepdims=True)
            weights = jnp.exp(scores - top)
            total = jnp.sum(weights, axis=0, keepdims=True)
            probs = (weights * (1.0 / total)).astype(BF16)
            probs_ref[0, at] = probs
            mixed = dot(values, probs, 0, 0)
            row_id = lax.broadcasted_iota(jnp.int32, (LANES, size), 0)
            mixed = jnp.where(row_id < HEAD_DIM, mixed[:, :size], mixed[:, size:])
            att_ref[here, :] = mixed.T.astype(BF16)
            store_slabs(attT_ref, mixed.astype(BF16), places_ref, pair * (LANES // slab), slab, here)


def attend(qkv, kv_rim, doc_start, first_pos, places, slab):
    rows, group = doc_start.shape
    tokens, width = qkv.shape[0], qkv.shape[1] // 3
    rim = kv_rim.shape[0]
    size = min(128, group)
    pairs = width // LANES
    count = rows * (group // size)
    grid_spec = pltpu.PrefetchScalarGridSpec(
        num_scalar_prefetch=2,
        grid=(pairs,),
        in_specs=[
            pl.BlockSpec((rows, group), lambda j, *_: (0, 0)),
            pl.BlockSpec((tokens, LANES), lambda j, *_: (0, j)),
            pl.BlockSpec((tokens, LANES), lambda j, *_: (0, pairs + j)),
            pl.BlockSpec((tokens, LANES), lambda j, *_: (0, 2 * pairs + j)),
            pl.BlockSpec((rim, LANES), lambda j, *_: (0, j)),
            pl.BlockSpec((rim, LANES), lambda j, *_: (0, pairs + j)),
        ],
        out_specs=[
            pl.BlockSpec((tokens, LANES), lambda j, *_: (0, j)),
            pl.BlockSpec((width, tokens), lambda j, *_: (0, 0)),
            pl.BlockSpec((1, count, size + WINDOW, 2 * size), lambda j, *_: (j, 0, 0, 0)),
        ],
        scratch_shapes=[pltpu.VMEM((count, size + WINDOW, 2 * size), F32)],
    )
    return pl.pallas_call(
        functools.partial(attend_kernel, rows=rows, group=group, size=size, slab=slab),
        grid_spec=grid_spec,
        out_shape=[
            jax.ShapeDtypeStruct((tokens, width), BF16),
            jax.ShapeDtypeStruct((width, tokens), BF16),
            jax.ShapeDtypeStruct((pairs, count, size + WINDOW, 2 * size), BF16),
        ],
        compiler_params=params(),
        cost_estimate=cost(6e9, 16e6),
        name="attend",
    )(places, first_pos, doc_start, qkv, qkv, qkv, kv_rim, kv_rim)


def attend_back_kernel(q_ref, k_ref, v_ref, kr_ref, vr_ref, probs_ref, da_ref,
                       dqkv_ref, drim_ref, *, rows, group, size):
    blocks = group // size
    low = head_masks(size)
    scale = HEAD_DIM ** (-0.5)
    for row in range(rows):
        late_k = late_v = None
        for block in range(blocks):
            at = row * blocks + block
            start = row * group + block * size
            here = slice(start, start + size)
            queries = two_heads(q_ref[here, :] * jnp.asarray(scale, BF16), low)
            grads = two_heads(da_ref[here, :], low)
            keys = key_window(k_ref, kr_ref, row, block, group, size)
            values = key_window(v_ref, vr_ref, row, block, group, size)
            probs = probs_ref[0, at]
            wide = probs.astype(F32)
            part = wide * dot(values, grads, 1, 1)
            dscores = (part - wide * jnp.sum(part, axis=0, keepdims=True)).astype(BF16)
            dk = dot(dscores, queries)
            dv = dot(probs, grads)
            dq = dot(keys, dscores, 0, 0)
            row_id = lax.broadcasted_iota(jnp.int32, (LANES, size), 0)
            dq = jnp.where(row_id < HEAD_DIM, dq[:, :size], dq[:, size:]) * scale
            dqkv_ref[0, here, :] = dq.T.astype(BF16)
            for kind, grad, late in ((1, dk, late_k), (2, dv, late_v)):
                early = grad[:WINDOW]
                if block == 0:
                    drim_ref[kind - 1, row * WINDOW : (row + 1) * WINDOW, :] = early.astype(BF16)
                else:
                    dqkv_ref[kind, start - WINDOW : start, :] = (late + early).astype(BF16)
                if size > WINDOW:
                    dqkv_ref[kind, start : start + size - WINDOW, :] = grad[WINDOW:size].astype(BF16)
            late_k, late_v = dk[size:], dv[size:]
        end = (row + 1) * group
        dqkv_ref[1, end - WINDOW : end, :] = late_k.astype(BF16)
        dqkv_ref[2, end - WINDOW : end, :] = late_v.astype(BF16)


def attend_back(qkv, kv_rim, probs, grad_att, rows, group):
    tokens, width = grad_att.shape
    rim = kv_rim.shape[0]
    size = min(128, group)
    pairs = width // LANES
    count = rows * (group // size)
    return pl.pallas_call(
        functools.partial(attend_back_kernel, rows=rows, group=group, size=size),
        grid=(pairs,),
        in_specs=[
            pl.BlockSpec((tokens, LANES), lambda j: (0, j)),
            pl.BlockSpec((tokens, LANES), lambda j: (0, pairs + j)),
            pl.BlockSpec((tokens, LANES), lambda j: (0, 2 * pairs + j)),
            pl.BlockSpec((rim, LANES), lambda j: (0, j)),
            pl.BlockSpec((rim, LANES), lambda j: (0, pairs + j)),
            pl.BlockSpec((1, count, size + WINDOW, 2 * size), lambda j: (j, 0, 0, 0)),
            pl.BlockSpec((tokens, LANES), lambda j: (0, j)),
        ],
        out_specs=[
            pl.BlockSpec((3, tokens, LANES), lambda j: (0, 0, j)),
            pl.BlockSpec((2, rim, LANES), lambda j: (0, 0, j)),
        ],
        out_shape=[
            jax.ShapeDtypeStruct((3, tokens, width), BF16),
            jax.ShapeDtypeStruct((2, rim, width), BF16),
        ],
        compiler_params=params(),
        cost_estimate=cost(10e9, 22e6),
        name="attend_back",
    )(qkv, qkv, qkv, kv_rim, kv_rim, probs, grad_att)


def norm_matmul_kernel(places_ref, x_ref, gain_ref, w_ref, out_ref, normedT_ref, normed_ref, *, slab, step):
    @pl.when(pl.program_id(0) == 0)
    def _():
        tokens = x_ref.shape[0]
        for at in range(0, tokens, step):
            x = x_ref[at : at + step, :].astype(F32)
            inv = lax.rsqrt(jnp.mean(x * x, axis=-1, keepdims=True) + epsilon)
            normed = (x * inv * gain_ref[...]).astype(BF16)
            normed_ref[at : at + step, :] = normed
            store_slabs(normedT_ref, normed.T, places_ref, 0, slab, slice(at, at + step))

    out_ref[...] = dot(normed_ref[...], w_ref[...]).astype(BF16)


def norm_matmul(x, gain, weight, first_column, places, slab):
    tokens, width = x.shape
    columns = weight.shape[1] - first_column
    tile = 512
    skip = first_column // tile
    grid_spec = pltpu.PrefetchScalarGridSpec(
        num_scalar_prefetch=1,
        grid=(columns // tile,),
        in_specs=[
            pl.BlockSpec((tokens, width), lambda j, *_: (0, 0)),
            pl.BlockSpec((1, width), lambda j, *_: (0, 0)),
            pl.BlockSpec((width, tile), lambda j, *_: (0, skip + j)),
        ],
        out_specs=[
            pl.BlockSpec((tokens, tile), lambda j, *_: (0, j)),
            pl.BlockSpec((width, tokens), lambda j, *_: (0, 0)),
        ],
        scratch_shapes=[pltpu.VMEM((tokens, width), BF16)],
    )
    return pl.pallas_call(
        functools.partial(norm_matmul_kernel, slab=slab, step=min(256, tokens)),
        grid_spec=grid_spec,
        out_shape=[
            jax.ShapeDtypeStruct((tokens, columns), BF16),
            jax.ShapeDtypeStruct((width, tokens), BF16),
        ],
        compiler_params=params(),
        cost_estimate=cost(2 * tokens * width * columns, 2 * (tokens + width) * columns),
        name="norm_matmul",
    )(places, x, gain.reshape(1, width), weight)


def turn_kernel(places_ref, x_ref, out_ref, *, slab):
    store_slabs(out_ref, x_ref[...].T, places_ref, 0, slab)


def turn(x, places, slab):
    tokens, width = x.shape
    step = 256
    grid_spec = pltpu.PrefetchScalarGridSpec(
        num_scalar_prefetch=1,
        grid=(tokens // step,),
        in_specs=[pl.BlockSpec((step, width), lambda m, *_: (m, 0))],
        out_specs=pl.BlockSpec((width, step), lambda m, *_: (0, m)),
    )
    return pl.pallas_call(
        functools.partial(turn_kernel, slab=slab),
        grid_spec=grid_spec,
        out_shape=jax.ShapeDtypeStruct((width, tokens), BF16),
        compiler_params=params(),
        cost_estimate=cost(1e9, 4 * tokens * width),
        name="turn",
    )(places, x)


def out_proj_kernel(places_ref, att_ref, w_ref, x_ref, gain_ref, resid_ref, normed_ref, normedT_ref, *, slab):
    resid = x_ref[...].astype(F32) + dot(att_ref[...], w_ref[...])
    resid_ref[...] = resid
    inv = lax.rsqrt(jnp.mean(resid * resid, axis=-1, keepdims=True) + epsilon)
    normed = (resid * inv * gain_ref[...]).astype(BF16)
    normed_ref[...] = normed
    store_slabs(normedT_ref, normed.T, places_ref, 0, slab)


def out_proj(att, w_out, x, gain, places, slab):
    tokens, width = x.shape
    step = 256
    rows = pl.BlockSpec((step, width), lambda m, *_: (m, 0))
    grid_spec = pltpu.PrefetchScalarGridSpec(
        num_scalar_prefetch=1,
        grid=(tokens // step,),
        in_specs=[
            rows,
            pl.BlockSpec((width, width), lambda m, *_: (0, 0)),
            rows,
            pl.BlockSpec((1, width), lambda m, *_: (0, 0)),
        ],
        out_specs=[rows, rows, pl.BlockSpec((width, step), lambda m, *_: (0, m))],
    )
    return pl.pallas_call(
        functools.partial(out_proj_kernel, slab=slab),
        grid_spec=grid_spec,
        out_shape=[
            jax.ShapeDtypeStruct((tokens, width), F32),
            jax.ShapeDtypeStruct((tokens, width), BF16),
            jax.ShapeDtypeStruct((width, tokens), BF16),
        ],
        compiler_params=params(),
        cost_estimate=cost(2 * tokens * width * width, 14 * tokens * width),
        name="out_proj",
    )(places, att, w_out, x, gain.reshape(1, width))


FF_TILE = 256
FF_TILES = -(-FF // FF_TILE)
FF_WIDE = FF_TILES * FF_TILE


def ff_act_kernel(normed_ref, dy_ref, wg_ref, wu_ref, wd_ref, hidden_ref, dgu_ref, *, first, step):
    column = (pl.program_id(0) + first) * FF_TILE + lax.broadcasted_iota(jnp.int32, (step, FF_TILE), 1)
    inside = column < FF
    for at in range(0, normed_ref.shape[0], step):
        here = slice(at, at + step)
        normed = normed_ref[here, :]
        gate = dot(normed, wg_ref[...])
        up = dot(normed, wu_ref[...])
        back = dot(dy_ref[here, :], wd_ref[...])
        sigma = 1.0 / (1.0 + jnp.exp(-gate))
        silu = gate * sigma
        hidden_ref[here, :] = jnp.where(inside, silu * up, 0.0).astype(BF16)
        dgate = back * up * (sigma * (1.0 + gate * (1.0 - sigma)))
        dgu_ref[0, here, :] = jnp.where(inside, dgate, 0.0).astype(BF16)
        dgu_ref[1, here, :] = jnp.where(inside, back * silu, 0.0).astype(BF16)


def ff_act(normed, dy, w_gate_up, w_up, w_down, first, count):
    tokens, width = normed.shape
    whole = pl.BlockSpec((tokens, width), lambda j: (0, 0))
    tile = pl.BlockSpec((width, FF_TILE), lambda j: (0, first + j))
    wide = count * FF_TILE
    return pl.pallas_call(
        functools.partial(ff_act_kernel, first=first, step=256),
        grid=(count,),
        in_specs=[whole, whole, tile, tile, tile],
        out_specs=[
            pl.BlockSpec((tokens, FF_TILE), lambda j: (0, j)),
            pl.BlockSpec((2, tokens, FF_TILE), lambda j: (0, 0, j)),
        ],
        out_shape=[
            jax.ShapeDtypeStruct((tokens, wide), BF16),
            jax.ShapeDtypeStruct((2, tokens, wide), BF16),
        ],
        compiler_params=params(),
        cost_estimate=cost(6 * tokens * width * wide, 6 * (tokens + width) * wide),
        name="ff_act",
    )(normed, dy, w_gate_up, w_up, w_down)


def norm_back(grad, values, gain):
    inv = lax.rsqrt(jnp.mean(values * values, axis=-1, keepdims=True) + epsilon)
    scaled = grad * gain
    return inv * scaled - values * (inv * inv * inv) * jnp.mean(scaled * values, axis=-1, keepdims=True)


def ff_back_kernel(dgu_ref, wg_ref, wu_ref, dy_ref, resid_ref, gain_ref, w_out_ref,
                   dr_ref, drb_ref, da_ref, acc_ref, *, step):
    tile = pl.program_id(0)

    @pl.when(tile == 0)
    def _():
        acc_ref[...] = jnp.zeros_like(acc_ref)

    for at in range(0, acc_ref.shape[0], step):
        here = slice(at, at + step)
        acc_ref[here, :] += dot(dgu_ref[0, here, :], wg_ref[...], 1, 1) + dot(
            dgu_ref[1, here, :], wu_ref[...], 1, 1
        )

    @pl.when(tile == pl.num_programs(0) - 1)
    def _():
        for at in range(0, acc_ref.shape[0], step):
            here = slice(at, at + step)
            grad = norm_back(acc_ref[here, :], resid_ref[here, :], gain_ref[...])
            grad = dy_ref[here, :].astype(F32) + grad
            dr_ref[here, :] = grad
            branch = grad.astype(BF16)
            drb_ref[here, :] = branch
            da_ref[here, :] = dot(branch, w_out_ref[...], 1, 1).astype(BF16)


def ff_back(dgu, w_gate_up, w_up, dy, resid, gain, w_out):
    tokens, width = dy.shape
    wide = dgu.shape[2]
    whole = pl.BlockSpec((tokens, width), lambda j: (0, 0))
    tile = pl.BlockSpec((width, FF_TILE), lambda j: (0, j))
    return pl.pallas_call(
        functools.partial(ff_back_kernel, step=256),
        grid=(wide // FF_TILE,),
        in_specs=[
            pl.BlockSpec((2, tokens, FF_TILE), lambda j: (0, 0, j)),
            tile,
            tile,
            whole,
            whole,
            pl.BlockSpec((1, width), lambda j: (0, 0)),
            pl.BlockSpec((width, width), lambda j: (0, 0)),
        ],
        out_specs=[whole, whole, whole],
        out_shape=[
            jax.ShapeDtypeStruct((tokens, width), F32),
            jax.ShapeDtypeStruct((tokens, width), BF16),
            jax.ShapeDtypeStruct((tokens, width), BF16),
        ],
        scratch_shapes=[pltpu.VMEM((tokens, width), F32)],
        compiler_params=params(),
        cost_estimate=cost(4 * tokens * width * wide + 2 * tokens * width * width, 10 * tokens * wide),
        name="ff_back",
    )(dgu, w_gate_up, w_up, dy, resid, gain.reshape(1, width), w_out)


def ff_out_kernel(hidden_ref, wd_ref, resid_ref, out_ref, acc_ref, *, step, tile):
    k = pl.program_id(0)
    column = k * tile + lax.broadcasted_iota(jnp.int32, wd_ref.shape, 1)
    weight = jnp.where(column < FF, wd_ref[...], jnp.zeros_like(wd_ref))

    @pl.when(k == 0)
    def _():
        acc_ref[...] = resid_ref[...]

    for at in range(0, acc_ref.shape[0], step):
        here = slice(at, at + step)
        acc_ref[here, :] += dot(hidden_ref[here, :], weight, 1, 1)

    @pl.when(k == pl.num_programs(0) - 1)
    def _():
        out_ref[...] = acc_ref[...].astype(BF16)


def ff_out(hidden, w_down, resid):
    tokens, width = resid.shape
    wide = hidden.shape[1]
    tile = wide // 2
    whole = pl.BlockSpec((tokens, width), lambda j: (0, 0))
    return pl.pallas_call(
        functools.partial(ff_out_kernel, step=256, tile=tile),
        grid=(wide // tile,),
        in_specs=[
            pl.BlockSpec((tokens, tile), lambda j: (0, j)),
            pl.BlockSpec((width, tile), lambda j: (0, j)),
            whole,
        ],
        out_specs=whole,
        out_shape=jax.ShapeDtypeStruct((tokens, width), BF16),
        scratch_shapes=[pltpu.VMEM((tokens, width), F32)],
        compiler_params=params(),
        cost_estimate=cost(2 * tokens * width * wide, 4 * tokens * wide + 6 * tokens * width),
        name="ff_out",
    )(hidden, w_down, resid)


def grad_kernel(left_ref, right_ref, out_ref):
    out_ref[...] = dot(left_ref[...], right_ref[...]).astype(BF16)


def grad_add_kernel(left_ref, right_ref, got_ref, out_ref):
    out_ref[...] = (dot(left_ref[...], right_ref[...]) + got_ref[...].astype(F32)).astype(BF16)


def weight_grad(turned, half, right, got=None, tile=None):
    width, tokens = turned.shape
    kinds, _, columns = right.shape
    tile = tile or columns // 2
    steps = columns // tile
    place = pl.BlockSpec((width // 2, tile), lambda k, j: (0, k * steps + j))
    in_specs = [
        pl.BlockSpec((width // 2, tokens), lambda k, j: (half, 0)),
        pl.BlockSpec((None, tokens, tile), lambda k, j: (k, 0, j)),
    ]
    operands = [turned, right]
    if got is not None:
        in_specs.append(place)
        operands.append(got)
    return pl.pallas_call(
        grad_kernel if got is None else grad_add_kernel,
        grid=(kinds, steps),
        in_specs=in_specs,
        out_specs=place,
        out_shape=jax.ShapeDtypeStruct((width // 2, kinds * columns), BF16),
        compiler_params=params(),
        cost_estimate=cost(tokens * width * kinds * columns, 4 * tokens * kinds * columns),
        name="weight_grad",
    )(*operands)


def grad_qkv_kernel(left_ref, right_ref, left_rim_ref, right_rim_ref, *rest):
    out_ref = rest[-1]

    def put(total):
        if len(rest) == 2:
            total += rest[0][...].astype(F32)
        out_ref[...] = total.astype(BF16)

    kind = pl.program_id(0)

    @pl.when(kind == 0)
    def _():
        put(dot(left_ref[...], right_ref[...]))

    @pl.when(kind > 0)
    def _():
        put(dot(left_ref[...], right_ref[...]) + dot(left_rim_ref[...], right_rim_ref[...]))


def weight_grad_qkv(turned, turned_rim, half, right, right_rim, got=None):
    width, tokens = turned.shape
    rim = turned_rim.shape[1]
    kinds, _, columns = right.shape
    tile = 512
    steps = columns // tile
    place = pl.BlockSpec((width // 2, tile), lambda k, j: (0, k * steps + j))
    in_specs = [
        pl.BlockSpec((width // 2, tokens), lambda k, j: (half, 0)),
        pl.BlockSpec((None, tokens, tile), lambda k, j: (k, 0, j)),
        pl.BlockSpec((width // 2, rim), lambda k, j: (half, 0)),
        pl.BlockSpec((None, rim, tile), lambda k, j: (jnp.maximum(k - 1, 0), 0, j)),
    ]
    operands = [turned, right, turned_rim, right_rim]
    if got is not None:
        in_specs.append(place)
        operands.append(got)
    return pl.pallas_call(
        grad_qkv_kernel,
        grid=(kinds, steps),
        in_specs=in_specs,
        out_specs=place,
        out_shape=jax.ShapeDtypeStruct((width // 2, kinds * columns), BF16),
        compiler_params=params(),
        cost_estimate=cost(tokens * width * kinds * columns, 4 * tokens * kinds * columns),
        name="weight_grad_qkv",
    )(*operands)


def input_grad_kernel(dqkv_ref, w_ref, x_ref, gain_ref, dr_ref, back_ref, out_ref, acc_ref, *, step, rows, group):
    k = pl.program_id(0)

    @pl.when(k == 0)
    def _():
        acc_ref[...] = jnp.zeros_like(acc_ref)

    for at in range(0, acc_ref.shape[0], step):
        here = slice(at, at + step)
        acc_ref[here, :] += dot(dqkv_ref[here, :], w_ref[...], 1, 1)

    @pl.when(k == pl.num_programs(0) - 1)
    def _():
        for at in range(0, acc_ref.shape[0], step):
            here = slice(at, at + step)
            grad = norm_back(acc_ref[here, :], x_ref[here, :].astype(F32), gain_ref[...])
            out_ref[here, :] = grad + dr_ref[here, :]
        for row in range(rows):
            tail = slice((row + 1) * group - WINDOW, (row + 1) * group)
            out_ref[tail, :] += back_ref[row * WINDOW : (row + 1) * WINDOW, :].astype(F32)


def input_grad(dqkv, w_qkv, x, gain, dr, back, rows, group):
    kinds, tokens, width = dqkv.shape
    tile = 512
    steps = width // tile
    whole = pl.BlockSpec((tokens, width), lambda j: (0, 0))
    return pl.pallas_call(
        functools.partial(input_grad_kernel, step=256, rows=rows, group=group),
        grid=(kinds * steps,),
        in_specs=[
            pl.BlockSpec((None, tokens, tile), lambda j: (j // steps, 0, j % steps)),
            pl.BlockSpec((width, tile), lambda j: (0, j)),
            whole,
            pl.BlockSpec((1, width), lambda j: (0, 0)),
            whole,
            pl.BlockSpec((rows * WINDOW, width), lambda j: (0, 0)),
        ],
        out_specs=whole,
        out_shape=jax.ShapeDtypeStruct((tokens, width), F32),
        scratch_shapes=[pltpu.VMEM((tokens, width), F32)],
        compiler_params=params(),
        cost_estimate=cost(2 * tokens * width * kinds * width, 20 * tokens * width),
        name="input_grad",
    )(dqkv, w_qkv, x, gain.reshape(1, width), dr, back)


def log2(count):
    return count.bit_length() - 1


def stage_orders(n_dp, n_seq):
    dp = [("dp", bit) for bit in range(1, log2(n_dp))]
    seq = [("seq", bit) for bit in range(log2(n_seq))]
    return dp + seq, seq[:1] + dp[::-1] + seq[1:]


def row_bits(n_dp, n_seq):
    return [("seq", bit) for bit in reversed(range(log2(n_seq)))] + [
        ("dp", bit) for bit in reversed(range(log2(n_dp)))
    ]


def block_places(n_dp, n_seq):
    bits, orders = row_bits(n_dp, n_seq), stage_orders(n_dp, n_seq)
    count = n_dp * n_seq
    tables = []
    for core in range(2):
        table = []
        for block in range(count):
            value = {step: (block >> (len(bits) - 1 - k)) & 1 for k, step in enumerate(bits)}
            owner = value[("dp", 0)]
            place = 0
            for step in orders[owner]:
                place = place * 2 + value[step]
            table.append(place + (count // 2 if owner == core else 0))
        tables.append(np.array(table, np.int32))
    return tables


def swap_pairs(n_dp, n_seq, steps):
    pairs = []
    for d in range(n_dp):
        for s in range(n_seq):
            axis, bit = steps[d % 2]
            there = (d ^ (1 << bit), s) if axis == "dp" else (d, s ^ (1 << bit))
            pairs.append((d * n_seq + s, there[0] * n_seq + there[1]))
    return pairs


def swap(value, steps):
    n_dp, n_seq = lax.axis_size("dp"), lax.axis_size("seq")
    return lax.ppermute(value, ("dp", "seq"), swap_pairs(n_dp, n_seq, steps))


def bit_of(step):
    axis, bit = step
    return (lax.axis_index(axis) >> bit) & 1


def own_bit(steps):
    core = lax.axis_index("dp") & 1
    return jnp.where(core == 0, bit_of(steps[0]), bit_of(steps[1]))


CORE = (("dp", 0), ("dp", 0))


def pick(value, index):
    return lax.dynamic_index_in_dim(value, index, axis=0, keepdims=False)


def add(left, right):
    return (left.astype(F32) + right.astype(F32)).astype(BF16)


def scatter_sum(value):
    n_dp, n_seq = lax.axis_size("dp"), lax.axis_size("seq")
    rows, columns = value.shape
    for steps in zip(*stage_orders(n_dp, n_seq)):
        rows //= 2
        value = value.reshape(2, rows, columns)
        bit = own_bit(steps)
        got = swap(pick(value, 1 - bit), steps)
        value = add(pick(value, bit), got)
    return value


def gather_share(value):
    n_dp, n_seq = lax.axis_size("dp"), lax.axis_size("seq")
    dp_orders = [[step for step in order if step[0] == "dp"] for order in stage_orders(n_dp, n_seq)]
    part, columns = value.shape
    for steps in zip(*(order[::-1] for order in dp_orders)):
        bit = own_bit(steps)
        got = swap(value, steps)
        value = jnp.stack([jnp.where(bit == 0, value, got), jnp.where(bit == 0, got, value)])
    got = swap(value, CORE)
    core = lax.axis_index("dp") & 1
    dims = [("dp", bit) for bit in reversed(range(1, log2(n_dp)))]
    halves = []
    for which in range(2):
        half = jnp.where(core == which, value, got)
        order = [dp_orders[which].index(step) for step in dims]
        halves.append(half.transpose(order + [len(dims), len(dims) + 1]))
    whole = jnp.stack(halves, axis=len(dims))
    return whole.reshape(n_dp * part, columns)


def place_rows(turned, places):
    count = places.shape[0]
    blocks = turned.reshape((count, turned.shape[0] // count) + turned.shape[1:])
    return jnp.zeros_like(blocks).at[places].set(blocks).reshape(turned.shape)


def shifted(value, axis, steps):
    count = lax.axis_size(axis)
    leading, last = (max(0, -steps), min(count, count - steps))
    return lax.ppermute(value, axis, [(source, source + steps) for source in range(leading, last)])


def per_device(inputs, w_qkv, w_out, w_gate_up, w_down, gain_attn, gain_mlp, doc_start, cotangent):
    n_dp, n_seq = lax.axis_size("dp"), lax.axis_size("seq")
    rows, group, width = inputs.shape
    tokens = rows * group
    core = lax.axis_index("dp") & 1
    first_pos = (lax.axis_index("seq") * group).reshape(1)
    tables = block_places(n_dp, n_seq)
    places = jnp.where(core == 0, tables[0], tables[1])
    slab = width // (n_dp * n_seq)
    if slab % 16 == 0:
        put, turned_in_order = places, lambda turned: turned
    else:
        slab = 32
        put, turned_in_order = jnp.arange(width // slab, dtype=jnp.int32), lambda turned: place_rows(turned, places)
    x = inputs.reshape(tokens, width)
    dy = cotangent.reshape(tokens, width)
    x_rim = shifted(inputs[:, group - WINDOW :], "seq", 1).reshape(rows * WINDOW, width)
    w_up = jnp.pad(w_gate_up[:, FF:], ((0, 0), (0, FF_WIDE - FF)))

    qkv, one_turned = norm_matmul(x, gain_attn, w_qkv, 0, put, slab)
    dy_turned = turn(dy, put, slab)
    kv_rim, rim_turned = norm_matmul(x_rim, gain_attn, w_qkv, width, put, slab)
    att, att_turned, probs = attend(qkv, kv_rim, doc_start, first_pos, put, slab)
    resid, normed_two, two_turned = out_proj(att, w_out, x, gain_mlp, put, slab)
    one_turned, rim_turned, att_turned, two_turned, dy_turned = [
        turned_in_order(turned) for turned in (one_turned, rim_turned, att_turned, two_turned, dy_turned)
    ]
    hidden, dgu = ff_act(normed_two, dy, w_gate_up, w_up, w_down, 0, FF_TILES)

    def summed(grad):
        return scatter_sum(grad(1, swap(grad(0, None), CORE)))

    share_down = summed(lambda half, got: weight_grad(dy_turned, half, hidden[None], got))
    share_gu = summed(lambda half, got: weight_grad(two_turned, half, dgu, got))
    dr, drb, da = ff_back(dgu, w_gate_up, w_up, dy, resid, gain_mlp, w_out)
    share_out = summed(lambda half, got: weight_grad(att_turned, half, drb[None], got))
    dqkv, drim = attend_back(qkv, kv_rim, probs, da, rows, group)

    rim_grad = dot(drim[0], w_qkv[:, width : 2 * width], 1, 1) + dot(drim[1], w_qkv[:, 2 * width :], 1, 1)
    rim_back = norm_back(rim_grad, x_rim.astype(F32), gain_attn[None])
    rim_back = shifted(rim_back.astype(BF16), "seq", -1)
    share_qkv = summed(
        lambda half, got: weight_grad_qkv(one_turned, rim_turned, half, dqkv, drim, got)
    )
    grad_inputs = input_grad(dqkv, w_qkv, x, gain_attn, dr, rim_back, rows, group)
    outputs = ff_out(hidden, w_down, resid)

    total_down = gather_share(share_down)
    total_gu = gather_share(share_gu)
    total_rest = gather_share(jnp.concatenate([share_out, share_qkv], axis=1))
    total_down = total_down[:, :FF].astype(F32)
    total_gate_up = jnp.concatenate([total_gu[:, :FF], total_gu[:, FF_WIDE : FF_WIDE + FF]], axis=1).astype(F32)
    total_out = total_rest[:, :width].astype(F32)
    total_qkv = total_rest[:, width:].astype(F32)
    kept = total_qkv.shape[0]
    first_row = lax.axis_index("seq") * kept

    def gain_total(total, weight, gain):
        mine = lax.dynamic_slice_in_dim(weight, first_row, kept, axis=0).astype(F32)
        return jnp.sum(total * mine, axis=1) / lax.dynamic_slice_in_dim(gain, first_row, kept)

    return (
        outputs.reshape(rows, group, width),
        grad_inputs.reshape(rows, group, width),
        total_qkv,
        total_out,
        total_gate_up,
        total_down,
        gain_total(total_qkv, w_qkv, gain_attn),
        gain_total(total_gate_up, w_gate_up, gain_mlp),
    )


def solution(mesh):
    in_specs = (
        P("dp", "seq", None),
        P(),
        P(),
        P(),
        P(),
        P(),
        P(),
        P("dp", "seq"),
        P("dp", "seq", None),
    )
    out_specs = (
        P("dp", "seq", None),
        P("dp", "seq", None),
        P("seq", None),
        P("seq", None),
        P("seq", None),
        P("seq", None),
        P("seq"),
        P("seq"),
    )
    return jax.shard_map(
        per_device, mesh=mesh, in_specs=in_specs, out_specs=out_specs, check_vma=False
    )
```

```python
import functools
import math

import jax
import jax.numpy as jnp
import numpy as np
from jax import lax
from jax.experimental import pallas as pl
from jax.experimental.pallas import tpu as pltpu
from jax.sharding import PartitionSpec as P

HEADS = 16
HEAD_DIM = 64
FF = 2752
WINDOW = 64
LANES = 128
PAIRS = 2
FF_TILE = 256
FF_TILES = -(-FF // FF_TILE)
FF_CHUNKS = (7, 4)
STEP = 256
epsilon = 1e-05
masked_value = -1e30
F32 = jnp.float32
BF16 = jnp.bfloat16
VMEM_LIMIT = 64 * 1024 * 1024 - 256 * 1024
PER_US = 1.1e9


def dot(left, right, left_dim=1, right_dim=0):
    return lax.dot_general(
        left, right, (((left_dim,), (right_dim,)), ((), ())), preferred_element_type=F32
    )


def launch(kernel, name, grid, scalars, inputs, outputs, scratch=(), us=5, after=()):
    known = len(scalars) + len(inputs)

    def body(*refs):
        kernel(*refs[:known], *refs[known + len(after) :])

    specs = [spec for _, spec in inputs] + [pl.BlockSpec(memory_space=pl.ANY)] * len(after)
    shapes = [pltpu.HBM(shape, kind) for shape, kind, _ in outputs]
    moved = sum(array.size * array.dtype.itemsize for array, _ in inputs)
    moved += sum(math.prod(shape) * np.dtype(kind).itemsize for shape, kind, _ in outputs)
    return pl.pallas_call(
        body,
        grid_spec=pltpu.PrefetchScalarGridSpec(
            num_scalar_prefetch=len(scalars),
            grid=grid,
            in_specs=specs,
            out_specs=[spec for _, _, spec in outputs],
            scratch_shapes=list(scratch),
        ),
        out_shape=shapes,
        compiler_params=pltpu.CompilerParams(vmem_limit_bytes=VMEM_LIMIT),
        cost_estimate=pl.CostEstimate(flops=int(us * PER_US), bytes_accessed=int(moved / 100), transcendentals=0),
        name=name,
    )(*scalars, *[array for array, _ in inputs], *after)


def full(*shape):
    return pl.BlockSpec(shape, lambda *_: (0,) * len(shape))


def store_slabs(out_ref, value, places_ref, first, slab, columns=slice(None)):
    for k in range(value.shape[0] // slab):
        row = pl.multiple_of(places_ref[first + k] * slab, slab)
        out_ref[pl.ds(row, slab), columns] = value[k * slab : (k + 1) * slab]


def side_by_side(ref):
    return jnp.concatenate([ref[k] for k in range(ref.shape[0])], axis=1)


def put_blocks(ref, value, rows=slice(None)):
    for k in range(ref.shape[0]):
        ref[k, rows, :] = value[:, k * LANES : (k + 1) * LANES]

def two_heads(value, low):
    zero = jnp.zeros_like(value)
    return jnp.concatenate([jnp.where(low, value, zero), jnp.where(low, zero, value)], axis=0)


def one_of_two(value, size):
    feature = lax.broadcasted_iota(jnp.int32, (LANES, size), 0)
    return jnp.where(feature < HEAD_DIM, value[:, :size], value[:, size:])


class Spans:
    def __init__(self, rows, group):
        self.rows, self.group = rows, group
        self.size = min(128, group)
        self.blocks = group // self.size
        self.count = rows * self.blocks
        self.window = self.size + WINDOW

    def queries(self, at):
        return slice(at * self.size, (at + 1) * self.size)

    def keys(self, own_ref, rim_ref, pair, at):
        row, block = divmod(at, self.blocks)
        start = at * self.size
        if block == 0:
            rim = rim_ref[pair, row * WINDOW : (row + 1) * WINDOW, :]
            return jnp.concatenate([rim, own_ref[pair, start : start + self.size, :]], axis=0)
        return own_ref[pair, start - WINDOW : start + self.size, :]

    def fill_bias(self, bias_ref, starts_ref, first_ref):
        size = self.size
        key = lax.broadcasted_iota(jnp.int32, (self.window, size), 0) - WINDOW
        query = lax.broadcasted_iota(jnp.int32, (self.window, size), 1)
        near = (key <= query) & (query - key <= WINDOW)
        for at in range(self.count):
            row, block = divmod(at, self.blocks)
            begin = starts_ref[row : row + 1, block * size : (block + 1) * size]
            begin = begin - first_ref[0] - block * size
            bias = jnp.where(near & (key >= begin), 0.0, masked_value).astype(F32)
            bias_ref[at, :, :size] = bias
            bias_ref[at, :, size:] = bias

    def scratch(self, kind):
        return pltpu.VMEM((self.count, self.window, 2 * self.size), kind)


def softmax(scores):
    weights = jnp.exp(scores - jnp.max(scores, axis=0, keepdims=True))
    return weights * (1.0 / jnp.sum(weights, axis=0, keepdims=True))


def attend_kernel(places_ref, first_ref, starts_ref, q_ref, k_ref, v_ref, kr_ref, vr_ref,
                  att_ref, attT_ref, bias_ref, score_ref, probs_ref, *, spans, slab, pairs):
    step = pl.program_id(0)
    size, count = spans.size, spans.count

    @pl.when(step == 0)
    def _():
        spans.fill_bias(bias_ref, starts_ref, first_ref)

    low = lax.broadcasted_iota(jnp.int32, (size, LANES), 1) < HEAD_DIM
    for pair in range(pairs):
        for at in range(count):
            queries = q_ref[pair, spans.queries(at), :] * jnp.asarray(HEAD_DIM ** (-0.5), BF16)
            keys = spans.keys(k_ref, kr_ref, pair, at)
            score_ref[at] = dot(keys, two_heads(queries, low), 1, 1)
        for at in range(count):
            probs_ref[at] = softmax(score_ref[at] + bias_ref[at]).astype(BF16)
        for at in range(count):
            values = spans.keys(v_ref, vr_ref, pair, at)
            mixed = one_of_two(dot(values, probs_ref[at], 0, 0), size)
            att_ref[pair, spans.queries(at), :] = mixed.T.astype(BF16)
            first = (step * pairs + pair) * (LANES // slab)
            store_slabs(attT_ref, mixed.astype(BF16), places_ref, first, slab, spans.queries(at))


def attend(qkv, kv_rim, doc_start, first_pos, places, slab, after=()):
    rows, group = doc_start.shape
    all_pairs, tokens = qkv.shape[0] // 3, qkv.shape[1]
    rim = kv_rim.shape[1]
    spans = Spans(rows, group)
    steps = all_pairs // PAIRS
    own = lambda kind: pl.BlockSpec((PAIRS, tokens, LANES), lambda j, *_: (kind * steps + j, 0, 0))
    edge = lambda kind: pl.BlockSpec((PAIRS, rim, LANES), lambda j, *_: (kind * steps + j, 0, 0))
    width = all_pairs * LANES
    return launch(
        functools.partial(attend_kernel, spans=spans, slab=slab, pairs=PAIRS),
        "attend",
        (steps,),
        [places, first_pos],
        [
            (doc_start, full(rows, group)),
            (qkv, own(0)),
            (qkv, own(1)),
            (qkv, own(2)),
            (kv_rim, edge(0)),
            (kv_rim, edge(1)),
        ],
        [
            ((all_pairs, tokens, LANES), BF16, own(0)),
            ((width, tokens), BF16, full(width, tokens)),
        ],
        [spans.scratch(F32), spans.scratch(F32), spans.scratch(BF16)],
        us=10.5,
        after=after,
    )


def attend_back_kernel(first_ref, starts_ref, q_ref, k_ref, v_ref, kr_ref, vr_ref, da_ref,
                       dqkv_ref, drim_ref,
                       bias_ref, score_ref, grad_ref, probs_ref, dscore_ref, *, spans, pairs):
    size, count = spans.size, spans.count

    @pl.when(pl.program_id(0) == 0)
    def _():
        spans.fill_bias(bias_ref, starts_ref, first_ref)

    low = lax.broadcasted_iota(jnp.int32, (size, LANES), 1) < HEAD_DIM
    scale = HEAD_DIM ** (-0.5)

    def scaled_queries(pair, at):
        return two_heads(q_ref[pair, spans.queries(at), :] * jnp.asarray(scale, BF16), low)

    for pair in range(pairs):
        for at in range(count):
            score_ref[at] = dot(spans.keys(k_ref, kr_ref, pair, at), scaled_queries(pair, at), 1, 1)
            grads = two_heads(da_ref[pair, spans.queries(at), :], low)
            grad_ref[at] = dot(spans.keys(v_ref, vr_ref, pair, at), grads, 1, 1)
        for at in range(count):
            probs = softmax(score_ref[at] + bias_ref[at])
            probs_ref[at] = probs.astype(BF16)
            part = probs * grad_ref[at]
            dscore_ref[at] = (part - probs * jnp.sum(part, axis=0, keepdims=True)).astype(BF16)
        late = [None, None]
        for at in range(count):
            here = spans.queries(at)
            row, block = divmod(at, spans.blocks)
            dscores = dscore_ref[at]
            grads = two_heads(da_ref[pair, here, :], low)
            dk = dot(dscores, scaled_queries(pair, at))
            dv = dot(probs_ref[at], grads)
            dq = one_of_two(dot(spans.keys(k_ref, kr_ref, pair, at), dscores, 0, 0), size) * scale
            dqkv_ref[0, pair, here, :] = dq.T.astype(BF16)
            start = at * size
            for kind, grad in ((0, dk), (1, dv)):
                out_ref, rim_ref = dqkv_ref.at[kind + 1], drim_ref.at[kind]
                early = grad[:WINDOW]
                if block == 0:
                    rim_ref[pair, row * WINDOW : (row + 1) * WINDOW, :] = early.astype(BF16)
                else:
                    out_ref[pair, start - WINDOW : start, :] = (late[kind] + early).astype(BF16)
                if size > WINDOW:
                    out_ref[pair, start : start + size - WINDOW, :] = grad[WINDOW:size].astype(BF16)
                late[kind] = grad[size:]
                if block == spans.blocks - 1:
                    out_ref[pair, start + size - WINDOW : start + size, :] = late[kind].astype(BF16)


def attend_back(qkv, kv_rim, doc_start, first_pos, grad_att, after=()):
    rows, group = doc_start.shape
    all_pairs, tokens = qkv.shape[0] // 3, qkv.shape[1]
    rim = kv_rim.shape[1]
    spans = Spans(rows, group)
    steps = all_pairs // PAIRS
    own = lambda kind: pl.BlockSpec((PAIRS, tokens, LANES), lambda j, *_: (kind * steps + j, 0, 0))
    edge = lambda kind: pl.BlockSpec((PAIRS, rim, LANES), lambda j, *_: (kind * steps + j, 0, 0))
    return launch(
        functools.partial(attend_back_kernel, spans=spans, pairs=PAIRS),
        "attend_back",
        (steps,),
        [first_pos],
        [
            (doc_start, full(rows, group)),
            (qkv, own(0)),
            (qkv, own(1)),
            (qkv, own(2)),
            (kv_rim, edge(0)),
            (kv_rim, edge(1)),
            (grad_att, own(0)),
        ],
        [
            ((3, all_pairs, tokens, LANES), BF16, pl.BlockSpec((3, PAIRS, tokens, LANES), lambda j, *_: (0, j, 0, 0))),
            ((2, all_pairs, rim, LANES), BF16, pl.BlockSpec((2, PAIRS, rim, LANES), lambda j, *_: (0, j, 0, 0))),
        ],
        [spans.scratch(kind) for kind in (F32, F32, F32, BF16, BF16)],
        us=16,
        after=after,
    )


def norm_matmul_kernel(places_ref, x_ref, gain_ref, w_ref, out_ref, normedT_ref, normed_ref, *, slab, step):
    @pl.when(pl.program_id(0) == 0)
    def _():
        for at in range(0, x_ref.shape[0], step):
            x = x_ref[at : at + step, :].astype(F32)
            inv = lax.rsqrt(jnp.mean(x * x, axis=-1, keepdims=True) + epsilon)
            normed = (x * inv * gain_ref[...]).astype(BF16)
            normed_ref[at : at + step, :] = normed
            store_slabs(normedT_ref, normed.T, places_ref, 0, slab, slice(at, at + step))

    put_blocks(out_ref, dot(normed_ref[...], w_ref[...]).astype(BF16))


def norm_matmul(x, gain, weight, first_column, places, slab, after=()):
    tokens, width = x.shape
    columns = weight.shape[1] - first_column
    tile = 1024
    skip, wide = first_column // tile, tile // LANES
    return launch(
        functools.partial(norm_matmul_kernel, slab=slab, step=min(STEP, tokens)),
        "norm_matmul",
        (columns // tile,),
        [places],
        [
            (x, full(tokens, width)),
            (gain[None], full(1, width)),
            (weight, pl.BlockSpec((width, tile), lambda j, *_: (0, skip + j))),
        ],
        [
            ((columns // LANES, tokens, LANES), BF16, pl.BlockSpec((wide, tokens, LANES), lambda j, *_: (j, 0, 0))),
            ((width, tokens), BF16, full(width, tokens)),
        ],
        [pltpu.VMEM((tokens, width), BF16)],
        us=13 * tokens / 1024,
        after=after,
    )


def turn_kernel(places_ref, x_ref, out_ref, *, slab):
    store_slabs(out_ref, x_ref[...].T, places_ref, 0, slab)


def turn(x, places, slab, after=()):
    tokens, width = x.shape
    return launch(
        functools.partial(turn_kernel, slab=slab),
        "turn",
        (tokens // STEP,),
        [places],
        [(x, pl.BlockSpec((STEP, width), lambda m, *_: (m, 0)))],
        [((width, tokens), BF16, pl.BlockSpec((width, STEP), lambda m, *_: (0, m)))],
        us=5,
        after=after,
    )[0]


def out_proj_kernel(places_ref, att_ref, w_ref, x_ref, gain_ref, resid_ref, normed_ref, normedT_ref, *, slab):
    resid = x_ref[...].astype(F32) + dot(side_by_side(att_ref), w_ref[...])
    resid_ref[...] = resid
    inv = lax.rsqrt(jnp.mean(resid * resid, axis=-1, keepdims=True) + epsilon)
    normed = (resid * inv * gain_ref[...]).astype(BF16)
    normed_ref[...] = normed
    store_slabs(normedT_ref, normed.T, places_ref, 0, slab)


def out_proj(att, w_out, x, gain, places, slab, after=()):
    tokens, width = x.shape
    pairs = att.shape[0]
    rows = pl.BlockSpec((STEP, width), lambda m, *_: (m, 0))
    return launch(
        functools.partial(out_proj_kernel, slab=slab),
        "out_proj",
        (tokens // STEP,),
        [places],
        [
            (att, pl.BlockSpec((pairs, STEP, LANES), lambda m, *_: (0, m, 0))),
            (w_out, full(width, width)),
            (x, rows),
            (gain[None], full(1, width)),
        ],
        [
            ((tokens, width), F32, rows),
            ((tokens, width), BF16, rows),
            ((width, tokens), BF16, pl.BlockSpec((width, STEP), lambda m, *_: (0, m))),
        ],
        us=9,
        after=after,
    )


def ff_kernel(*refs, first, given):
    normed_ref, dy_ref, dyT_ref, normedT_ref, wg_ref, wu0_ref, wu1_ref, wu2_ref, wd_ref = refs[:9]
    hidden_ref, dgu_ref, send_ref, total_ref, acc_ref = refs[9 + given :]
    tile = pl.program_id(0)
    tokens = normed_ref.shape[0]

    @pl.when(tile == 0)
    def _():
        acc_ref[...] = refs[9][...] if given else jnp.zeros_like(acc_ref)

    half = FF % LANES
    w_up = jnp.concatenate([wu0_ref[:, half:], wu1_ref[...], wu2_ref[:, :half]], axis=1)
    column = (tile + first) * FF_TILE + lax.broadcasted_iota(jnp.int32, (STEP, FF_TILE), 1)
    inside = column < FF
    for at in range(0, tokens, STEP):
        here = slice(at, at + STEP)
        normed = normed_ref[here, :]
        gate = dot(normed, wg_ref[...])
        up = dot(normed, w_up)
        back = dot(dy_ref[here, :], wd_ref[...], 1, 1)
        sigma = 1.0 / (1.0 + jnp.exp(-gate))
        silu = gate * sigma
        hidden_ref[here, :] = jnp.where(inside, silu * up, 0.0).astype(BF16)
        dgate = back * up * (sigma * (1.0 + gate * (1.0 - sigma)))
        dgate = jnp.where(inside, dgate, 0.0).astype(BF16)
        dup = jnp.where(inside, back * silu, 0.0).astype(BF16)
        dgu_ref[0, here, :] = dgate
        dgu_ref[1, here, :] = dup
        acc_ref[here, :] += dot(dgate, wg_ref[...], 1, 1) + dot(dup, w_up, 1, 1)
    send_ref[0] = dot(dyT_ref[...], hidden_ref[...]).astype(BF16)
    send_ref[1] = dot(normedT_ref[...], dgu_ref[0]).astype(BF16)
    send_ref[2] = dot(normedT_ref[...], dgu_ref[1]).astype(BF16)

    @pl.when(tile == pl.num_programs(0) - 1)
    def _():
        total_ref[...] = acc_ref[...]


def feed_forward(normed, dy, dy_turned, normed_turned, w_gate_up, w_down, first, count, total=None, after=()):
    tokens, width = normed.shape
    wide = count * FF_TILE
    last = w_gate_up.shape[1] // LANES - 1
    skip = FF // LANES + first * (FF_TILE // LANES)
    up = lambda k: pl.BlockSpec(
        (width, LANES), lambda j: (0, jnp.minimum(skip + k + j * (FF_TILE // LANES), last))
    )
    other_half = full(width // 2, tokens)
    given = [] if total is None else [(total, full(tokens, width))]
    return launch(
        functools.partial(ff_kernel, first=first, given=len(given)),
        "feed_forward",
        (count,),
        [],
        [
            (normed, full(tokens, width)),
            (dy, full(tokens, width)),
            (dy_turned, other_half),
            (normed_turned, other_half),
            (w_gate_up, pl.BlockSpec((width, FF_TILE), lambda j: (0, first + j))),
            (w_gate_up, up(0)),
            (w_gate_up, up(1)),
            (w_gate_up, up(2)),
            (w_down.T, pl.BlockSpec((FF_TILE, width), lambda j: (first + j, 0))),
        ]
        + given,
        [
            ((tokens, wide), BF16, pl.BlockSpec((tokens, FF_TILE), lambda j: (0, j))),
            ((2, tokens, wide), BF16, pl.BlockSpec((2, tokens, FF_TILE), lambda j: (0, 0, j))),
            ((3, width // 2, wide), BF16, pl.BlockSpec((3, width // 2, FF_TILE), lambda j: (0, 0, j))),
            ((tokens, width), F32, full(tokens, width)),
        ],
        [pltpu.VMEM((tokens, width), F32)],
        us=5.5 * count,
        after=after,
    )


def ff_grad_kernel(bit_ref, dyT_ref, normedT_ref, hidden_ref, dgu_ref, got_ref, send_ref, keep_ref):
    part = send_ref.shape[1]
    rights = (hidden_ref[...], dgu_ref[0], dgu_ref[1])
    for kind, (left_ref, right) in enumerate(zip((dyT_ref, normedT_ref, normedT_ref), rights)):
        for out_ref, index in ((send_ref, 1 - bit_ref[0]), (keep_ref, bit_ref[0])):
            rows = pl.ds(pl.multiple_of(index * part, part), part)
            total = dot(left_ref[rows, :], right) + got_ref[kind, rows, :].astype(F32)
            out_ref[kind] = total.astype(BF16)


def ff_grad(bit, dy_turned, normed_turned, hidden, dgu, got, after=()):
    width, tokens = dy_turned.shape
    wide = hidden.shape[1]
    tile = 512 if wide % 512 == 0 else FF_TILE
    own_half = pl.BlockSpec((width // 2, tokens), lambda j, *_: (1, 0))
    part = ((3, width // 4, wide), BF16, pl.BlockSpec((3, width // 4, tile), lambda j, *_: (0, 0, j)))
    return launch(
        ff_grad_kernel,
        "ff_grad",
        (wide // tile,),
        [bit],
        [
            (dy_turned, own_half),
            (normed_turned, own_half),
            (hidden, pl.BlockSpec((tokens, tile), lambda j, *_: (0, j))),
            (dgu, pl.BlockSpec((2, tokens, tile), lambda j, *_: (0, 0, j))),
            (got, pl.BlockSpec((3, width // 2, tile), lambda j, *_: (0, 0, j))),
        ],
        [part, part],
        us=2 * wide / FF_TILE,
        after=after,
    )


def norm_back(grad, values, gain):
    inv = lax.rsqrt(jnp.mean(values * values, axis=-1, keepdims=True) + epsilon)
    scaled = grad * gain
    return inv * scaled - values * (inv * inv * inv) * jnp.mean(scaled * values, axis=-1, keepdims=True)


def branch_back_kernel(total_ref, dy_ref, resid_ref, gain_ref, w_out_ref, drb_ref, da_ref):
    grad = norm_back(total_ref[...], resid_ref[...], gain_ref[...])
    grad = dy_ref[...].astype(F32) + grad
    branch = grad.astype(BF16)
    put_blocks(drb_ref, branch)
    put_blocks(da_ref, dot(branch, w_out_ref[...], 1, 1).astype(BF16))


def branch_back(total, dy, resid, gain, w_out, after=()):
    tokens, width = dy.shape
    rows = pl.BlockSpec((STEP, width), lambda m: (m, 0))
    blocks = ((width // LANES, tokens, LANES), BF16, pl.BlockSpec((width // LANES, STEP, LANES), lambda m: (0, m, 0)))
    return launch(
        branch_back_kernel,
        "branch_back",
        (tokens // STEP,),
        [],
        [
            (total, rows),
            (dy, rows),
            (resid, rows),
            (gain[None], full(1, width)),
            (w_out, full(width, width)),
        ],
        [blocks, blocks],
        us=9,
        after=after,
    )


def ff_out_kernel(*refs):
    wd_ref, resid_ref, out_ref = refs[-3:]
    total, first = resid_ref[...], 0
    for hidden_ref in refs[:-3]:
        count = min(hidden_ref.shape[1], FF - first)
        total += dot(hidden_ref[:, :count], wd_ref[first : first + count, :])
        first += count
    out_ref[...] = total.astype(BF16)


def ff_out(hiddens, w_down, resid, after=()):
    tokens, width = resid.shape
    rows = lambda columns: pl.BlockSpec((STEP, columns), lambda m: (m, 0))
    return launch(
        ff_out_kernel,
        "ff_out",
        (tokens // STEP,),
        [],
        [(hidden, rows(hidden.shape[1])) for hidden in hiddens]
        + [(w_down.T, full(FF, width)), (resid, rows(width))],
        [((tokens, width), BF16, rows(width))],
        us=11,
        after=after,
    )[0]


def att_grad_kernel(*refs, split):
    scalars = 1 if split else 0
    attT_ref, oneT_ref, rimT_ref, drb_ref, dqkv_ref, drim_ref = refs[scalars : scalars + 6]
    kind = pl.program_id(0)

    def put(total, late):
        if split:
            got_ref = refs[-3 if late else -4]
            send_ref, keep_ref = refs[-2:]
            part = send_ref.shape[0]
            for out_ref, half in ((send_ref, 1 - refs[0][0]), (keep_ref, refs[0][0])):
                rows = pl.ds(pl.multiple_of(half * part, part), part)
                out_ref[...] = (total(rows) + got_ref[rows, :].astype(F32)).astype(BF16)
        else:
            refs[-1 if late else -2][...] = total(slice(None)).astype(BF16)

    @pl.when(kind == 0)
    def _():
        right = side_by_side(drb_ref)
        put(lambda rows: dot(attT_ref[rows, :], right), False)

    @pl.when(kind == 1)
    def _():
        right = side_by_side(dqkv_ref)
        put(lambda rows: dot(oneT_ref[rows, :], right), False)

    @pl.when(kind > 1)
    def _():
        right, rim = side_by_side(dqkv_ref), side_by_side(drim_ref)
        put(lambda rows: dot(oneT_ref[rows, :], right) + dot(rimT_ref[rows, :], rim), True)


def att_grad(att_turned, one_turned, rim_turned, drb, dqkv, drim, bit=None, got=None, after=()):
    width, tokens = one_turned.shape
    rim = rim_turned.shape[1]
    split = got is not None
    half = 1 if split else 0
    inputs = [
        (turned, pl.BlockSpec((width // 2, turned.shape[1]), lambda j, *_: (half, 0)))
        for turned in (att_turned, one_turned, rim_turned)
    ]
    blocks = width // LANES
    inputs += [
        (drb, full(blocks, tokens, LANES)),
        (dqkv, pl.BlockSpec((None, blocks, tokens, LANES), lambda j, *_: (jnp.maximum(j - 1, 0), 0, 0, 0))),
        (drim, pl.BlockSpec((None, blocks, rim, LANES), lambda j, *_: (jnp.maximum(j - 2, 0), 0, 0, 0))),
    ]
    columns = 4 * width
    parts = [
        pl.BlockSpec((width // 2, width), lambda j, *_: (0, jnp.minimum(j, 1))),
        pl.BlockSpec((width // 2, width), lambda j, *_: (0, jnp.maximum(j - 2, 0))),
    ]
    if split:
        inputs += list(zip(got, parts))
        part = ((width // 4, columns), BF16, pl.BlockSpec((width // 4, width), lambda j, *_: (0, j)))
        outputs = [part, part]
    else:
        outputs = [((width // 2, columns // 2), BF16, spec) for spec in parts]
    return launch(
        functools.partial(att_grad_kernel, split=split),
        "att_grad",
        (4,),
        [bit] if split else [],
        inputs,
        outputs,
        us=11,
        after=after,
    )


def input_grad_kernel(dqkv_ref, w_ref, x_ref, gain_ref, drb_ref, back_ref, out_ref, acc_ref, *, rows, group):
    k = pl.program_id(0)
    tokens = acc_ref.shape[0]
    part = dot(side_by_side(dqkv_ref), w_ref[...], 1, 1)

    @pl.when(k == 0)
    def _():
        acc_ref[...] = part

    @pl.when(k > 0)
    def _():
        acc_ref[...] += part

    @pl.when(k == 2)
    def _():
        for at in range(0, tokens, STEP):
            here = slice(at, at + STEP)
            grad = norm_back(acc_ref[here, :], x_ref[here, :].astype(F32), gain_ref[...])
            out_ref[here, :] = grad + side_by_side(drb_ref.at[:, here, :]).astype(F32)
        for row in range(rows):
            tail = slice((row + 1) * group - WINDOW, (row + 1) * group)
            out_ref[tail, :] += back_ref[row * WINDOW : (row + 1) * WINDOW, :].astype(F32)


def input_grad(dqkv, w_qkv, x, gain, drb, back, rows, group, after=()):
    tokens, width = x.shape
    whole = full(tokens, width)
    return launch(
        functools.partial(input_grad_kernel, rows=rows, group=group),
        "input_grad",
        (3,),
        [],
        [
            (dqkv, pl.BlockSpec((None, width // LANES, tokens, LANES), lambda j: (j, 0, 0, 0))),
            (w_qkv, pl.BlockSpec((width, width), lambda j: (0, j))),
            (x, whole),
            (gain[None], full(1, width)),
            (drb, full(*drb.shape)),
            (back, full(rows * WINDOW, width)),
        ],
        [((tokens, width), F32, whole)],
        [pltpu.VMEM((tokens, width), F32)],
        us=15,
        after=after,
    )[0]


def rim_grad_kernel(drim_ref, wk_ref, wv_ref, x_ref, gain_ref, out_ref):
    grad = dot(side_by_side(drim_ref.at[0]), wk_ref[...], 1, 1)
    grad += dot(side_by_side(drim_ref.at[1]), wv_ref[...], 1, 1)
    out_ref[...] = norm_back(grad, x_ref[...].astype(F32), gain_ref[...]).astype(BF16)


def rim_grad(drim, w_qkv, x, gain, after=()):
    rim, width = x.shape
    part = lambda k: pl.BlockSpec((width, width), lambda j: (0, k))
    return launch(
        rim_grad_kernel,
        "rim_grad",
        (1,),
        [],
        [
            (drim, full(*drim.shape)),
            (w_qkv, part(1)),
            (w_qkv, part(2)),
            (x, full(rim, width)),
            (gain[None], full(1, width)),
        ],
        [((rim, width), BF16, full(rim, width))],
        us=5,
        after=after,
    )[0]


def add_kernel(bit_ref, *refs):
    count = len(refs) // 4
    for k in range(count):
        keep_ref, got_ref = refs[2 * k : 2 * k + 2]
        outs = refs[2 * count + 2 * k : 2 * count + 2 * k + 2]
        for out_ref, index in zip(outs, (1 - bit_ref[k], bit_ref[k])):
            out_ref[...] = (keep_ref[:, index].astype(F32) + got_ref[:, index].astype(F32)).astype(BF16)


def add_and_cut(items, after=()):
    inputs, outputs, bits, most = [], [], [], 1
    for keep, got, bit in items:
        kinds, rows, columns = keep.shape
        cut = lambda value: value.reshape(kinds, 2, rows // 2, columns)
        tile = 512 if columns % 1024 == 0 else 256
        steps = columns // tile
        most = max(most, steps)
        at = lambda j, *_, steps=steps: (0, 0, 0, jnp.minimum(j, steps - 1))
        out_at = lambda j, *_, steps=steps: (0, 0, jnp.minimum(j, steps - 1))
        spec = pl.BlockSpec((kinds, 2, rows // 2, tile), at)
        inputs += [(cut(keep), spec), (cut(got), spec)]
        outputs += [((kinds, rows // 2, columns), BF16, pl.BlockSpec((kinds, rows // 2, tile), out_at))] * 2
        bits.append(bit)
    parts = launch(add_kernel, "add_and_cut", (most,), [jnp.concatenate(bits)], inputs, outputs, after=after)
    return [(parts[2 * k], parts[2 * k + 1]) for k in range(len(items))]


def log2(count):
    return count.bit_length() - 1


def stage_orders(n_dp, n_seq, flavour):
    dp = [("dp", bit) for bit in range(1, log2(n_dp))]
    if flavour:
        dp = dp[::-1]
    seq = [("seq", bit) for bit in range(log2(n_seq))]
    return dp + seq, seq[:1] + dp + seq[1:]


def row_bits(n_dp, n_seq):
    return [("seq", bit) for bit in reversed(range(log2(n_seq)))] + [
        ("dp", bit) for bit in reversed(range(log2(n_dp)))
    ]


def block_places(n_dp, n_seq, flavour):
    bits, orders = row_bits(n_dp, n_seq), stage_orders(n_dp, n_seq, flavour)
    count = n_dp * n_seq
    tables = []
    for core in range(2):
        table = []
        for block in range(count):
            value = {step: (block >> (len(bits) - 1 - k)) & 1 for k, step in enumerate(bits)}
            owner = value[("dp", 0)]
            place = 0
            for step in orders[owner]:
                place = place * 2 + value[step]
            table.append(place + (count // 2 if owner == core else 0))
        tables.append(np.array(table, np.int32))
    return tables


def swap_pairs(n_dp, n_seq, steps):
    pairs = []
    for d in range(n_dp):
        for s in range(n_seq):
            axis, bit = steps[d % 2]
            there = (d ^ (1 << bit), s) if axis == "dp" else (d, s ^ (1 << bit))
            pairs.append((d * n_seq + s, there[0] * n_seq + there[1]))
    return pairs


def swap(value, steps):
    n_dp, n_seq = lax.axis_size("dp"), lax.axis_size("seq")
    return lax.ppermute(value, ("dp", "seq"), swap_pairs(n_dp, n_seq, steps))


def bit_of(step):
    axis, bit = step
    return (lax.axis_index(axis) >> bit) & 1


def own_bit(steps):
    core = lax.axis_index("dp") & 1
    return jnp.where(core == 0, bit_of(steps[0]), bit_of(steps[1])).astype(jnp.int32).reshape(1)


CORE = (("dp", 0), ("dp", 0))


class Chunk:
    def __init__(self, flavour):
        self.stages = list(zip(*stage_orders(lax.axis_size("dp"), lax.axis_size("seq"), flavour)))
        self.done = 0

    def bit(self):
        return own_bit(self.stages[self.done])

    def between_cores(self, *parts):
        self.got = [swap(part, CORE) for part in parts]

    def go(self, send, keep):
        self.keep = keep
        self.got = swap(send, self.stages[self.done])
        self.done += 1

    @property
    def last(self):
        return self.done == len(self.stages)

    def share(self):
        return (self.keep.astype(F32) + self.got.astype(F32)).astype(BF16)


def advance(*chunks, after=()):
    parts = add_and_cut([(chunk.keep, chunk.got, chunk.bit()) for chunk in chunks], after=after)
    for chunk, (send, keep) in zip(chunks, parts):
        chunk.go(send, keep)
    return parts[0][0]


def finish_kernel(*refs):
    out_ref, first = refs[-1], 0
    for keep_ref, got_ref in zip(refs[:-1:2], refs[1:-1:2]):
        columns = keep_ref.shape[2]
        total = keep_ref[...].astype(F32) + got_ref[...].astype(F32)
        out_ref[:, :, first : first + columns] = total.astype(BF16)
        first += columns


def finish(*chunks, after=()):
    kinds, part, _ = chunks[0].keep.shape
    inputs = [(array, full(*array.shape)) for chunk in chunks for array in (chunk.keep, chunk.got)]
    shape = (kinds, part, sum(chunk.keep.shape[2] for chunk in chunks))
    return launch(finish_kernel, "finish", (1,), [], inputs, [(shape, BF16, full(*shape))], us=2, after=after)[0]


def join_kernel(bit_ref, value_ref, got_ref, out_ref):
    count = value_ref.shape[1]
    first = bit_ref[0] * count
    out_ref[:, pl.ds(first, count)] = value_ref[...]
    out_ref[:, pl.ds(count - first, count)] = got_ref[...]


class Gather:
    def __init__(self, value):
        n_dp = lax.axis_size("dp")
        self.dims = [("dp", bit) for bit in range(1, log2(n_dp))]
        self.steps = list(zip(self.dims[::-1], self.dims))
        self.kinds, self.part, self.columns = value.shape
        self.value = value[:, None]
        self.done = 0
        self.send()

    @property
    def last(self):
        return self.done == len(self.steps)

    def send(self):
        self.got = swap(self.value, CORE if self.last else self.steps[self.done])

    def step(self, after=()):
        bit = own_bit(self.steps[self.done])
        kinds, count, part, columns = self.value.shape
        tile = columns // 2
        spec = lambda count: pl.BlockSpec((kinds, count, part, tile), lambda j, *_: (0, 0, 0, j))
        (self.value,) = launch(
            join_kernel,
            "join",
            (2,),
            [bit],
            [(self.value, spec(count)), (self.got, spec(count))],
            [((kinds, 2 * count, part, columns), BF16, spec(2 * count))],
            us=2,
            after=after,
        )
        self.done += 1
        self.send()
        return self.value

    def whole(self):
        dims = self.dims
        core = lax.axis_index("dp") & 1
        halves = []
        for which, order in enumerate((dims[::-1], dims)):
            half = jnp.where(core == which, self.value, self.got)
            half = half.reshape((self.kinds,) + (2,) * len(dims) + (self.part, self.columns))
            wanted = [1 + order[::-1].index(step) for step in dims[::-1]]
            halves.append(half.transpose([0] + wanted + [len(dims) + 1, len(dims) + 2]))
        whole = jnp.stack(halves, axis=len(dims) + 1)
        return whole.reshape(self.kinds, lax.axis_size("dp") * self.part, self.columns)


def natural_rows(core_ref, own_ref, got_ref, kind, step, columns):
    pieces = []
    for x in range(2):
        for which in range(2):
            index = x * 2 + step if which == 0 else step * 2 + x
            own, got = own_ref[kind, index, :, columns], got_ref[kind, index, :, columns]
            pieces.append(jnp.where(core_ref[0] == which, own, got))
    return jnp.concatenate(pieces, axis=0).astype(F32)


def row_sums(value):
    total = jnp.sum(value, axis=1, keepdims=True)
    return jnp.broadcast_to(total, (total.shape[0], LANES)).T[:1, :]


def put_ff_kernel(core_ref, seq_ref, own_ref, got_ref, w_ref, gain_ref, gate_up_ref, down_ref, dgain_ref):
    step = pl.program_id(0)
    rows = lambda kind: natural_rows(core_ref, own_ref, got_ref, kind, step, slice(0, FF))
    down_ref[...] = rows(0).T
    gate, up = rows(1), rows(2)
    gate_up_ref[:, :FF] = gate
    gate_up_ref[:, FF:] = up
    weight = w_ref[...].astype(F32)
    total = row_sums(gate * weight[:, :FF]) + row_sums(up * weight[:, FF:])
    dgain_ref[...] = total / gain_ref[...]


def put_ff(gather, w_gate_up, gain, after=()):
    kept = 8 * gather.part
    half = kept // 2
    core = (lax.axis_index("dp") & 1).reshape(1)
    seq = lax.axis_index("seq").reshape(1)
    whole = full(*gather.value.shape)
    return launch(
        put_ff_kernel,
        "put_ff",
        (2,),
        [core, seq],
        [
            (gather.value, whole),
            (gather.got, whole),
            (w_gate_up, pl.BlockSpec((half, 2 * FF), lambda j, core, seq: (2 * seq[0] + j, 0))),
            (gain[None], pl.BlockSpec((1, half), lambda j, core, seq: (0, 2 * seq[0] + j))),
        ],
        [
            ((kept, 2 * FF), F32, pl.BlockSpec((half, 2 * FF), lambda j, *_: (j, 0))),
            ((FF, kept), F32, pl.BlockSpec((FF, half), lambda j, *_: (0, j))),
            ((1, kept), F32, pl.BlockSpec((1, half), lambda j, *_: (0, j))),
        ],
        us=9,
        after=after,
    )


def put_att_kernel(core_ref, seq_ref, own_ref, got_ref, w_ref, gain_ref, qkv_ref, out_ref, dgain_ref):
    step = pl.program_id(0)
    width = out_ref.shape[1]
    out_ref[...] = natural_rows(core_ref, own_ref, got_ref, 0, step, slice(0, width))
    qkv = natural_rows(core_ref, own_ref, got_ref, 0, step, slice(width, 4 * width))
    qkv_ref[...] = qkv
    dgain_ref[...] = row_sums(qkv * w_ref[...].astype(F32)) / gain_ref[...]


def put_att(gather, w_qkv, gain, after=()):
    kept = 8 * gather.part
    half, width = kept // 2, gather.columns // 4
    core = (lax.axis_index("dp") & 1).reshape(1)
    seq = lax.axis_index("seq").reshape(1)
    whole = full(*gather.value.shape)
    return launch(
        put_att_kernel,
        "put_att",
        (2,),
        [core, seq],
        [
            (gather.value, whole),
            (gather.got, whole),
            (w_qkv, pl.BlockSpec((half, 3 * width), lambda j, core, seq: (2 * seq[0] + j, 0))),
            (gain[None], pl.BlockSpec((1, half), lambda j, core, seq: (0, 2 * seq[0] + j))),
        ],
        [
            ((kept, 3 * width), F32, pl.BlockSpec((half, 3 * width), lambda j, *_: (j, 0))),
            ((kept, width), F32, pl.BlockSpec((half, width), lambda j, *_: (j, 0))),
            ((1, kept), F32, pl.BlockSpec((1, half), lambda j, *_: (0, j))),
        ],
        us=5,
        after=after,
    )


def place_rows(turned, places):
    count = places.shape[0]
    blocks = turned.reshape((count, turned.shape[0] // count) + turned.shape[1:])
    return jnp.zeros_like(blocks).at[places].set(blocks).reshape(turned.shape)


def shifted(value, axis, steps):
    count = lax.axis_size(axis)
    leading, last = (max(0, -steps), min(count, count - steps))
    return lax.ppermute(value, axis, [(source, source + steps) for source in range(leading, last)])


def per_device(inputs, w_qkv, w_out, w_gate_up, w_down, gain_attn, gain_mlp, doc_start, cotangent):
    n_dp, n_seq = lax.axis_size("dp"), lax.axis_size("seq")
    rows, group, width = inputs.shape
    tokens = rows * group
    core = lax.axis_index("dp") & 1
    first_pos = (lax.axis_index("seq") * group).reshape(1)
    slab = width // (n_dp * n_seq)
    places = []
    for flavour in range(2):
        tables = block_places(n_dp, n_seq, flavour)
        places.append(jnp.where(core == 0, tables[0], tables[1]))
    if slab % 16 == 0:
        put, in_order = places, lambda turned, flavour: turned
    else:
        slab = 32
        put = [jnp.arange(width // slab, dtype=jnp.int32)] * 2
        in_order = lambda turned, flavour: place_rows(turned, places[flavour])
    x = inputs.reshape(tokens, width)
    dy = cotangent.reshape(tokens, width)
    x_rim = shifted(inputs[:, group - WINDOW :], "seq", 1).reshape(rows * WINDOW, width)

    qkv, one_turned = norm_matmul(x, gain_attn, w_qkv, 0, put[0], slab)
    dy_turned = turn(dy, put[1], slab, after=[qkv])
    kv_rim, rim_turned = norm_matmul(x_rim, gain_attn, w_qkv, width, put[0], slab, after=[dy_turned])
    att, att_turned = attend(qkv, kv_rim, doc_start, first_pos, put[0], slab)
    resid, normed_two, two_turned = out_proj(att, w_out, x, gain_mlp, put[1], slab)
    one_turned, rim_turned, att_turned = [in_order(turned, 0) for turned in (one_turned, rim_turned, att_turned)]
    two_turned, dy_turned = [in_order(turned, 1) for turned in (two_turned, dy_turned)]

    chunks, hiddens, dgus, total, first = [], [], [], None, 0
    for count in FF_CHUNKS:
        hidden, dgu, send, total = feed_forward(
            normed_two, dy, dy_turned, two_turned, w_gate_up, w_down, first, count, total
        )
        chunk = Chunk(1)
        chunk.between_cores(send)
        chunks.append(chunk)
        hiddens.append(hidden)
        dgus.append(dgu)
        first += count
    one, two = chunks

    def keep_ff(chunk, k, after):
        send, keep = ff_grad(chunk.bit(), dy_turned, two_turned, hiddens[k], dgus[k], chunk.got[0], after=after)
        chunk.go(send, keep)
        return send

    token = keep_ff(one, 0, [total])
    drb, da = branch_back(total, dy, resid, gain_mlp, w_out, after=[token, *two.got])
    token = keep_ff(two, 1, [da])
    dqkv, drim = attend_back(qkv, kv_rim, doc_start, first_pos, da, after=[token])
    att = Chunk(0)
    grads = (att_turned, one_turned, rim_turned, drb, dqkv, drim)
    sends = att_grad(*grads, after=[one.got])
    att.between_cores(*sends)
    token = advance(one, two, after=sends)
    back = rim_grad(drim, w_qkv, x_rim, gain_attn, after=[token])
    back_got = shifted(back, "seq", -1)
    token = back
    send, keep = att_grad(*grads, att.bit(), att.got, after=[token])
    att.go(send[None], keep[None])
    token = advance(one, two, after=[send])
    grad_inputs = input_grad(dqkv, w_qkv, x, gain_attn, drb, back_got, rows, group, after=[token])
    token = advance(one, two, att, after=[grad_inputs])
    outputs = ff_out(hiddens, w_down, resid, after=[token])
    while not (one.last and two.last):
        token = advance(one, two, att, after=[outputs])
    gather_ff = Gather(finish(one, two, after=[outputs]))
    token = advance(att, after=[gather_ff.value])
    token = gather_ff.step(after=[token])
    while not att.last:
        token = advance(att, after=[token])
    while not gather_ff.last:
        token = gather_ff.step(after=[token])
    gather = Gather(finish(att, after=[token]))
    if slab % 16 == 0 and n_dp == 8:
        total_gate_up, turned_down, gain_two = put_ff(gather_ff, w_gate_up, gain_mlp, after=[gather.value])
        total_down = turned_down.T
        token = total_gate_up
        while not gather.last:
            token = gather.step(after=[token])
        total_qkv, total_out, gain_one = put_att(gather, w_qkv, gain_attn)
        gain_one, gain_two = gain_one[0], gain_two[0]
    else:
        total_ff = gather_ff.whole()
        while not gather.last:
            gather.step()
        rest = gather.whole()[0]
        total_down, total_gate, total_up = [total_ff[kind, :, :FF] for kind in range(3)]
        total_down = total_down.astype(F32)
        total_gate_up = jnp.concatenate([total_gate, total_up], axis=1).astype(F32)
        total_out = rest[:, :width].astype(F32)
        total_qkv = rest[:, width:].astype(F32)
        kept = total_qkv.shape[0]
        first_row = lax.axis_index("seq") * kept

        def gain_total(total, weight, gain):
            mine = lax.dynamic_slice_in_dim(weight, first_row, kept, axis=0).astype(F32)
            return jnp.sum(total * mine, axis=1) / lax.dynamic_slice_in_dim(gain, first_row, kept)

        gain_one = gain_total(total_qkv, w_qkv, gain_attn)
        gain_two = gain_total(total_gate_up, w_gate_up, gain_mlp)

    return (
        outputs.reshape(rows, group, width),
        grad_inputs.reshape(rows, group, width),
        total_qkv,
        total_out,
        total_gate_up,
        total_down,
        gain_one,
        gain_two,
    )


def solution(mesh):
    in_specs = (
        P("dp", "seq", None),
        P(),
        P(),
        P(),
        P(),
        P(),
        P(),
        P("dp", "seq"),
        P("dp", "seq", None),
    )
    out_specs = (
        P("dp", "seq", None),
        P("dp", "seq", None),
        P("seq", None),
        P("seq", None),
        P("seq", None),
        P("seq", None),
        P("seq"),
        P("seq"),
    )
    return jax.shard_map(
        per_device, mesh=mesh, in_specs=in_specs, out_specs=out_specs, check_vma=False
    )
```

```python
import functools
import math

import jax
import jax.numpy as jnp
import numpy as np
from jax import lax
from jax.experimental import pallas as pl
from jax.experimental.pallas import tpu as pltpu
from jax.sharding import PartitionSpec as P

HEADS = 16
HEAD_DIM = 64
FF = 2752
WINDOW = 64
LANES = 128
PAIRS = 2
FF_TILE = 256
FF_TILES = -(-FF // FF_TILE)
FF_CHUNKS = (6, 5)
STEP = 256
epsilon = 1e-05
masked_value = -1e30
F32 = jnp.float32
BF16 = jnp.bfloat16
VMEM_LIMIT = 64 * 1024 * 1024 - 256 * 1024
PER_US = 1.1e9


def dot(left, right, left_dim=1, right_dim=0):
    return lax.dot_general(
        left, right, (((left_dim,), (right_dim,)), ((), ())), preferred_element_type=F32
    )


def launch(kernel, name, grid, scalars, inputs, outputs, scratch=(), us=8, after=()):
    known = len(scalars) + len(inputs)

    def body(*refs):
        kernel(*refs[:known], *refs[known + len(after) :])

    specs = [spec for _, spec in inputs] + [pl.BlockSpec(memory_space=pl.ANY)] * len(after)
    shapes = [pltpu.HBM(shape, kind) for shape, kind, _ in outputs]
    moved = sum(array.size * array.dtype.itemsize for array, _ in inputs)
    moved += sum(math.prod(shape) * np.dtype(kind).itemsize for shape, kind, _ in outputs)
    return pl.pallas_call(
        body,
        grid_spec=pltpu.PrefetchScalarGridSpec(
            num_scalar_prefetch=len(scalars),
            grid=grid,
            in_specs=specs,
            out_specs=[spec for _, _, spec in outputs],
            scratch_shapes=list(scratch),
        ),
        out_shape=shapes,
        compiler_params=pltpu.CompilerParams(vmem_limit_bytes=VMEM_LIMIT),
        cost_estimate=pl.CostEstimate(flops=int(us * PER_US), bytes_accessed=int(moved / 100), transcendentals=0),
        name=name,
    )(*scalars, *[array for array, _ in inputs], *after)


def full(*shape):
    return pl.BlockSpec(shape, lambda *_: (0,) * len(shape))


CORE_INDEX, SEQ_INDEX, POSITION = range(3)


def store_slabs(out_ref, value, facts_ref, first, slab, columns=slice(None)):
    for k in range(value.shape[0] // slab):
        row = pl.multiple_of(facts_ref[first + k] * slab, slab)
        out_ref[pl.ds(row, slab), columns] = value[k * slab : (k + 1) * slab]


def side_by_side(ref):
    return jnp.concatenate([ref[k] for k in range(ref.shape[0])], axis=1)


def put_blocks(ref, value, rows=slice(None)):
    for k in range(ref.shape[0]):
        ref[k, rows, :] = value[:, k * LANES : (k + 1) * LANES]

def two_heads(value, low):
    zero = jnp.zeros_like(value)
    return jnp.concatenate([jnp.where(low, value, zero), jnp.where(low, zero, value)], axis=0)


def one_of_two(value, size):
    feature = lax.broadcasted_iota(jnp.int32, (LANES, size), 0)
    return jnp.where(feature < HEAD_DIM, value[:, :size], value[:, size:])


class Spans:
    def __init__(self, rows, group):
        self.rows, self.group = rows, group
        self.size = min(128, group)
        self.blocks = group // self.size
        self.count = rows * self.blocks
        self.window = self.size + WINDOW

    def queries(self, at):
        return slice(at * self.size, (at + 1) * self.size)

    def keys(self, own_ref, rim_ref, pair, at):
        row, block = divmod(at, self.blocks)
        start = at * self.size
        if block == 0:
            rim = rim_ref[pair, row * WINDOW : (row + 1) * WINDOW, :]
            return jnp.concatenate([rim, own_ref[pair, start : start + self.size, :]], axis=0)
        return own_ref[pair, start - WINDOW : start + self.size, :]

    def fill_bias(self, bias_ref, starts_ref, facts_ref):
        size = self.size
        key = lax.broadcasted_iota(jnp.int32, (self.window, size), 0) - WINDOW
        query = lax.broadcasted_iota(jnp.int32, (self.window, size), 1)
        near = (key <= query) & (query - key <= WINDOW)
        for at in range(self.count):
            row, block = divmod(at, self.blocks)
            begin = starts_ref[row : row + 1, block * size : (block + 1) * size]
            begin = begin - facts_ref[POSITION] - block * size
            bias = jnp.where(near & (key >= begin), 0.0, masked_value).astype(F32)
            bias_ref[at, :, :size] = bias
            bias_ref[at, :, size:] = bias

    def scratch(self, kind):
        return pltpu.VMEM((self.count, self.window, 2 * self.size), kind)


def softmax(scores):
    weights = jnp.exp(scores - jnp.max(scores, axis=0, keepdims=True))
    return weights * (1.0 / jnp.sum(weights, axis=0, keepdims=True))


def attend_kernel(facts_ref, starts_ref, q_ref, k_ref, v_ref, kr_ref, vr_ref,
                  att_ref, attT_ref, bias_ref, score_ref, probs_ref, *, spans, slab, put, pairs):
    step = pl.program_id(0)
    size, count = spans.size, spans.count

    @pl.when(step == 0)
    def _():
        spans.fill_bias(bias_ref, starts_ref, facts_ref)

    low = lax.broadcasted_iota(jnp.int32, (size, LANES), 1) < HEAD_DIM
    for pair in range(pairs):
        for at in range(count):
            queries = q_ref[pair, spans.queries(at), :] * jnp.asarray(HEAD_DIM ** (-0.5), BF16)
            keys = spans.keys(k_ref, kr_ref, pair, at)
            score_ref[at] = dot(keys, two_heads(queries, low), 1, 1)
        for at in range(count):
            probs_ref[at] = softmax(score_ref[at] + bias_ref[at]).astype(BF16)
        for at in range(count):
            values = spans.keys(v_ref, vr_ref, pair, at)
            mixed = one_of_two(dot(values, probs_ref[at], 0, 0), size)
            att_ref[pair, spans.queries(at), :] = mixed.T.astype(BF16)
            first = put + (step * pairs + pair) * (LANES // slab)
            store_slabs(attT_ref, mixed.astype(BF16), facts_ref, first, slab, spans.queries(at))


def attend(qkv, kv_rim, doc_start, facts, put, slab, after=()):
    rows, group = doc_start.shape
    all_pairs, tokens = qkv.shape[0] // 3, qkv.shape[1]
    rim = kv_rim.shape[1]
    spans = Spans(rows, group)
    steps = all_pairs // PAIRS
    own = lambda kind: pl.BlockSpec((PAIRS, tokens, LANES), lambda j, *_: (kind * steps + j, 0, 0))
    edge = lambda kind: pl.BlockSpec((PAIRS, rim, LANES), lambda j, *_: (kind * steps + j, 0, 0))
    width = all_pairs * LANES
    return launch(
        functools.partial(attend_kernel, spans=spans, slab=slab, put=put, pairs=PAIRS),
        "attend",
        (steps,),
        [facts],
        [
            (doc_start, full(rows, group)),
            (qkv, own(0)),
            (qkv, own(1)),
            (qkv, own(2)),
            (kv_rim, edge(0)),
            (kv_rim, edge(1)),
        ],
        [
            ((all_pairs, tokens, LANES), BF16, own(0)),
            ((width, tokens), BF16, full(width, tokens)),
        ],
        [spans.scratch(F32), spans.scratch(F32), spans.scratch(BF16)],
        us=8,
        after=after,
    )


def attend_back_kernel(facts_ref, starts_ref, q_ref, k_ref, v_ref, kr_ref, vr_ref, da_ref,
                       dqkv_ref, drim_ref,
                       bias_ref, score_ref, grad_ref, probs_ref, dscore_ref, *, spans, pairs):
    size, count = spans.size, spans.count

    @pl.when(pl.program_id(0) == 0)
    def _():
        spans.fill_bias(bias_ref, starts_ref, facts_ref)

    low = lax.broadcasted_iota(jnp.int32, (size, LANES), 1) < HEAD_DIM
    scale = HEAD_DIM ** (-0.5)

    def scaled_queries(pair, at):
        return two_heads(q_ref[pair, spans.queries(at), :] * jnp.asarray(scale, BF16), low)

    for pair in range(pairs):
        for at in range(count):
            score_ref[at] = dot(spans.keys(k_ref, kr_ref, pair, at), scaled_queries(pair, at), 1, 1)
            grads = two_heads(da_ref[pair, spans.queries(at), :], low)
            grad_ref[at] = dot(spans.keys(v_ref, vr_ref, pair, at), grads, 1, 1)
        for at in range(count):
            probs = softmax(score_ref[at] + bias_ref[at])
            probs_ref[at] = probs.astype(BF16)
            part = probs * grad_ref[at]
            dscore_ref[at] = (part - probs * jnp.sum(part, axis=0, keepdims=True)).astype(BF16)
        late = [None, None]
        for at in range(count):
            here = spans.queries(at)
            row, block = divmod(at, spans.blocks)
            dscores = dscore_ref[at]
            grads = two_heads(da_ref[pair, here, :], low)
            dk = dot(dscores, scaled_queries(pair, at))
            dv = dot(probs_ref[at], grads)
            dq = one_of_two(dot(spans.keys(k_ref, kr_ref, pair, at), dscores, 0, 0), size) * scale
            dqkv_ref[0, pair, here, :] = dq.T.astype(BF16)
            start = at * size
            for kind, grad in ((0, dk), (1, dv)):
                out_ref, rim_ref = dqkv_ref.at[kind + 1], drim_ref.at[kind]
                early = grad[:WINDOW]
                if block == 0:
                    rim_ref[pair, row * WINDOW : (row + 1) * WINDOW, :] = early.astype(BF16)
                else:
                    out_ref[pair, start - WINDOW : start, :] = (late[kind] + early).astype(BF16)
                if size > WINDOW:
                    out_ref[pair, start : start + size - WINDOW, :] = grad[WINDOW:size].astype(BF16)
                late[kind] = grad[size:]
                if block == spans.blocks - 1:
                    out_ref[pair, start + size - WINDOW : start + size, :] = late[kind].astype(BF16)


def attend_back(qkv, kv_rim, doc_start, facts, grad_att, after=()):
    rows, group = doc_start.shape
    all_pairs, tokens = qkv.shape[0] // 3, qkv.shape[1]
    rim = kv_rim.shape[1]
    spans = Spans(rows, group)
    steps = all_pairs // PAIRS
    own = lambda kind: pl.BlockSpec((PAIRS, tokens, LANES), lambda j, *_: (kind * steps + j, 0, 0))
    edge = lambda kind: pl.BlockSpec((PAIRS, rim, LANES), lambda j, *_: (kind * steps + j, 0, 0))
    return launch(
        functools.partial(attend_back_kernel, spans=spans, pairs=PAIRS),
        "attend_back",
        (steps,),
        [facts],
        [
            (doc_start, full(rows, group)),
            (qkv, own(0)),
            (qkv, own(1)),
            (qkv, own(2)),
            (kv_rim, edge(0)),
            (kv_rim, edge(1)),
            (grad_att, own(0)),
        ],
        [
            ((3, all_pairs, tokens, LANES), BF16, pl.BlockSpec((3, PAIRS, tokens, LANES), lambda j, *_: (0, j, 0, 0))),
            ((2, all_pairs, rim, LANES), BF16, pl.BlockSpec((2, PAIRS, rim, LANES), lambda j, *_: (0, j, 0, 0))),
        ],
        [spans.scratch(kind) for kind in (F32, F32, F32, BF16, BF16)],
        us=8,
        after=after,
    )


def norm_matmul_kernel(facts_ref, x_ref, gain_ref, w_ref, out_ref, normedT_ref, tail_ref, normed_ref, *, slab, put, step, tails):
    @pl.when(pl.program_id(0) == 0)
    def _():
        for at in range(0, x_ref.shape[0], step):
            x = x_ref[at : at + step, :].astype(F32)
            inv = lax.rsqrt(jnp.mean(x * x, axis=-1, keepdims=True) + epsilon)
            normed = (x * inv * gain_ref[...]).astype(BF16)
            normed_ref[at : at + step, :] = normed
            store_slabs(normedT_ref, normed.T, facts_ref, put, slab, slice(at, at + step))

        for k, end in enumerate(tails):
            tail_ref[k * WINDOW : (k + 1) * WINDOW, :] = x_ref[end - WINDOW : end, :]

    put_blocks(out_ref, dot(normed_ref[...], w_ref[...]).astype(BF16))


def norm_matmul(x, gain, weight, first_column, facts, put, slab, tails, after=()):
    tokens, width = x.shape
    columns = weight.shape[1] - first_column
    tile = 1024
    skip, wide = first_column // tile, tile // LANES
    return launch(
        functools.partial(norm_matmul_kernel, slab=slab, put=put, step=min(STEP, tokens), tails=tails),
        "norm_matmul",
        (columns // tile,),
        [facts],
        [
            (x, full(tokens, width)),
            (gain[None], full(1, width)),
            (weight, pl.BlockSpec((width, tile), lambda j, *_: (0, skip + j))),
        ],
        [
            ((columns // LANES, tokens, LANES), BF16, pl.BlockSpec((wide, tokens, LANES), lambda j, *_: (j, 0, 0))),
            ((width, tokens), BF16, full(width, tokens)),
            ((len(tails) * WINDOW, width), BF16, full(len(tails) * WINDOW, width)),
        ],
        [pltpu.VMEM((tokens, width), BF16)],
        us=8,
        after=after,
    )


def turn_kernel(facts_ref, x_ref, out_ref, *, slab, put):
    store_slabs(out_ref, x_ref[...].T, facts_ref, put, slab)


def turn(x, facts, put, slab, after=()):
    tokens, width = x.shape
    step = 2 * STEP
    return launch(
        functools.partial(turn_kernel, slab=slab, put=put),
        "turn",
        (tokens // step,),
        [facts],
        [(x, pl.BlockSpec((step, width), lambda m, *_: (m, 0)))],
        [((width, tokens), BF16, pl.BlockSpec((width, step), lambda m, *_: (0, m)))],
        us=8,
        after=after,
    )[0]


def out_proj_kernel(facts_ref, att_ref, w_ref, x_ref, gain_ref, resid_ref, normed_ref, normedT_ref, *, slab, put):
    resid = x_ref[...].astype(F32) + dot(side_by_side(att_ref), w_ref[...])
    resid_ref[...] = resid.astype(BF16)
    inv = lax.rsqrt(jnp.mean(resid * resid, axis=-1, keepdims=True) + epsilon)
    normed = (resid * inv * gain_ref[...]).astype(BF16)
    normed_ref[...] = normed
    store_slabs(normedT_ref, normed.T, facts_ref, put, slab)


def out_proj(att, w_out, x, gain, facts, put, slab, after=()):
    tokens, width = x.shape
    pairs = att.shape[0]
    step = 2 * STEP
    rows = pl.BlockSpec((step, width), lambda m, *_: (m, 0))
    return launch(
        functools.partial(out_proj_kernel, slab=slab, put=put),
        "out_proj",
        (tokens // step,),
        [facts],
        [
            (att, pl.BlockSpec((pairs, step, LANES), lambda m, *_: (0, m, 0))),
            (w_out, full(width, width)),
            (x, rows),
            (gain[None], full(1, width)),
        ],
        [
            ((tokens, width), BF16, rows),
            ((tokens, width), BF16, rows),
            ((width, tokens), BF16, pl.BlockSpec((width, step), lambda m, *_: (0, m))),
        ],
        us=8,
        after=after,
    )


def ff_kernel(*refs, first, given, ends):
    normed_ref, dy_ref, dyT_ref, normedT_ref, wg_ref, wu0_ref, wu1_ref, wu2_ref, wd_ref = refs[:9]
    rest = list(refs[9:])
    total_in = rest.pop(0) if given else None
    if ends:
        resid_ref, gain_ref, w_out_ref = rest[:3]
        rest = rest[3:]
    hidden_ref, dgu_ref, send_down, send_gate, send_up, *totals, acc_ref = rest
    tile = pl.program_id(0)
    tokens = normed_ref.shape[0]

    @pl.when(tile == 0)
    def _():
        acc_ref[...] = total_in[...] if given else jnp.zeros_like(acc_ref)

    half = FF % LANES
    w_both = jnp.concatenate([wg_ref[...], wu0_ref[:, half:], wu1_ref[...], wu2_ref[:, :half]], axis=1)
    limit = FF - (tile + first) * FF_TILE
    inside = lax.broadcasted_iota(jnp.int32, (STEP, FF_TILE), 1) < limit

    def products(at):
        here = slice(at, at + STEP)
        both = dot(normed_ref[here, :], w_both)
        return both[:, :FF_TILE], both[:, FF_TILE:], dot(dy_ref[here, :], wd_ref[...], 1, 1)

    def act(at, gate, up, back):
        here = slice(at, at + STEP)
        sigma = 1.0 / (1.0 + jnp.exp(-gate))
        silu = gate * sigma
        hidden_ref[here, :] = jnp.where(inside, silu * up, 0.0).astype(BF16)
        dgate = back * up * (sigma * (1.0 + gate * (1.0 - sigma)))
        dgu_ref[0, here, :] = jnp.where(inside, dgate, 0.0).astype(BF16)
        dgu_ref[1, here, :] = jnp.where(inside, back * silu, 0.0).astype(BF16)

    def norm_grad(at):
        here = slice(at, at + STEP)
        grads = jnp.concatenate([dgu_ref[0, here, :], dgu_ref[1, here, :]], axis=1)
        acc_ref[here, :] += dot(grads, w_both, 1, 1)

    held = products(0)
    for at in range(0, tokens, STEP):
        ahead = products(at + STEP) if at + STEP < tokens else None
        act(at, *held)
        norm_grad(at)
        held = ahead
    send_down[...] = dot(dyT_ref[...], hidden_ref[...]).astype(BF16)
    both = dot(normedT_ref[...], jnp.concatenate([dgu_ref[0], dgu_ref[1]], axis=1)).astype(BF16)
    send_gate[...] = both[:, :FF_TILE]
    send_up[...] = both[:, FF_TILE:]

    @pl.when(tile == pl.num_programs(0) - 1)
    def _():
        if not ends:
            totals[0][...] = acc_ref[...]
            return
        drb_ref, da_ref = totals
        for at in range(0, tokens, STEP):
            here = slice(at, at + STEP)
            grad = norm_back(acc_ref[here, :], resid_ref[here, :].astype(F32), gain_ref[...])
            branch = (dy_ref[here, :].astype(F32) + grad).astype(BF16)
            put_blocks(drb_ref, branch, here)
            put_blocks(da_ref, dot(branch, w_out_ref[...], 1, 1).astype(BF16), here)


def feed_forward(normed, dy, dy_turned, normed_turned, w_gate_up, w_down, first, count, total=None, end=None, after=()):
    tokens, width = normed.shape
    wide = count * FF_TILE
    last = w_gate_up.shape[1] // LANES - 1
    skip = FF // LANES + first * (FF_TILE // LANES)
    up = lambda k: pl.BlockSpec(
        (width, LANES), lambda j: (0, jnp.minimum(skip + k + j * (FF_TILE // LANES), last))
    )
    other_half = full(width // 2, tokens)
    given = [] if total is None else [(total, full(tokens, width))]
    ending, results = [], [((tokens, width), F32, full(tokens, width))]
    if end is not None:
        resid, gain, w_out = end
        ending = [(resid, full(tokens, width)), (gain[None], full(1, width)), (w_out, full(width, width))]
        blocks = (width // LANES, tokens, LANES)
        results = [(blocks, BF16, full(*blocks))] * 2
    return launch(
        functools.partial(ff_kernel, first=first, given=len(given), ends=end is not None),
        "feed_forward",
        (count,),
        [],
        [
            (normed, full(tokens, width)),
            (dy, full(tokens, width)),
            (dy_turned, other_half),
            (normed_turned, other_half),
            (w_gate_up, pl.BlockSpec((width, FF_TILE), lambda j: (0, first + j))),
            (w_gate_up, up(0)),
            (w_gate_up, up(1)),
            (w_gate_up, up(2)),
            (w_down.T, pl.BlockSpec((FF_TILE, width), lambda j: (first + j, 0))),
        ]
        + given
        + ending,
        [
            ((tokens, wide), BF16, pl.BlockSpec((tokens, FF_TILE), lambda j: (0, j))),
            ((2, tokens, wide), BF16, pl.BlockSpec((2, tokens, FF_TILE), lambda j: (0, 0, j))),
        ]
        + [((width // 2, wide), BF16, pl.BlockSpec((width // 2, FF_TILE), lambda j: (0, j)))] * 3
        + results,
        [pltpu.VMEM((tokens, width), F32)],
        us=8,
        after=after,
    )


def ff_grad_kernel(facts_ref, dyT_ref, normedT_ref, hidden_ref, dgu_ref, got_down, got_gate, got_up, send_ref, keep_ref, *, bit):
    part = send_ref.shape[1]
    own = facts_ref[bit]
    rights = (hidden_ref[...], dgu_ref[0], dgu_ref[1])
    lefts, gots = (dyT_ref, normedT_ref, normedT_ref), (got_down, got_gate, got_up)
    for kind, (left_ref, right, got_ref) in enumerate(zip(lefts, rights, gots)):
        for out_ref, index in ((send_ref, 1 - own), (keep_ref, own)):
            rows = pl.ds(pl.multiple_of(index * part, part), part)
            total = dot(left_ref[rows, :], right) + got_ref[rows, :].astype(F32)
            out_ref[kind] = total.astype(BF16)


def ff_grad(facts, bit, dy_turned, normed_turned, hidden, dgu, got, after=()):
    width, tokens = dy_turned.shape
    wide = hidden.shape[1]
    tile = 512 if wide % 512 == 0 else FF_TILE
    own_half = pl.BlockSpec((width // 2, tokens), lambda j, *_: (1, 0))
    part = ((3, width // 4, wide), BF16, pl.BlockSpec((3, width // 4, tile), lambda j, *_: (0, 0, j)))
    return launch(
        functools.partial(ff_grad_kernel, bit=bit),
        "ff_grad",
        (wide // tile,),
        [facts],
        [
            (dy_turned, own_half),
            (normed_turned, own_half),
            (hidden, pl.BlockSpec((tokens, tile), lambda j, *_: (0, j))),
            (dgu, pl.BlockSpec((2, tokens, tile), lambda j, *_: (0, 0, j))),
        ]
        + [(part, pl.BlockSpec((width // 2, tile), lambda j, *_: (0, j))) for part in got],
        [part, part],
        us=8,
        after=after,
    )


def norm_back(grad, values, gain):
    inv = lax.rsqrt(jnp.mean(values * values, axis=-1, keepdims=True) + epsilon)
    scaled = grad * gain
    return inv * scaled - values * (inv * inv * inv) * jnp.mean(scaled * values, axis=-1, keepdims=True)


def ff_out_kernel(*refs):
    wd_ref, resid_ref, out_ref = refs[-3:]
    total, first = resid_ref[...].astype(F32), 0
    for hidden_ref in refs[:-3]:
        count = min(hidden_ref.shape[1], FF - first)
        total += dot(hidden_ref[:, :count], wd_ref[first : first + count, :])
        first += count
    out_ref[...] = total.astype(BF16)


def ff_out(hiddens, w_down, resid, after=()):
    tokens, width = resid.shape
    rows = lambda columns: pl.BlockSpec((STEP, columns), lambda m: (m, 0))
    return launch(
        ff_out_kernel,
        "ff_out",
        (tokens // STEP,),
        [],
        [(hidden, rows(hidden.shape[1])) for hidden in hiddens]
        + [(w_down.T, full(FF, width)), (resid, rows(width))],
        [((tokens, width), BF16, rows(width))],
        us=1,
        after=after,
    )[0]


def att_grad_kernel(facts_ref, *refs, bit):
    split = bit is not None
    attT_ref, oneT_ref, rimT_ref, drb_ref, dqkv_ref, drim_ref = refs[:6]
    kind = pl.program_id(0)

    def put(total, index):
        if split:
            got_ref = refs[6 + index]
            send_ref, keep_ref = refs[-2:]
            part = send_ref.shape[0]
            own = facts_ref[bit]
            for out_ref, half in ((send_ref, 1 - own), (keep_ref, own)):
                rows = pl.ds(pl.multiple_of(half * part, part), part)
                out_ref[...] = (total(rows) + got_ref[rows, :].astype(F32)).astype(BF16)
        else:
            refs[6 + index][...] = total(slice(None)).astype(BF16)

    @pl.when(kind == 0)
    def _():
        right = side_by_side(drb_ref)
        put(lambda rows: dot(attT_ref[rows, :], right), 0)

    @pl.when(kind == 1)
    def _():
        right = side_by_side(dqkv_ref)
        put(lambda rows: dot(oneT_ref[rows, :], right), 1)

    for index in (2, 3):

        @pl.when(kind == index)
        def _():
            right, rim = side_by_side(dqkv_ref), side_by_side(drim_ref)
            put(lambda rows: dot(oneT_ref[rows, :], right) + dot(rimT_ref[rows, :], rim), index)


def att_grad(facts, att_turned, one_turned, rim_turned, drb, dqkv, drim, bit=None, got=None, us=8, after=()):
    width, tokens = one_turned.shape
    rim = rim_turned.shape[1]
    split = got is not None
    half = 1 if split else 0
    inputs = [
        (turned, pl.BlockSpec((width // 2, turned.shape[1]), lambda j, *_: (half, 0)))
        for turned in (att_turned, one_turned, rim_turned)
    ]
    blocks = width // LANES
    inputs += [
        (drb, full(blocks, tokens, LANES)),
        (dqkv, pl.BlockSpec((None, blocks, tokens, LANES), lambda j, *_: (jnp.maximum(j - 1, 0), 0, 0, 0))),
        (drim, pl.BlockSpec((None, blocks, rim, LANES), lambda j, *_: (jnp.maximum(j - 2, 0), 0, 0, 0))),
    ]
    columns = 4 * width
    parts = [full(width // 2, width)] * 4
    if split:
        inputs += list(zip(got, parts))
        part = ((width // 4, columns), BF16, pl.BlockSpec((width // 4, width), lambda j, *_: (0, j)))
        outputs = [part, part]
    else:
        outputs = [((width // 2, width), BF16, spec) for spec in parts]
    return launch(
        functools.partial(att_grad_kernel, bit=bit),
        "att_grad",
        (4,),
        [facts],
        inputs,
        outputs,
        us=us,
        after=after,
    )


def input_grad_kernel(dqkv_ref, w_ref, x_ref, gain_ref, drb_ref, back_ref, out_ref, acc_ref, *, rows, group):
    k = pl.program_id(0)
    tokens = acc_ref.shape[0]
    part = dot(side_by_side(dqkv_ref), w_ref[...], 1, 1)

    @pl.when(k == 0)
    def _():
        acc_ref[...] = part

    @pl.when(k > 0)
    def _():
        acc_ref[...] += part

    @pl.when(k == 2)
    def _():
        for at in range(0, tokens, STEP):
            here = slice(at, at + STEP)
            grad = norm_back(acc_ref[here, :], x_ref[here, :].astype(F32), gain_ref[...])
            out_ref[here, :] = grad + side_by_side(drb_ref.at[:, here, :]).astype(F32)
        for row in range(rows):
            tail = slice((row + 1) * group - WINDOW, (row + 1) * group)
            out_ref[tail, :] += back_ref[row * WINDOW : (row + 1) * WINDOW, :].astype(F32)


def input_grad(dqkv, w_qkv, x, gain, drb, back, rows, group, after=()):
    tokens, width = x.shape
    whole = full(tokens, width)
    return launch(
        functools.partial(input_grad_kernel, rows=rows, group=group),
        "input_grad",
        (3,),
        [],
        [
            (dqkv, pl.BlockSpec((None, width // LANES, tokens, LANES), lambda j: (j, 0, 0, 0))),
            (w_qkv, pl.BlockSpec((width, width), lambda j: (0, j))),
            (x, whole),
            (gain[None], full(1, width)),
            (drb, full(*drb.shape)),
            (back, full(rows * WINDOW, width)),
        ],
        [((tokens, width), F32, whole)],
        [pltpu.VMEM((tokens, width), F32)],
        us=8,
        after=after,
    )[0]


def rim_grad_kernel(drim_ref, wk_ref, wv_ref, x_ref, gain_ref, out_ref):
    grad = dot(side_by_side(drim_ref.at[0]), wk_ref[...], 1, 1)
    grad += dot(side_by_side(drim_ref.at[1]), wv_ref[...], 1, 1)
    out_ref[...] = norm_back(grad, x_ref[...].astype(F32), gain_ref[...]).astype(BF16)


def rim_grad(drim, w_qkv, x, gain, after=()):
    rim, width = x.shape
    part = lambda k: pl.BlockSpec((width, width), lambda j: (0, k))
    return launch(
        rim_grad_kernel,
        "rim_grad",
        (1,),
        [],
        [
            (drim, full(*drim.shape)),
            (w_qkv, part(1)),
            (w_qkv, part(2)),
            (x, full(rim, width)),
            (gain[None], full(1, width)),
        ],
        [((rim, width), BF16, full(rim, width))],
        us=8,
        after=after,
    )[0]


def add_kernel(facts_ref, *refs, bits):
    count = len(bits)
    for k, bit in enumerate(bits):
        keep_ref, got_ref = refs[2 * k : 2 * k + 2]
        outs = refs[2 * count + 2 * k : 2 * count + 2 * k + 2]
        for out_ref, index in zip(outs, (1 - facts_ref[bit], facts_ref[bit])):
            out_ref[...] = (keep_ref[:, index].astype(F32) + got_ref[:, index].astype(F32)).astype(BF16)


def add_and_cut(facts, items, after=()):
    inputs, outputs = [], []
    for keep, got, _ in items:
        kinds, rows, columns = keep.shape
        cut = lambda value: value.reshape(kinds, 2, rows // 2, columns)
        spec = pl.BlockSpec((kinds, 2, rows // 2, columns // 2), lambda j, *_: (0, 0, 0, j))
        inputs += [(cut(keep), spec), (cut(got), spec)]
        part = pl.BlockSpec((kinds, rows // 2, columns // 2), lambda j, *_: (0, 0, j))
        outputs += [((kinds, rows // 2, columns), BF16, part)] * 2
    kernel = functools.partial(add_kernel, bits=[bit for _, _, bit in items])
    parts = launch(kernel, "add_and_cut", (2,), [facts], inputs, outputs, us=8, after=after)
    return [(parts[2 * k], parts[2 * k + 1]) for k in range(len(items))]


def log2(count):
    return count.bit_length() - 1


def stage_orders(n_dp, n_seq, flavour):
    dp = [("dp", bit) for bit in range(1, log2(n_dp))]
    if flavour:
        dp = dp[::-1]
    seq = [("seq", bit) for bit in range(log2(n_seq))]
    return dp + seq, seq[:1] + dp + seq[1:]


def row_bits(n_dp, n_seq):
    return [("seq", bit) for bit in reversed(range(log2(n_seq)))] + [
        ("dp", bit) for bit in reversed(range(log2(n_dp)))
    ]


def block_places(n_dp, n_seq, flavour):
    bits, orders = row_bits(n_dp, n_seq), stage_orders(n_dp, n_seq, flavour)
    count = n_dp * n_seq
    tables = []
    for core in range(2):
        table = []
        for block in range(count):
            value = {step: (block >> (len(bits) - 1 - k)) & 1 for k, step in enumerate(bits)}
            owner = value[("dp", 0)]
            place = 0
            for step in orders[owner]:
                place = place * 2 + value[step]
            table.append(place + (count // 2 if owner == core else 0))
        tables.append(np.array(table, np.int32))
    return tables


def swap_pairs(n_dp, n_seq, steps):
    pairs = []
    for d in range(n_dp):
        for s in range(n_seq):
            axis, bit = steps[d % 2]
            there = (d ^ (1 << bit), s) if axis == "dp" else (d, s ^ (1 << bit))
            pairs.append((d * n_seq + s, there[0] * n_seq + there[1]))
    return pairs


def swap(value, steps):
    n_dp, n_seq = lax.axis_size("dp"), lax.axis_size("seq")
    return lax.ppermute(value, ("dp", "seq"), swap_pairs(n_dp, n_seq, steps))


def gather_steps(n_dp):
    dims = [("dp", bit) for bit in range(1, log2(n_dp))]
    return list(zip(dims[::-1], dims))


def stage_fact(n_dp, n_seq, flavour, stage):
    return 3 + flavour * (log2(n_dp * n_seq) - 1) + stage


def gather_fact(n_dp, n_seq, step):
    return 3 + 2 * (log2(n_dp * n_seq) - 1) + step


def places_fact(n_dp, n_seq, flavour, count):
    return gather_fact(n_dp, n_seq, log2(n_dp)) + flavour * count


def facts_table(n_dp, n_seq, group, places):
    table = []
    for d in range(n_dp):
        for s in range(n_seq):
            core = d & 1
            bit = lambda steps: ((d if steps[core][0] == "dp" else s) >> steps[core][1]) & 1
            row = [core, s, s * group]
            for flavour in range(2):
                row += [bit(steps) for steps in zip(*stage_orders(n_dp, n_seq, flavour))]
            row += [bit(steps) for steps in gather_steps(n_dp)] + [0]
            assert len(row) == places_fact(n_dp, n_seq, 0, 0)
            for flavour in range(2):
                row += list(places[flavour][core])
            table.append(row)
    return np.array(table, np.int32)


CORE = (("dp", 0), ("dp", 0))


class Chunk:
    def __init__(self, flavour):
        self.sizes = lax.axis_size("dp"), lax.axis_size("seq")
        self.flavour = flavour
        self.stages = list(zip(*stage_orders(*self.sizes, flavour)))
        self.done = 0

    def bit(self):
        return stage_fact(*self.sizes, self.flavour, self.done)

    def between_cores(self, *parts):
        self.got = [swap(part, CORE) for part in parts]

    def go(self, send, keep):
        self.keep = keep
        self.got = swap(send, self.stages[self.done])
        self.done += 1

    @property
    def last(self):
        return self.done == len(self.stages)


def advance(facts, *chunks, after=()):
    parts = add_and_cut(facts, [(chunk.keep, chunk.got, chunk.bit()) for chunk in chunks], after=after)
    for chunk, (send, keep) in zip(chunks, parts):
        chunk.go(send, keep)
    return parts[0][0]


def finish_kernel(*refs):
    out_ref, first = refs[-1], 0
    for keep_ref, got_ref in zip(refs[:-1:2], refs[1:-1:2]):
        columns = keep_ref.shape[2]
        total = keep_ref[...].astype(F32) + got_ref[...].astype(F32)
        out_ref[:, :, first : first + columns] = total.astype(BF16)
        first += columns


def finish(*chunks, us=8, after=()):
    kinds, part, _ = chunks[0].keep.shape
    inputs = [(array, full(*array.shape)) for chunk in chunks for array in (chunk.keep, chunk.got)]
    shape = (kinds, part, sum(chunk.keep.shape[2] for chunk in chunks))
    return launch(finish_kernel, "finish", (1,), [], inputs, [(shape, BF16, full(*shape))], us=us, after=after)[0]


def join_kernel(facts_ref, value_ref, got_ref, out_ref, *, bit):
    count = value_ref.shape[1]
    first = facts_ref[bit] * count
    out_ref[:, pl.ds(first, count)] = value_ref[...]
    out_ref[:, pl.ds(count - first, count)] = got_ref[...]


class Gather:
    def __init__(self, facts, value):
        self.facts = facts
        n_dp = lax.axis_size("dp")
        self.dims = [("dp", bit) for bit in range(1, log2(n_dp))]
        self.steps = gather_steps(n_dp)
        self.kinds, self.part, self.columns = value.shape
        self.value = value[:, None]
        self.done = 0
        self.send()

    @property
    def last(self):
        return self.done == len(self.steps)

    def send(self):
        self.got = swap(self.value, CORE if self.last else self.steps[self.done])

    def step(self, us=8, after=()):
        bit = gather_fact(lax.axis_size("dp"), lax.axis_size("seq"), self.done)
        kinds, count, part, columns = self.value.shape
        tile = columns // 2
        spec = lambda count: pl.BlockSpec((kinds, count, part, tile), lambda j, *_: (0, 0, 0, j))
        (self.value,) = launch(
            functools.partial(join_kernel, bit=bit),
            "join",
            (2,),
            [self.facts],
            [(self.value, spec(count)), (self.got, spec(count))],
            [((kinds, 2 * count, part, columns), BF16, spec(2 * count))],
            us=us,
            after=after,
        )
        self.done += 1
        self.send()
        return self.value

    def whole(self):
        dims = self.dims
        core = lax.axis_index("dp") & 1
        halves = []
        for which, order in enumerate((dims[::-1], dims)):
            half = jnp.where(core == which, self.value, self.got)
            half = half.reshape((self.kinds,) + (2,) * len(dims) + (self.part, self.columns))
            wanted = [1 + order[::-1].index(step) for step in dims[::-1]]
            halves.append(half.transpose([0] + wanted + [len(dims) + 1, len(dims) + 2]))
        whole = jnp.stack(halves, axis=len(dims) + 1)
        return whole.reshape(self.kinds, lax.axis_size("dp") * self.part, self.columns)


def natural_rows(facts_ref, own_ref, got_ref, kind, step, columns):
    pieces = []
    for x in range(2):
        for which in range(2):
            index = x * 2 + step if which == 0 else step * 2 + x
            own, got = own_ref[kind, index, :, columns], got_ref[kind, index, :, columns]
            pieces.append(jnp.where(facts_ref[CORE_INDEX] == which, own, got))
    return jnp.concatenate(pieces, axis=0).astype(F32)


def row_sums(value):
    total = jnp.sum(value, axis=1, keepdims=True)
    return jnp.broadcast_to(total, (total.shape[0], LANES)).T[:1, :]


def put_ff_kernel(facts_ref, own_ref, got_ref, w_ref, gain_ref, gate_up_ref, down_ref, dgain_ref):
    step = pl.program_id(0)
    rows = lambda kind: natural_rows(facts_ref, own_ref, got_ref, kind, step, slice(0, FF))
    down_ref[...] = rows(0).T
    gate, up = rows(1), rows(2)
    gate_up_ref[:, :FF] = gate
    gate_up_ref[:, FF:] = up
    weight = w_ref[...].astype(F32)
    total = row_sums(gate * weight[:, :FF]) + row_sums(up * weight[:, FF:])
    dgain_ref[...] = total / gain_ref[...]


def put_ff(gather, w_gate_up, gain, after=()):
    kept = 8 * gather.part
    half = kept // 2
    whole = full(*gather.value.shape)
    return launch(
        put_ff_kernel,
        "put_ff",
        (2,),
        [gather.facts],
        [
            (gather.value, whole),
            (gather.got, whole),
            (w_gate_up, pl.BlockSpec((half, 2 * FF), lambda j, facts: (2 * facts[SEQ_INDEX] + j, 0))),
            (gain[None], pl.BlockSpec((1, half), lambda j, facts: (0, 2 * facts[SEQ_INDEX] + j))),
        ],
        [
            ((kept, 2 * FF), F32, pl.BlockSpec((half, 2 * FF), lambda j, *_: (j, 0))),
            ((FF, kept), F32, pl.BlockSpec((FF, half), lambda j, *_: (0, j))),
            ((1, kept), F32, pl.BlockSpec((1, half), lambda j, *_: (0, j))),
        ],
        us=8,
        after=after,
    )


def put_att_kernel(facts_ref, own_ref, got_ref, w_ref, gain_ref, qkv_ref, out_ref, dgain_ref):
    step = pl.program_id(0)
    width = out_ref.shape[1]
    out_ref[...] = natural_rows(facts_ref, own_ref, got_ref, 0, step, slice(0, width))
    qkv = natural_rows(facts_ref, own_ref, got_ref, 0, step, slice(width, 4 * width))
    qkv_ref[...] = qkv
    dgain_ref[...] = row_sums(qkv * w_ref[...].astype(F32)) / gain_ref[...]


def put_att(gather, w_qkv, gain, after=()):
    kept = 8 * gather.part
    half, width = kept // 2, gather.columns // 4
    whole = full(*gather.value.shape)
    return launch(
        put_att_kernel,
        "put_att",
        (2,),
        [gather.facts],
        [
            (gather.value, whole),
            (gather.got, whole),
            (w_qkv, pl.BlockSpec((half, 3 * width), lambda j, facts: (2 * facts[SEQ_INDEX] + j, 0))),
            (gain[None], pl.BlockSpec((1, half), lambda j, facts: (0, 2 * facts[SEQ_INDEX] + j))),
        ],
        [
            ((kept, 3 * width), F32, pl.BlockSpec((half, 3 * width), lambda j, *_: (j, 0))),
            ((kept, width), F32, pl.BlockSpec((half, width), lambda j, *_: (j, 0))),
            ((1, kept), F32, pl.BlockSpec((1, half), lambda j, *_: (0, j))),
        ],
        us=8,
        after=after,
    )


def place_rows(turned, places):
    count = places.shape[0]
    blocks = turned.reshape((count, turned.shape[0] // count) + turned.shape[1:])
    return jnp.zeros_like(blocks).at[places].set(blocks).reshape(turned.shape)


def shifted(value, axis, steps):
    count = lax.axis_size(axis)
    leading, last = (max(0, -steps), min(count, count - steps))
    return lax.ppermute(value, axis, [(source, source + steps) for source in range(leading, last)])


def per_device(inputs, w_qkv, w_out, w_gate_up, w_down, gain_attn, gain_mlp, doc_start, cotangent):
    n_dp, n_seq = lax.axis_size("dp"), lax.axis_size("seq")
    rows, group, width = inputs.shape
    tokens = rows * group
    slab = width // (n_dp * n_seq)
    places = [block_places(n_dp, n_seq, flavour) for flavour in range(2)]
    ordered = slab % 16 == 0
    if not ordered:
        slab = 32
    blocks = width // slab
    listed = places if ordered else [[np.arange(blocks)] * 2] * 2
    table = facts_table(n_dp, n_seq, group, listed)
    device = lax.axis_index("dp") * n_seq + lax.axis_index("seq")
    facts = lax.dynamic_index_in_dim(jnp.asarray(table), device, axis=0, keepdims=False)
    put = [places_fact(n_dp, n_seq, flavour, blocks) for flavour in range(2)]
    core = lax.axis_index("dp") & 1

    def in_order(turned, flavour):
        if ordered:
            return turned
        return place_rows(turned, jnp.where(core == 0, *places[flavour]))

    x = inputs.reshape(tokens, width)
    dy = cotangent.reshape(tokens, width)

    tails = [(row + 1) * group for row in range(rows)]
    qkv, one_turned, x_tail = norm_matmul(x, gain_attn, w_qkv, 0, facts, put[0], slab, tails)
    x_rim = shifted(x_tail, "seq", 1)
    dy_turned = turn(dy, facts, put[1], slab, after=[qkv])
    kv_rim, rim_turned, _ = norm_matmul(
        x_rim, gain_attn, w_qkv, width, facts, put[0], slab, [WINDOW], after=[dy_turned]
    )
    att, att_turned = attend(qkv, kv_rim, doc_start, facts, put[0], slab)
    resid, normed_two, two_turned = out_proj(att, w_out, x, gain_mlp, facts, put[1], slab)
    one_turned, rim_turned, att_turned = [in_order(turned, 0) for turned in (one_turned, rim_turned, att_turned)]
    two_turned, dy_turned = [in_order(turned, 1) for turned in (two_turned, dy_turned)]

    def feed(first, count, total=None, end=None, after=()):
        hidden, dgu, *rest = feed_forward(
            normed_two, dy, dy_turned, two_turned, w_gate_up, w_down, first, count, total, end, after
        )
        chunk = Chunk(1)
        chunk.between_cores(*rest[:3])
        return hidden, dgu, chunk, rest[3:]

    def keep_ff(chunk, hidden, dgu, after=()):
        send, keep = ff_grad(facts, chunk.bit(), dy_turned, two_turned, hidden, dgu, chunk.got, after=after)
        chunk.go(send, keep)
        return send

    count = FF_CHUNKS[0]
    hidden_one, dgu_one, one, (total,) = feed(0, count)
    token = keep_ff(one, hidden_one, dgu_one)
    hidden_two, dgu_two, two, (drb, da) = feed(count, FF_CHUNKS[1], total, (resid, gain_mlp, w_out), after=[token])
    token = advance(facts, one, after=[da])
    token = keep_ff(two, hidden_two, dgu_two, after=[token])
    dqkv, drim = attend_back(qkv, kv_rim, doc_start, facts, da, after=[token])
    att = Chunk(0)
    grads = (facts, att_turned, one_turned, rim_turned, drb, dqkv, drim)
    sends = att_grad(*grads, after=[one.got])
    att.between_cores(*sends)
    token = advance(facts, one, two, after=sends)
    send, keep = att_grad(*grads, att.bit(), att.got, after=[token])
    att.go(send[None], keep[None])
    token = advance(facts, one, two, after=[send])
    back = rim_grad(drim, w_qkv, x_rim, gain_attn, after=[token])
    back_got = shifted(back, "seq", -1)
    outputs = ff_out([hidden_one, hidden_two], w_down, resid, after=[back])
    token = advance(facts, att, two, after=[outputs, one.got])
    while not (one.last and two.last):
        token = advance(facts, *(chunk for chunk in (one, two) if not chunk.last), after=[token])
    grad_inputs = input_grad(dqkv, w_qkv, x, gain_attn, drb, back_got, rows, group, after=[token])
    token = advance(facts, att, after=[grad_inputs])
    gather_ff = Gather(facts, finish(one, two, after=[token]))
    token = gather_ff.value
    while not att.last:
        token = advance(facts, att, after=[token])
    token = gather_ff.step(after=[token])
    gather = Gather(facts, finish(att, after=[token]))
    if ordered and n_dp == 8:
        token = gather_ff.step(after=[gather.value])
        token = gather.step(us=24, after=[token])
        total_gate_up, turned_down, gain_two = put_ff(gather_ff, w_gate_up, gain_mlp, after=[token])
        total_down = turned_down.T
        gather.step(after=[total_gate_up])
        total_qkv, total_out, gain_one = put_att(gather, w_qkv, gain_attn)
        gain_one, gain_two = gain_one[0], gain_two[0]
    else:
        for both in (gather_ff, gather):
            while not both.last:
                both.step()
        total_ff = gather_ff.whole()
        rest = gather.whole()[0]
        total_down, total_gate, total_up = [total_ff[kind, :, :FF] for kind in range(3)]
        total_down = total_down.astype(F32)
        total_gate_up = jnp.concatenate([total_gate, total_up], axis=1).astype(F32)
        total_out = rest[:, :width].astype(F32)
        total_qkv = rest[:, width:].astype(F32)
        kept = total_qkv.shape[0]
        first_row = lax.axis_index("seq") * kept

        def gain_total(total, weight, gain):
            mine = lax.dynamic_slice_in_dim(weight, first_row, kept, axis=0).astype(F32)
            return jnp.sum(total * mine, axis=1) / lax.dynamic_slice_in_dim(gain, first_row, kept)

        gain_one = gain_total(total_qkv, w_qkv, gain_attn)
        gain_two = gain_total(total_gate_up, w_gate_up, gain_mlp)

    return (
        outputs.reshape(rows, group, width),
        grad_inputs.reshape(rows, group, width),
        total_qkv,
        total_out,
        total_gate_up,
        total_down,
        gain_one,
        gain_two,
    )


def solution(mesh):
    in_specs = (
        P("dp", "seq", None),
        P(),
        P(),
        P(),
        P(),
        P(),
        P(),
        P("dp", "seq"),
        P("dp", "seq", None),
    )
    out_specs = (
        P("dp", "seq", None),
        P("dp", "seq", None),
        P("seq", None),
        P("seq", None),
        P("seq", None),
        P("seq", None),
        P("seq"),
        P("seq"),
    )
    return jax.shard_map(
        per_device, mesh=mesh, in_specs=in_specs, out_specs=out_specs, check_vma=False
    )
```

```python
import functools
import math

import jax
import jax.numpy as jnp
import numpy as np
from jax import lax
from jax.experimental import pallas as pl
from jax.experimental.pallas import tpu as pltpu
from jax.sharding import PartitionSpec as P

HEADS = 16
HEAD_DIM = 64
FF = 2752
WINDOW = 64
LANES = 128
PAIRS = 2
FF_TILE = 256
FF_TILES = -(-FF // FF_TILE)
FF_CHUNKS = (6, 5)
STEP = 256
epsilon = 1e-05
masked_value = -1e30
F32 = jnp.float32
BF16 = jnp.bfloat16
VMEM_LIMIT = 64 * 1024 * 1024 - 256 * 1024
PER_US = 1.1e9


def dot(left, right, left_dim=1, right_dim=0):
    return lax.dot_general(
        left, right, (((left_dim,), (right_dim,)), ((), ())), preferred_element_type=F32
    )


def launch(kernel, name, grid, scalars, inputs, outputs, scratch=(), us=8, after=()):
    known = len(scalars) + len(inputs)

    def body(*refs):
        kernel(*refs[:known], *refs[known + len(after) :])

    specs = [spec for _, spec in inputs] + [pl.BlockSpec(memory_space=pl.ANY)] * len(after)
    shapes = [pltpu.HBM(shape, kind) for shape, kind, _ in outputs]
    moved = sum(array.size * array.dtype.itemsize for array, _ in inputs)
    moved += sum(math.prod(shape) * np.dtype(kind).itemsize for shape, kind, _ in outputs)
    return pl.pallas_call(
        body,
        grid_spec=pltpu.PrefetchScalarGridSpec(
            num_scalar_prefetch=len(scalars),
            grid=grid,
            in_specs=specs,
            out_specs=[spec for _, _, spec in outputs],
            scratch_shapes=list(scratch),
        ),
        out_shape=shapes,
        compiler_params=pltpu.CompilerParams(vmem_limit_bytes=VMEM_LIMIT),
        cost_estimate=pl.CostEstimate(flops=int(us * PER_US), bytes_accessed=int(moved / 100), transcendentals=0),
        name=name,
    )(*scalars, *[array for array, _ in inputs], *after)


def full(*shape):
    return pl.BlockSpec(shape, lambda *_: (0,) * len(shape))


CORE_INDEX, SEQ_INDEX, POSITION = range(3)


def store_slabs(out_ref, value, facts_ref, first, slab, columns=slice(None)):
    for k in range(value.shape[0] // slab):
        row = pl.multiple_of(facts_ref[first + k] * slab, slab)
        out_ref[pl.ds(row, slab), columns] = value[k * slab : (k + 1) * slab]


def side_by_side(ref):
    return jnp.concatenate([ref[k] for k in range(ref.shape[0])], axis=1)


def put_blocks(ref, value, rows=slice(None)):
    for k in range(ref.shape[0]):
        ref[k, rows, :] = value[:, k * LANES : (k + 1) * LANES]

def two_heads(value, low):
    zero = jnp.zeros_like(value)
    return jnp.concatenate([jnp.where(low, value, zero), jnp.where(low, zero, value)], axis=0)


def one_of_two(value, size):
    feature = lax.broadcasted_iota(jnp.int32, (LANES, size), 0)
    return jnp.where(feature < HEAD_DIM, value[:, :size], value[:, size:])


class Spans:
    def __init__(self, rows, group):
        self.rows, self.group = rows, group
        self.size = min(128, group)
        self.blocks = group // self.size
        self.count = rows * self.blocks
        self.window = self.size + WINDOW

    def queries(self, at):
        return slice(at * self.size, (at + 1) * self.size)

    def keys(self, own_ref, rim_ref, pair, at):
        row, block = divmod(at, self.blocks)
        start = at * self.size
        if block == 0:
            rim = rim_ref[pair, row * WINDOW : (row + 1) * WINDOW, :]
            return jnp.concatenate([rim, own_ref[pair, start : start + self.size, :]], axis=0)
        return own_ref[pair, start - WINDOW : start + self.size, :]

    def fill_bias(self, bias_ref, starts_ref, facts_ref):
        size = self.size
        key = lax.broadcasted_iota(jnp.int32, (self.window, size), 0) - WINDOW
        query = lax.broadcasted_iota(jnp.int32, (self.window, size), 1)
        near = (key <= query) & (query - key <= WINDOW)
        for at in range(self.count):
            row, block = divmod(at, self.blocks)
            begin = starts_ref[row : row + 1, block * size : (block + 1) * size]
            begin = begin - facts_ref[POSITION] - block * size
            bias = jnp.where(near & (key >= begin), 0.0, masked_value).astype(F32)
            bias_ref[at, :, :size] = bias
            bias_ref[at, :, size:] = bias

    def scratch(self, kind):
        return pltpu.VMEM((self.count, self.window, 2 * self.size), kind)


def softmax(scores):
    weights = jnp.exp(scores - jnp.max(scores, axis=0, keepdims=True))
    return weights * (1.0 / jnp.sum(weights, axis=0, keepdims=True))


def attend_kernel(facts_ref, starts_ref, q_ref, k_ref, v_ref, kr_ref, vr_ref,
                  att_ref, attT_ref, bias_ref, score_ref, probs_ref, *, spans, slab, put, pairs):
    step = pl.program_id(0)
    size, count = spans.size, spans.count

    @pl.when(step == 0)
    def _():
        spans.fill_bias(bias_ref, starts_ref, facts_ref)

    low = lax.broadcasted_iota(jnp.int32, (size, LANES), 1) < HEAD_DIM
    for pair in range(pairs):
        for at in range(count):
            queries = q_ref[pair, spans.queries(at), :] * jnp.asarray(HEAD_DIM ** (-0.5), BF16)
            keys = spans.keys(k_ref, kr_ref, pair, at)
            score_ref[at] = dot(keys, two_heads(queries, low), 1, 1)
        for at in range(count):
            probs_ref[at] = softmax(score_ref[at] + bias_ref[at]).astype(BF16)
        for at in range(count):
            values = spans.keys(v_ref, vr_ref, pair, at)
            mixed = one_of_two(dot(values, probs_ref[at], 0, 0), size)
            att_ref[pair, spans.queries(at), :] = mixed.T.astype(BF16)
            first = put + (step * pairs + pair) * (LANES // slab)
            store_slabs(attT_ref, mixed.astype(BF16), facts_ref, first, slab, spans.queries(at))


def attend(qkv, kv_rim, doc_start, facts, put, slab, after=()):
    rows, group = doc_start.shape
    all_pairs, tokens = qkv.shape[0] // 3, qkv.shape[1]
    rim = kv_rim.shape[1]
    spans = Spans(rows, group)
    steps = all_pairs // PAIRS
    own = lambda kind: pl.BlockSpec((PAIRS, tokens, LANES), lambda j, *_: (kind * steps + j, 0, 0))
    edge = lambda kind: pl.BlockSpec((PAIRS, rim, LANES), lambda j, *_: (kind * steps + j, 0, 0))
    width = all_pairs * LANES
    return launch(
        functools.partial(attend_kernel, spans=spans, slab=slab, put=put, pairs=PAIRS),
        "attend",
        (steps,),
        [facts],
        [
            (doc_start, full(rows, group)),
            (qkv, own(0)),
            (qkv, own(1)),
            (qkv, own(2)),
            (kv_rim, edge(0)),
            (kv_rim, edge(1)),
        ],
        [
            ((all_pairs, tokens, LANES), BF16, own(0)),
            ((width, tokens), BF16, full(width, tokens)),
        ],
        [spans.scratch(F32), spans.scratch(F32), spans.scratch(BF16)],
        us=8,
        after=after,
    )


def attend_back_kernel(facts_ref, starts_ref, q_ref, k_ref, v_ref, kr_ref, vr_ref, da_ref,
                       dqkv_ref, drim_ref,
                       bias_ref, score_ref, grad_ref, probs_ref, dscore_ref, *, spans, pairs):
    size, count = spans.size, spans.count

    @pl.when(pl.program_id(0) == 0)
    def _():
        spans.fill_bias(bias_ref, starts_ref, facts_ref)

    low = lax.broadcasted_iota(jnp.int32, (size, LANES), 1) < HEAD_DIM
    scale = HEAD_DIM ** (-0.5)

    def scaled_queries(pair, at):
        return two_heads(q_ref[pair, spans.queries(at), :] * jnp.asarray(scale, BF16), low)

    for pair in range(pairs):
        for at in range(count):
            score_ref[at] = dot(spans.keys(k_ref, kr_ref, pair, at), scaled_queries(pair, at), 1, 1)
            grads = two_heads(da_ref[pair, spans.queries(at), :], low)
            grad_ref[at] = dot(spans.keys(v_ref, vr_ref, pair, at), grads, 1, 1)
        for at in range(count):
            probs = softmax(score_ref[at] + bias_ref[at])
            probs_ref[at] = probs.astype(BF16)
            part = probs * grad_ref[at]
            dscore_ref[at] = (part - probs * jnp.sum(part, axis=0, keepdims=True)).astype(BF16)
        late = [None, None]
        for at in range(count):
            here = spans.queries(at)
            row, block = divmod(at, spans.blocks)
            dscores = dscore_ref[at]
            grads = two_heads(da_ref[pair, here, :], low)
            dk = dot(dscores, scaled_queries(pair, at))
            dv = dot(probs_ref[at], grads)
            dq = one_of_two(dot(spans.keys(k_ref, kr_ref, pair, at), dscores, 0, 0), size) * scale
            dqkv_ref[0, pair, here, :] = dq.T.astype(BF16)
            start = at * size
            for kind, grad in ((0, dk), (1, dv)):
                out_ref, rim_ref = dqkv_ref.at[kind + 1], drim_ref.at[kind]
                early = grad[:WINDOW]
                if block == 0:
                    rim_ref[pair, row * WINDOW : (row + 1) * WINDOW, :] = early.astype(BF16)
                else:
                    out_ref[pair, start - WINDOW : start, :] = (late[kind] + early).astype(BF16)
                if size > WINDOW:
                    out_ref[pair, start : start + size - WINDOW, :] = grad[WINDOW:size].astype(BF16)
                late[kind] = grad[size:]
                if block == spans.blocks - 1:
                    out_ref[pair, start + size - WINDOW : start + size, :] = late[kind].astype(BF16)


def attend_back(qkv, kv_rim, doc_start, facts, grad_att, after=()):
    rows, group = doc_start.shape
    all_pairs, tokens = qkv.shape[0] // 3, qkv.shape[1]
    rim = kv_rim.shape[1]
    spans = Spans(rows, group)
    steps = all_pairs // PAIRS
    own = lambda kind: pl.BlockSpec((PAIRS, tokens, LANES), lambda j, *_: (kind * steps + j, 0, 0))
    edge = lambda kind: pl.BlockSpec((PAIRS, rim, LANES), lambda j, *_: (kind * steps + j, 0, 0))
    return launch(
        functools.partial(attend_back_kernel, spans=spans, pairs=PAIRS),
        "attend_back",
        (steps,),
        [facts],
        [
            (doc_start, full(rows, group)),
            (qkv, own(0)),
            (qkv, own(1)),
            (qkv, own(2)),
            (kv_rim, edge(0)),
            (kv_rim, edge(1)),
            (grad_att, own(0)),
        ],
        [
            ((3, all_pairs, tokens, LANES), BF16, pl.BlockSpec((3, PAIRS, tokens, LANES), lambda j, *_: (0, j, 0, 0))),
            ((2, all_pairs, rim, LANES), BF16, pl.BlockSpec((2, PAIRS, rim, LANES), lambda j, *_: (0, j, 0, 0))),
        ],
        [spans.scratch(kind) for kind in (F32, F32, F32, BF16, BF16)],
        us=8,
        after=after,
    )


def norm_matmul_kernel(facts_ref, x_ref, gain_ref, w_ref, *refs, slab, put, step, beside):
    if beside:
        other_ref, out_ref, normedT_ref, otherT_ref, normed_ref = refs
    else:
        out_ref, normedT_ref, normed_ref = refs

    @pl.when(pl.program_id(0) == 0)
    def _():
        for at in range(0, x_ref.shape[0], step):
            x = x_ref[at : at + step, :].astype(F32)
            inv = lax.rsqrt(jnp.mean(x * x, axis=-1, keepdims=True) + epsilon)
            normed = (x * inv * gain_ref[...]).astype(BF16)
            normed_ref[at : at + step, :] = normed
            store_slabs(normedT_ref, normed.T, facts_ref, put, slab, slice(at, at + step))

    put_blocks(out_ref, dot(normed_ref[...], w_ref[...]).astype(BF16))
    if beside:
        store_slabs(otherT_ref, other_ref[...].T, facts_ref, put, slab)


def norm_matmul(x, gain, weight, first_column, facts, put, slab, beside=None, after=()):
    tokens, width = x.shape
    columns = weight.shape[1] - first_column
    tile = 1024 if beside is None else 768
    skip, wide, steps = first_column // tile, tile // LANES, columns // tile
    part = tokens // steps
    others, turned = [], []
    if beside is not None:
        others = [(beside, pl.BlockSpec((part, width), lambda j, *_: (j, 0)))]
        turned = [((width, tokens), BF16, pl.BlockSpec((width, part), lambda j, *_: (0, j)))]
    return launch(
        functools.partial(norm_matmul_kernel, slab=slab, put=put, step=min(STEP, tokens), beside=beside is not None),
        "norm_matmul",
        (steps,),
        [facts],
        [
            (x, full(tokens, width)),
            (gain[None], full(1, width)),
            (weight, pl.BlockSpec((width, tile), lambda j, *_: (0, skip + j))),
        ]
        + others,
        [
            ((columns // LANES, tokens, LANES), BF16, pl.BlockSpec((wide, tokens, LANES), lambda j, *_: (j, 0, 0))),
            ((width, tokens), BF16, full(width, tokens)),
        ]
        + turned,
        [pltpu.VMEM((tokens, width), BF16)],
        us=8,
        after=after,
    )


def out_proj_kernel(facts_ref, att_ref, w_ref, x_ref, gain_ref, resid_ref, normed_ref, normedT_ref, *, slab, put):
    resid = x_ref[...].astype(F32) + dot(side_by_side(att_ref), w_ref[...])
    resid_ref[...] = resid.astype(BF16)
    inv = lax.rsqrt(jnp.mean(resid * resid, axis=-1, keepdims=True) + epsilon)
    normed = (resid * inv * gain_ref[...]).astype(BF16)
    normed_ref[...] = normed
    store_slabs(normedT_ref, normed.T, facts_ref, put, slab)


def out_proj(att, w_out, x, gain, facts, put, slab, after=()):
    tokens, width = x.shape
    pairs = att.shape[0]
    step = 2 * STEP
    rows = pl.BlockSpec((step, width), lambda m, *_: (m, 0))
    return launch(
        functools.partial(out_proj_kernel, slab=slab, put=put),
        "out_proj",
        (tokens // step,),
        [facts],
        [
            (att, pl.BlockSpec((pairs, step, LANES), lambda m, *_: (0, m, 0))),
            (w_out, full(width, width)),
            (x, rows),
            (gain[None], full(1, width)),
        ],
        [
            ((tokens, width), BF16, rows),
            ((tokens, width), BF16, rows),
            ((width, tokens), BF16, pl.BlockSpec((width, step), lambda m, *_: (0, m))),
        ],
        us=8,
        after=after,
    )


def ff_kernel(*refs, first, given, ends):
    normed_ref, dy_ref, dyT_ref, normedT_ref, wg_ref, wu0_ref, wu1_ref, wu2_ref, wd_ref = refs[:9]
    rest = list(refs[9:])
    total_in = rest.pop(0) if given else None
    if ends:
        resid_ref, gain_ref, w_out_ref = rest[:3]
        rest = rest[3:]
    hidden_ref, dgu_ref, send_down, send_gate, send_up, *totals, acc_ref = rest
    tile = pl.program_id(0)
    tokens = normed_ref.shape[0]

    @pl.when(tile == 0)
    def _():
        acc_ref[...] = total_in[...] if given else jnp.zeros_like(acc_ref)

    half = FF % LANES
    w_both = jnp.concatenate([wg_ref[...], wu0_ref[:, half:], wu1_ref[...], wu2_ref[:, :half]], axis=1)
    limit = FF - (tile + first) * FF_TILE
    inside = lax.broadcasted_iota(jnp.int32, (STEP, FF_TILE), 1) < limit

    def products(at):
        here = slice(at, at + STEP)
        both = dot(normed_ref[here, :], w_both)
        return both[:, :FF_TILE], both[:, FF_TILE:], dot(dy_ref[here, :], wd_ref[...], 1, 1)

    def act(at, gate, up, back):
        here = slice(at, at + STEP)
        sigma = 1.0 / (1.0 + jnp.exp(-gate))
        silu = gate * sigma
        hidden_ref[here, :] = jnp.where(inside, silu * up, 0.0).astype(BF16)
        dgate = back * up * (sigma * (1.0 + gate * (1.0 - sigma)))
        dgu_ref[0, here, :] = jnp.where(inside, dgate, 0.0).astype(BF16)
        dgu_ref[1, here, :] = jnp.where(inside, back * silu, 0.0).astype(BF16)

    def norm_grad(at):
        here = slice(at, at + STEP)
        grads = jnp.concatenate([dgu_ref[0, here, :], dgu_ref[1, here, :]], axis=1)
        acc_ref[here, :] += dot(grads, w_both, 1, 1)

    held = products(0)
    for at in range(0, tokens, STEP):
        ahead = products(at + STEP) if at + STEP < tokens else None
        act(at, *held)
        norm_grad(at)
        held = ahead
    send_down[...] = dot(dyT_ref[...], hidden_ref[...]).astype(BF16)
    both = dot(normedT_ref[...], jnp.concatenate([dgu_ref[0], dgu_ref[1]], axis=1)).astype(BF16)
    send_gate[...] = both[:, :FF_TILE]
    send_up[...] = both[:, FF_TILE:]

    @pl.when(tile == pl.num_programs(0) - 1)
    def _():
        if not ends:
            totals[0][...] = acc_ref[...]
            return
        drb_ref, da_ref = totals
        for at in range(0, tokens, STEP):
            here = slice(at, at + STEP)
            grad = norm_back(acc_ref[here, :], resid_ref[here, :].astype(F32), gain_ref[...])
            branch = (dy_ref[here, :].astype(F32) + grad).astype(BF16)
            put_blocks(drb_ref, branch, here)
            put_blocks(da_ref, dot(branch, w_out_ref[...], 1, 1).astype(BF16), here)


def feed_forward(normed, dy, dy_turned, normed_turned, w_gate_up, w_down, first, count, total=None, end=None, after=()):
    tokens, width = normed.shape
    wide = count * FF_TILE
    last = w_gate_up.shape[1] // LANES - 1
    skip = FF // LANES + first * (FF_TILE // LANES)
    up = lambda k: pl.BlockSpec(
        (width, LANES), lambda j: (0, jnp.minimum(skip + k + j * (FF_TILE // LANES), last))
    )
    other_half = full(width // 2, tokens)
    given = [] if total is None else [(total, full(tokens, width))]
    ending, results = [], [((tokens, width), F32, full(tokens, width))]
    if end is not None:
        resid, gain, w_out = end
        ending = [(resid, full(tokens, width)), (gain[None], full(1, width)), (w_out, full(width, width))]
        blocks = (width // LANES, tokens, LANES)
        results = [(blocks, BF16, full(*blocks))] * 2
    return launch(
        functools.partial(ff_kernel, first=first, given=len(given), ends=end is not None),
        "feed_forward",
        (count,),
        [],
        [
            (normed, full(tokens, width)),
            (dy, full(tokens, width)),
            (dy_turned, other_half),
            (normed_turned, other_half),
            (w_gate_up, pl.BlockSpec((width, FF_TILE), lambda j: (0, first + j))),
            (w_gate_up, up(0)),
            (w_gate_up, up(1)),
            (w_gate_up, up(2)),
            (w_down.T, pl.BlockSpec((FF_TILE, width), lambda j: (first + j, 0))),
        ]
        + given
        + ending,
        [
            ((tokens, wide), BF16, pl.BlockSpec((tokens, FF_TILE), lambda j: (0, j))),
            ((2, tokens, wide), BF16, pl.BlockSpec((2, tokens, FF_TILE), lambda j: (0, 0, j))),
        ]
        + [((width // 2, wide), BF16, pl.BlockSpec((width // 2, FF_TILE), lambda j: (0, j)))] * 3
        + results,
        [pltpu.VMEM((tokens, width), F32)],
        us=8,
        after=after,
    )


def ff_grad_kernel(facts_ref, dyT_ref, normedT_ref, hidden_ref, dgu_ref, got_down, got_gate, got_up, send_ref, keep_ref, *, bit):
    part = send_ref.shape[1]
    own = facts_ref[bit]
    rights = (hidden_ref[...], dgu_ref[0], dgu_ref[1])
    lefts, gots = (dyT_ref, normedT_ref, normedT_ref), (got_down, got_gate, got_up)
    for kind, (left_ref, right, got_ref) in enumerate(zip(lefts, rights, gots)):
        for out_ref, index in ((send_ref, 1 - own), (keep_ref, own)):
            rows = pl.ds(pl.multiple_of(index * part, part), part)
            total = dot(left_ref[rows, :], right) + got_ref[rows, :].astype(F32)
            out_ref[kind] = total.astype(BF16)


def ff_grad(facts, bit, dy_turned, normed_turned, hidden, dgu, got, after=()):
    width, tokens = dy_turned.shape
    wide = hidden.shape[1]
    tile = 512 if wide % 512 == 0 else FF_TILE
    own_half = pl.BlockSpec((width // 2, tokens), lambda j, *_: (1, 0))
    part = ((3, width // 4, wide), BF16, pl.BlockSpec((3, width // 4, tile), lambda j, *_: (0, 0, j)))
    return launch(
        functools.partial(ff_grad_kernel, bit=bit),
        "ff_grad",
        (wide // tile,),
        [facts],
        [
            (dy_turned, own_half),
            (normed_turned, own_half),
            (hidden, pl.BlockSpec((tokens, tile), lambda j, *_: (0, j))),
            (dgu, pl.BlockSpec((2, tokens, tile), lambda j, *_: (0, 0, j))),
        ]
        + [(part, pl.BlockSpec((width // 2, tile), lambda j, *_: (0, j))) for part in got],
        [part, part],
        us=8,
        after=after,
    )


def norm_back(grad, values, gain):
    inv = lax.rsqrt(jnp.mean(values * values, axis=-1, keepdims=True) + epsilon)
    scaled = grad * gain
    return inv * scaled - values * (inv * inv * inv) * jnp.mean(scaled * values, axis=-1, keepdims=True)


def ff_out_kernel(*refs):
    wd_ref, resid_ref, out_ref = refs[-3:]
    total, first = resid_ref[...].astype(F32), 0
    for hidden_ref in refs[:-3]:
        count = min(hidden_ref.shape[1], FF - first)
        total += dot(hidden_ref[:, :count], wd_ref[first : first + count, :])
        first += count
    out_ref[...] = total.astype(BF16)


def ff_out(hiddens, w_down, resid, us, after=()):
    tokens, width = resid.shape
    rows = lambda columns: pl.BlockSpec((STEP, columns), lambda m: (m, 0))
    return launch(
        ff_out_kernel,
        "ff_out",
        (tokens // STEP,),
        [],
        [(hidden, rows(hidden.shape[1])) for hidden in hiddens]
        + [(w_down.T, full(FF, width)), (resid, rows(width))],
        [((tokens, width), BF16, rows(width))],
        us=us,
        after=after,
    )[0]


def att_grad_kernel(facts_ref, *refs, bit):
    split = bit is not None
    attT_ref, oneT_ref, rimT_ref, drb_ref, dqkv_ref, drim_ref = refs[:6]
    kind = pl.program_id(0)

    def put(total):
        if split:
            got_ref, send_ref, keep_ref = refs[-3:]
            part = send_ref.shape[0]
            own = facts_ref[bit]
            for out_ref, half in ((send_ref, 1 - own), (keep_ref, own)):
                rows = pl.ds(pl.multiple_of(half * part, part), part)
                out_ref[...] = (total(rows) + got_ref[rows, :].astype(F32)).astype(BF16)
        else:
            refs[-1][...] = total(slice(None)).astype(BF16)

    @pl.when(kind == 0)
    def _():
        right = side_by_side(drb_ref)
        put(lambda rows: dot(attT_ref[rows, :], right))

    @pl.when(kind == 1)
    def _():
        right = side_by_side(dqkv_ref)
        put(lambda rows: dot(oneT_ref[rows, :], right))

    @pl.when(kind > 1)
    def _():
        right, rim = side_by_side(dqkv_ref), side_by_side(drim_ref)
        put(lambda rows: dot(oneT_ref[rows, :], right) + dot(rimT_ref[rows, :], rim))


def att_grad(facts, att_turned, one_turned, rim_turned, drb, dqkv, drim, bit=None, got=None, us=8, after=()):
    width, tokens = one_turned.shape
    rim = rim_turned.shape[1]
    split = got is not None
    half = 1 if split else 0
    inputs = [
        (turned, pl.BlockSpec((width // 2, turned.shape[1]), lambda j, *_: (half, 0)))
        for turned in (att_turned, one_turned, rim_turned)
    ]
    blocks = width // LANES
    inputs += [
        (drb, full(blocks, tokens, LANES)),
        (dqkv, pl.BlockSpec((None, blocks, tokens, LANES), lambda j, *_: (jnp.maximum(j - 1, 0), 0, 0, 0))),
        (drim, pl.BlockSpec((None, blocks, rim, LANES), lambda j, *_: (jnp.maximum(j - 2, 0), 0, 0, 0))),
    ]
    columns = 4 * width
    tile = pl.BlockSpec((width // 2, width), lambda j, *_: (0, j))
    if split:
        inputs.append((got, tile))
        part = ((width // 4, columns), BF16, pl.BlockSpec((width // 4, width), lambda j, *_: (0, j)))
        outputs = [part, part]
    else:
        outputs = [((width // 2, columns), BF16, tile)]
    return launch(
        functools.partial(att_grad_kernel, bit=bit),
        "att_grad",
        (4,),
        [facts],
        inputs,
        outputs,
        us=us,
        after=after,
    )


def input_grad_kernel(dqkv_ref, w_ref, x_ref, gain_ref, drb_ref, back_ref, out_ref, *, tails):
    step = out_ref.shape[0]
    grads = jnp.concatenate([side_by_side(dqkv_ref.at[kind]) for kind in range(3)], axis=1)
    grad = norm_back(dot(grads, w_ref[...], 1, 1), x_ref[...].astype(F32), gain_ref[...])
    out_ref[...] = grad + side_by_side(drb_ref).astype(F32)
    for row, end in enumerate(tails):
        block, last = divmod(end - WINDOW, step)

        @pl.when(pl.program_id(0) == block)
        def _():
            out_ref[last : last + WINDOW, :] += back_ref[row * WINDOW : (row + 1) * WINDOW, :].astype(F32)


def input_grad(dqkv, w_qkv, x, gain, drb, back, tails, us, after=()):
    tokens, width = x.shape
    blocks = width // LANES
    rows = pl.BlockSpec((STEP, width), lambda m: (m, 0))
    return launch(
        functools.partial(input_grad_kernel, tails=tails),
        "input_grad",
        (tokens // STEP,),
        [],
        [
            (dqkv, pl.BlockSpec((3, blocks, STEP, LANES), lambda m: (0, 0, m, 0))),
            (w_qkv, full(*w_qkv.shape)),
            (x, rows),
            (gain[None], full(1, width)),
            (drb, pl.BlockSpec((blocks, STEP, LANES), lambda m: (0, m, 0))),
            (back, full(*back.shape)),
        ],
        [((tokens, width), F32, rows)],
        us=us,
        after=after,
    )[0]


def rim_grad_kernel(drim_ref, wk_ref, wv_ref, x_ref, gain_ref, out_ref):
    grad = dot(side_by_side(drim_ref.at[0]), wk_ref[...], 1, 1)
    grad += dot(side_by_side(drim_ref.at[1]), wv_ref[...], 1, 1)
    out_ref[...] = norm_back(grad, x_ref[...].astype(F32), gain_ref[...]).astype(BF16)


def rim_grad(drim, w_qkv, x, gain, after=()):
    rim, width = x.shape
    part = lambda k: pl.BlockSpec((width, width), lambda j: (0, k))
    return launch(
        rim_grad_kernel,
        "rim_grad",
        (1,),
        [],
        [
            (drim, full(*drim.shape)),
            (w_qkv, part(1)),
            (w_qkv, part(2)),
            (x, full(rim, width)),
            (gain[None], full(1, width)),
        ],
        [((rim, width), BF16, full(rim, width))],
        us=8,
        after=after,
    )[0]


def add_kernel(facts_ref, *refs, bits):
    count = len(bits)
    for k, bit in enumerate(bits):
        keep_ref, got_ref = refs[2 * k : 2 * k + 2]
        outs = refs[2 * count + 2 * k : 2 * count + 2 * k + 2]
        for out_ref, index in zip(outs, (1 - facts_ref[bit], facts_ref[bit])):
            out_ref[...] = (keep_ref[:, index].astype(F32) + got_ref[:, index].astype(F32)).astype(BF16)


def add_and_cut(facts, items, us, after=()):
    inputs, outputs = [], []
    for keep, got, _ in items:
        kinds, rows, columns = keep.shape
        cut = lambda value: value.reshape(kinds, 2, rows // 2, columns)
        spec = pl.BlockSpec((kinds, 2, rows // 2, columns // 2), lambda j, *_: (0, 0, 0, j))
        inputs += [(cut(keep), spec), (cut(got), spec)]
        part = pl.BlockSpec((kinds, rows // 2, columns // 2), lambda j, *_: (0, 0, j))
        outputs += [((kinds, rows // 2, columns), BF16, part)] * 2
    kernel = functools.partial(add_kernel, bits=[bit for _, _, bit in items])
    parts = launch(kernel, "add_and_cut", (2,), [facts], inputs, outputs, us=us, after=after)
    return [(parts[2 * k], parts[2 * k + 1]) for k in range(len(items))]


def merge_kernel(facts_ref, *refs, bit):
    *parts, send_ref, keep_ref = refs
    for out_ref, index in ((send_ref, 1 - facts_ref[bit]), (keep_ref, facts_ref[bit])):
        first = 0
        for keep, got in zip(parts[::2], parts[1::2]):
            columns = keep.shape[3]
            total = keep[:, index].astype(F32) + got[:, index].astype(F32)
            out_ref[:, :, first : first + columns] = total.astype(BF16)
            first += columns


def merge_and_cut(facts, pieces, bit, us, after=()):
    inputs = []
    for keep, got in pieces:
        kinds, rows, columns = keep.shape
        spec = pl.BlockSpec((1, 2, rows // 2, columns), lambda j, *_: (j, 0, 0, 0))
        inputs += [(value.reshape(kinds, 2, rows // 2, columns), spec) for value in (keep, got)]
    columns = sum(keep.shape[2] for keep, _ in pieces)
    part = ((kinds, rows // 2, columns), BF16, pl.BlockSpec((1, rows // 2, columns), lambda j, *_: (j, 0, 0)))
    kernel = functools.partial(merge_kernel, bit=bit)
    return launch(kernel, "merge_and_cut", (kinds,), [facts], inputs, [part, part], us=us, after=after)


def log2(count):
    return count.bit_length() - 1


def stage_orders(n_dp, n_seq, flavour):
    dp = [("dp", bit) for bit in range(1, log2(n_dp))]
    if flavour:
        dp = dp[::-1]
    seq = [("seq", bit) for bit in range(log2(n_seq))]
    return dp + seq, seq[:1] + dp + seq[1:]


def row_bits(n_dp, n_seq):
    return [("seq", bit) for bit in reversed(range(log2(n_seq)))] + [
        ("dp", bit) for bit in reversed(range(log2(n_dp)))
    ]


def block_places(n_dp, n_seq, flavour):
    bits, orders = row_bits(n_dp, n_seq), stage_orders(n_dp, n_seq, flavour)
    count = n_dp * n_seq
    tables = []
    for core in range(2):
        table = []
        for block in range(count):
            value = {step: (block >> (len(bits) - 1 - k)) & 1 for k, step in enumerate(bits)}
            owner = value[("dp", 0)]
            place = 0
            for step in orders[owner]:
                place = place * 2 + value[step]
            table.append(place + (count // 2 if owner == core else 0))
        tables.append(np.array(table, np.int32))
    return tables


def swap_pairs(n_dp, n_seq, steps):
    pairs = []
    for d in range(n_dp):
        for s in range(n_seq):
            axis, bit = steps[d % 2]
            there = (d ^ (1 << bit), s) if axis == "dp" else (d, s ^ (1 << bit))
            pairs.append((d * n_seq + s, there[0] * n_seq + there[1]))
    return pairs


def swap(value, steps):
    n_dp, n_seq = lax.axis_size("dp"), lax.axis_size("seq")
    return lax.ppermute(value, ("dp", "seq"), swap_pairs(n_dp, n_seq, steps))


def gather_steps(n_dp):
    dims = [("dp", bit) for bit in range(1, log2(n_dp))]
    return list(zip(dims[::-1], dims))


def stage_fact(n_dp, n_seq, flavour, stage):
    return 3 + flavour * (log2(n_dp * n_seq) - 1) + stage


def gather_fact(n_dp, n_seq, step):
    return 3 + 2 * (log2(n_dp * n_seq) - 1) + step


def places_fact(n_dp, n_seq, flavour, count):
    return gather_fact(n_dp, n_seq, log2(n_dp)) + flavour * count


def facts_table(n_dp, n_seq, group, places):
    table = []
    for d in range(n_dp):
        for s in range(n_seq):
            core = d & 1
            bit = lambda steps: ((d if steps[core][0] == "dp" else s) >> steps[core][1]) & 1
            row = [core, s, s * group]
            for flavour in range(2):
                row += [bit(steps) for steps in zip(*stage_orders(n_dp, n_seq, flavour))]
            row += [bit(steps) for steps in gather_steps(n_dp)] + [0]
            assert len(row) == places_fact(n_dp, n_seq, 0, 0)
            for flavour in range(2):
                row += list(places[flavour][core])
            table.append(row)
    return np.array(table, np.int32)


CORE = (("dp", 0), ("dp", 0))


class Chunk:
    def __init__(self, flavour):
        self.sizes = lax.axis_size("dp"), lax.axis_size("seq")
        self.flavour = flavour
        self.stages = list(zip(*stage_orders(*self.sizes, flavour)))
        self.done = 0

    def bit(self):
        return stage_fact(*self.sizes, self.flavour, self.done)

    def between_cores(self, *parts):
        self.got = [swap(part, CORE) for part in parts]

    def go(self, send, keep):
        self.keep = keep
        self.got = swap(send, self.stages[self.done])
        self.done += 1

    @property
    def last(self):
        return self.done == len(self.stages)


def advance(facts, *chunks, us=8, after=()):
    parts = add_and_cut(facts, [(chunk.keep, chunk.got, chunk.bit()) for chunk in chunks], us, after)
    for chunk, (send, keep) in zip(chunks, parts):
        chunk.go(send, keep)
    return parts[0][0]


def merge(facts, *chunks, us, after=()):
    whole = Chunk(chunks[0].flavour)
    whole.done = chunks[0].done
    pieces = [(chunk.keep, chunk.got) for chunk in chunks]
    whole.go(*merge_and_cut(facts, pieces, whole.bit(), us, after))
    return whole


def finish_kernel(*refs):
    out_ref, first = refs[-1], 0
    for keep_ref, got_ref in zip(refs[:-1:2], refs[1:-1:2]):
        columns = keep_ref.shape[2]
        total = keep_ref[...].astype(F32) + got_ref[...].astype(F32)
        out_ref[:, :, first : first + columns] = total.astype(BF16)
        first += columns


def finish(*chunks, us=8, after=()):
    kinds, part, _ = chunks[0].keep.shape
    inputs = [(array, full(*array.shape)) for chunk in chunks for array in (chunk.keep, chunk.got)]
    shape = (kinds, part, sum(chunk.keep.shape[2] for chunk in chunks))
    return launch(finish_kernel, "finish", (1,), [], inputs, [(shape, BF16, full(*shape))], us=us, after=after)[0]


def join_kernel(facts_ref, value_ref, got_ref, out_ref, *, bit):
    count = value_ref.shape[1]
    first = facts_ref[bit] * count
    out_ref[:, pl.ds(first, count)] = value_ref[...]
    out_ref[:, pl.ds(count - first, count)] = got_ref[...]


class Gather:
    def __init__(self, facts, value):
        self.facts = facts
        n_dp = lax.axis_size("dp")
        self.dims = [("dp", bit) for bit in range(1, log2(n_dp))]
        self.steps = gather_steps(n_dp)
        self.kinds, self.part, self.columns = value.shape
        self.value = value[:, None]
        self.done = 0
        self.send()

    @property
    def last(self):
        return self.done == len(self.steps)

    def send(self):
        self.got = swap(self.value, CORE if self.last else self.steps[self.done])

    def step(self, us=8, after=()):
        bit = gather_fact(lax.axis_size("dp"), lax.axis_size("seq"), self.done)
        kinds, count, part, columns = self.value.shape
        tile = columns // 2
        spec = lambda count: pl.BlockSpec((kinds, count, part, tile), lambda j, *_: (0, 0, 0, j))
        (self.value,) = launch(
            functools.partial(join_kernel, bit=bit),
            "join",
            (2,),
            [self.facts],
            [(self.value, spec(count)), (self.got, spec(count))],
            [((kinds, 2 * count, part, columns), BF16, spec(2 * count))],
            us=us,
            after=after,
        )
        self.done += 1
        self.send()
        return self.value

    def whole(self):
        dims = self.dims
        core = lax.axis_index("dp") & 1
        halves = []
        for which, order in enumerate((dims[::-1], dims)):
            half = jnp.where(core == which, self.value, self.got)
            half = half.reshape((self.kinds,) + (2,) * len(dims) + (self.part, self.columns))
            wanted = [1 + order[::-1].index(step) for step in dims[::-1]]
            halves.append(half.transpose([0] + wanted + [len(dims) + 1, len(dims) + 2]))
        whole = jnp.stack(halves, axis=len(dims) + 1)
        return whole.reshape(self.kinds, lax.axis_size("dp") * self.part, self.columns)


def natural_rows(facts_ref, own_ref, got_ref, kind, step, columns):
    pieces = []
    for x in range(2):
        for which in range(2):
            index = x * 2 + step if which == 0 else step * 2 + x
            own, got = own_ref[kind, index, :, columns], got_ref[kind, index, :, columns]
            pieces.append(jnp.where(facts_ref[CORE_INDEX] == which, own, got))
    return jnp.concatenate(pieces, axis=0).astype(F32)


def row_sums(value):
    total = jnp.sum(value, axis=1, keepdims=True)
    return jnp.broadcast_to(total, (total.shape[0], LANES)).T[:1, :]


def put_ff_kernel(facts_ref, own_ref, got_ref, w_ref, gain_ref, gate_up_ref, down_ref, dgain_ref):
    step = pl.program_id(0)
    rows = lambda kind: natural_rows(facts_ref, own_ref, got_ref, kind, step, slice(0, FF))
    down_ref[...] = rows(0).T
    gate, up = rows(1), rows(2)
    gate_up_ref[:, :FF] = gate
    gate_up_ref[:, FF:] = up
    weight = w_ref[...].astype(F32)
    total = row_sums(gate * weight[:, :FF]) + row_sums(up * weight[:, FF:])
    dgain_ref[...] = total / gain_ref[...]


def put_ff(gather, w_gate_up, gain, after=()):
    kept = 8 * gather.part
    half = kept // 2
    whole = full(*gather.value.shape)
    return launch(
        put_ff_kernel,
        "put_ff",
        (2,),
        [gather.facts],
        [
            (gather.value, whole),
            (gather.got, whole),
            (w_gate_up, pl.BlockSpec((half, 2 * FF), lambda j, facts: (2 * facts[SEQ_INDEX] + j, 0))),
            (gain[None], pl.BlockSpec((1, half), lambda j, facts: (0, 2 * facts[SEQ_INDEX] + j))),
        ],
        [
            ((kept, 2 * FF), F32, pl.BlockSpec((half, 2 * FF), lambda j, *_: (j, 0))),
            ((FF, kept), F32, pl.BlockSpec((FF, half), lambda j, *_: (0, j))),
            ((1, kept), F32, pl.BlockSpec((1, half), lambda j, *_: (0, j))),
        ],
        us=8,
        after=after,
    )


def put_att_kernel(facts_ref, own_ref, got_ref, w_ref, gain_ref, qkv_ref, out_ref, dgain_ref):
    step = pl.program_id(0)
    width = out_ref.shape[1]
    out_ref[...] = natural_rows(facts_ref, own_ref, got_ref, 0, step, slice(0, width))
    qkv = natural_rows(facts_ref, own_ref, got_ref, 0, step, slice(width, 4 * width))
    qkv_ref[...] = qkv
    dgain_ref[...] = row_sums(qkv * w_ref[...].astype(F32)) / gain_ref[...]


def put_att(gather, w_qkv, gain, after=()):
    kept = 8 * gather.part
    half, width = kept // 2, gather.columns // 4
    whole = full(*gather.value.shape)
    return launch(
        put_att_kernel,
        "put_att",
        (2,),
        [gather.facts],
        [
            (gather.value, whole),
            (gather.got, whole),
            (w_qkv, pl.BlockSpec((half, 3 * width), lambda j, facts: (2 * facts[SEQ_INDEX] + j, 0))),
            (gain[None], pl.BlockSpec((1, half), lambda j, facts: (0, 2 * facts[SEQ_INDEX] + j))),
        ],
        [
            ((kept, 3 * width), F32, pl.BlockSpec((half, 3 * width), lambda j, *_: (j, 0))),
            ((kept, width), F32, pl.BlockSpec((half, width), lambda j, *_: (j, 0))),
            ((1, kept), F32, pl.BlockSpec((1, half), lambda j, *_: (0, j))),
        ],
        us=8,
        after=after,
    )


def place_rows(turned, places):
    count = places.shape[0]
    blocks = turned.reshape((count, turned.shape[0] // count) + turned.shape[1:])
    return jnp.zeros_like(blocks).at[places].set(blocks).reshape(turned.shape)


def shifted(value, axis, steps):
    count = lax.axis_size(axis)
    leading, last = (max(0, -steps), min(count, count - steps))
    return lax.ppermute(value, axis, [(source, source + steps) for source in range(leading, last)])


def per_device(inputs, w_qkv, w_out, w_gate_up, w_down, gain_attn, gain_mlp, doc_start, cotangent):
    n_dp, n_seq = lax.axis_size("dp"), lax.axis_size("seq")
    rows, group, width = inputs.shape
    tokens = rows * group
    slab = width // (n_dp * n_seq)
    places = [block_places(n_dp, n_seq, flavour) for flavour in range(2)]
    ordered = slab % 16 == 0
    if not ordered:
        slab = 32
    blocks = width // slab
    listed = places if ordered else [[np.arange(blocks)] * 2] * 2
    table = facts_table(n_dp, n_seq, group, listed)
    device = lax.axis_index("dp") * n_seq + lax.axis_index("seq")
    facts = lax.dynamic_index_in_dim(jnp.asarray(table), device, axis=0, keepdims=False)
    put = [places_fact(n_dp, n_seq, flavour, blocks) for flavour in range(2)]
    core = lax.axis_index("dp") & 1

    def in_order(turned, flavour):
        if ordered:
            return turned
        return place_rows(turned, jnp.where(core == 0, *places[flavour]))

    x = inputs.reshape(tokens, width)
    dy = cotangent.reshape(tokens, width)

    tails = [(row + 1) * group for row in range(rows)]
    x_rim = shifted(inputs[:, group - WINDOW :], "seq", 1).reshape(rows * WINDOW, width)
    qkv, one_turned, dy_turned = norm_matmul(x, gain_attn, w_qkv, 0, facts, put[1], slab, dy)
    kv_rim, rim_turned = norm_matmul(x_rim, gain_attn, w_qkv, width, facts, put[1], slab, after=[qkv])
    att, att_turned = attend(qkv, kv_rim, doc_start, facts, put[1], slab)
    resid, normed_two, two_turned = out_proj(att, w_out, x, gain_mlp, facts, put[1], slab)
    one_turned, rim_turned, att_turned = [in_order(turned, 1) for turned in (one_turned, rim_turned, att_turned)]
    two_turned, dy_turned = [in_order(turned, 1) for turned in (two_turned, dy_turned)]

    def feed(first, count, total=None, end=None, after=()):
        hidden, dgu, *rest = feed_forward(
            normed_two, dy, dy_turned, two_turned, w_gate_up, w_down, first, count, total, end, after
        )
        chunk = Chunk(1)
        chunk.between_cores(*rest[:3])
        return hidden, dgu, chunk, rest[3:]

    def keep_ff(chunk, hidden, dgu, after=()):
        send, keep = ff_grad(facts, chunk.bit(), dy_turned, two_turned, hidden, dgu, chunk.got, after=after)
        chunk.go(send, keep)
        return send

    count = FF_CHUNKS[0]
    hidden_one, dgu_one, one, (total,) = feed(0, count)
    token = keep_ff(one, hidden_one, dgu_one)
    hidden_two, dgu_two, two, (drb, da) = feed(count, FF_CHUNKS[1], total, (resid, gain_mlp, w_out), after=[token])
    token = advance(facts, one, after=[da])
    token = keep_ff(two, hidden_two, dgu_two, after=[token])
    dqkv, drim = attend_back(qkv, kv_rim, doc_start, facts, da, after=[token])
    att = Chunk(1)
    grads = (facts, att_turned, one_turned, rim_turned, drb, dqkv, drim)
    (send,) = att_grad(*grads, after=[one.got])
    att.between_cores(send)
    token = advance(facts, one, two, us=30, after=[send])
    back = rim_grad(drim, w_qkv, x_rim, gain_attn, after=[token])
    back_got = shifted(back, "seq", -1)
    send, keep = att_grad(*grads, att.bit(), att.got[0], after=[back])
    att.go(send[None], keep[None])
    token = advance(facts, one, two, after=[send, back_got])
    grad_inputs = input_grad(dqkv, w_qkv, x, gain_attn, drb, back_got, tails, us=15, after=[token])
    token = advance(facts, att, two, after=[grad_inputs, one.got])
    while not (one.last and two.last):
        token = advance(facts, *(chunk for chunk in (one, two) if not chunk.last), after=[token])
    outputs = ff_out([hidden_one, hidden_two], w_down, resid, us=8, after=[token])
    token = advance(facts, att, after=[outputs])
    gather_ff = Gather(facts, finish(one, two, after=[token]))
    token = gather_ff.value
    while not att.last:
        token = advance(facts, att, after=[token])
    token = gather_ff.step(after=[token])
    gather = Gather(facts, finish(att, after=[token]))
    if ordered and n_dp == 8:
        token = gather.step(us=1, after=[gather.value])
        token = gather_ff.step(after=[token])
        token = gather.step(us=24, after=[token])
        total_gate_up, turned_down, gain_two = put_ff(gather_ff, w_gate_up, gain_mlp, after=[token])
        total_down = turned_down.T
        total_qkv, total_out, gain_one = put_att(gather, w_qkv, gain_attn, after=[total_gate_up])
        gain_one, gain_two = gain_one[0], gain_two[0]
    else:
        for both in (gather_ff, gather):
            while not both.last:
                both.step()
        total_ff = gather_ff.whole()
        rest = gather.whole()[0]
        total_down, total_gate, total_up = [total_ff[kind, :, :FF] for kind in range(3)]
        total_down = total_down.astype(F32)
        total_gate_up = jnp.concatenate([total_gate, total_up], axis=1).astype(F32)
        total_out = rest[:, :width].astype(F32)
        total_qkv = rest[:, width:].astype(F32)
        kept = total_qkv.shape[0]
        first_row = lax.axis_index("seq") * kept

        def gain_total(total, weight, gain):
            mine = lax.dynamic_slice_in_dim(weight, first_row, kept, axis=0).astype(F32)
            return jnp.sum(total * mine, axis=1) / lax.dynamic_slice_in_dim(gain, first_row, kept)

        gain_one = gain_total(total_qkv, w_qkv, gain_attn)
        gain_two = gain_total(total_gate_up, w_gate_up, gain_mlp)

    return (
        outputs.reshape(rows, group, width),
        grad_inputs.reshape(rows, group, width),
        total_qkv,
        total_out,
        total_gate_up,
        total_down,
        gain_one,
        gain_two,
    )


def solution(mesh):
    in_specs = (
        P("dp", "seq", None),
        P(),
        P(),
        P(),
        P(),
        P(),
        P(),
        P("dp", "seq"),
        P("dp", "seq", None),
    )
    out_specs = (
        P("dp", "seq", None),
        P("dp", "seq", None),
        P("seq", None),
        P("seq", None),
        P("seq", None),
        P("seq", None),
        P("seq"),
        P("seq"),
    )
    return jax.shard_map(
        per_device, mesh=mesh, in_specs=in_specs, out_specs=out_specs, check_vma=False
    )
```

```python
import functools
import math

import jax
import jax.numpy as jnp
import numpy as np
from jax import lax
from jax.experimental import pallas as pl
from jax.experimental.pallas import tpu as pltpu
from jax.sharding import PartitionSpec as P

HEADS = 16
HEAD_DIM = 64
FF = 2752
WINDOW = 64
LANES = 128
PAIRS = 2
FF_TILE = 256
FF_TILES = -(-FF // FF_TILE)
FF_CHUNKS = (7, 4)
FF_WIDE = FF_TILES * FF_TILE
STEP = 256
epsilon = 1e-05
masked_value = -1e30
F32 = jnp.float32
BF16 = jnp.bfloat16
VMEM_LIMIT = 64 * 1024 * 1024 - 256 * 1024
PER_US = 1.1e9


def dot(left, right, left_dim=1, right_dim=0):
    return lax.dot_general(
        left, right, (((left_dim,), (right_dim,)), ((), ())), preferred_element_type=F32
    )


def launch(kernel, name, grid, scalars, inputs, outputs, scratch=(), us=8, after=()):
    known = len(scalars) + len(inputs)

    def body(*refs):
        kernel(*refs[:known], *refs[known + len(after) :])

    specs = [spec for _, spec in inputs] + [pl.BlockSpec(memory_space=pl.ANY)] * len(after)
    shapes = [pltpu.HBM(shape, kind) for shape, kind, _ in outputs]
    moved = sum(array.size * array.dtype.itemsize for array, _ in inputs)
    moved += sum(math.prod(shape) * np.dtype(kind).itemsize for shape, kind, _ in outputs)
    return pl.pallas_call(
        body,
        grid_spec=pltpu.PrefetchScalarGridSpec(
            num_scalar_prefetch=len(scalars),
            grid=grid,
            in_specs=specs,
            out_specs=[spec for _, _, spec in outputs],
            scratch_shapes=list(scratch),
        ),
        out_shape=shapes,
        compiler_params=pltpu.CompilerParams(vmem_limit_bytes=VMEM_LIMIT),
        cost_estimate=pl.CostEstimate(flops=int(us * PER_US), bytes_accessed=int(moved / 100), transcendentals=0),
        name=name,
    )(*scalars, *[array for array, _ in inputs], *after)


def full(*shape):
    return pl.BlockSpec(shape, lambda *_: (0,) * len(shape))


CORE_INDEX, SEQ_INDEX, POSITION = range(3)


def store_slabs(out_ref, value, facts_ref, first, slab, columns=slice(None)):
    for k in range(value.shape[0] // slab):
        row = pl.multiple_of(facts_ref[first + k] * slab, slab)
        out_ref[pl.ds(row, slab), columns] = value[k * slab : (k + 1) * slab]


def side_by_side(ref):
    return jnp.concatenate([ref[k] for k in range(ref.shape[0])], axis=1)


def put_blocks(ref, value, rows=slice(None)):
    for k in range(ref.shape[0]):
        ref[k, rows, :] = value[:, k * LANES : (k + 1) * LANES]

def two_heads(value, low):
    zero = jnp.zeros_like(value)
    return jnp.concatenate([jnp.where(low, value, zero), jnp.where(low, zero, value)], axis=0)


def one_of_two(value, size):
    feature = lax.broadcasted_iota(jnp.int32, (LANES, size), 0)
    return jnp.where(feature < HEAD_DIM, value[:, :size], value[:, size:])


class Spans:
    def __init__(self, rows, group):
        self.rows, self.group = rows, group
        self.size = min(128, group)
        self.blocks = group // self.size
        self.count = rows * self.blocks
        self.window = self.size + WINDOW

    def queries(self, at):
        return slice(at * self.size, (at + 1) * self.size)

    def keys(self, own_ref, rim_ref, pair, at):
        row, block = divmod(at, self.blocks)
        start = at * self.size
        if block == 0:
            rim = rim_ref[pair, row * WINDOW : (row + 1) * WINDOW, :]
            return jnp.concatenate([rim, own_ref[pair, start : start + self.size, :]], axis=0)
        return own_ref[pair, start - WINDOW : start + self.size, :]

    def fill_bias(self, bias_ref, starts_ref, facts_ref):
        size = self.size
        key = lax.broadcasted_iota(jnp.int32, (self.window, size), 0) - WINDOW
        query = lax.broadcasted_iota(jnp.int32, (self.window, size), 1)
        near = (key <= query) & (query - key <= WINDOW)
        for at in range(self.count):
            row, block = divmod(at, self.blocks)
            begin = starts_ref[row : row + 1, block * size : (block + 1) * size]
            begin = begin - facts_ref[POSITION] - block * size
            bias = jnp.where(near & (key >= begin), 0.0, masked_value).astype(F32)
            bias_ref[at, :, :size] = bias
            bias_ref[at, :, size:] = bias

    def scratch(self, kind):
        return pltpu.VMEM((self.count, self.window, 2 * self.size), kind)


def softmax(scores):
    weights = jnp.exp(scores - jnp.max(scores, axis=0, keepdims=True))
    return weights * (1.0 / jnp.sum(weights, axis=0, keepdims=True))


def attend_kernel(facts_ref, starts_ref, q_ref, k_ref, v_ref, kr_ref, vr_ref,
                  att_ref, attT_ref, bias_ref, score_ref, probs_ref, *, spans, slab, put, pairs):
    step = pl.program_id(0)
    size, count = spans.size, spans.count

    @pl.when(step == 0)
    def _():
        spans.fill_bias(bias_ref, starts_ref, facts_ref)

    low = lax.broadcasted_iota(jnp.int32, (size, LANES), 1) < HEAD_DIM
    for pair in range(pairs):
        for at in range(count):
            queries = q_ref[pair, spans.queries(at), :] * jnp.asarray(HEAD_DIM ** (-0.5), BF16)
            keys = spans.keys(k_ref, kr_ref, pair, at)
            score_ref[at] = dot(keys, two_heads(queries, low), 1, 1)
        for at in range(count):
            probs_ref[at] = softmax(score_ref[at] + bias_ref[at]).astype(BF16)
        for at in range(count):
            values = spans.keys(v_ref, vr_ref, pair, at)
            mixed = one_of_two(dot(values, probs_ref[at], 0, 0), size)
            att_ref[pair, spans.queries(at), :] = mixed.T.astype(BF16)
            first = put + (step * pairs + pair) * (LANES // slab)
            store_slabs(attT_ref, mixed.astype(BF16), facts_ref, first, slab, spans.queries(at))


def attend(qkv, kv_rim, doc_start, facts, put, slab, after=()):
    rows, group = doc_start.shape
    all_pairs, tokens = qkv.shape[0] // 3, qkv.shape[1]
    rim = kv_rim.shape[1]
    spans = Spans(rows, group)
    steps = all_pairs // PAIRS
    own = lambda kind: pl.BlockSpec((PAIRS, tokens, LANES), lambda j, *_: (kind * steps + j, 0, 0))
    edge = lambda kind: pl.BlockSpec((PAIRS, rim, LANES), lambda j, *_: (kind * steps + j, 0, 0))
    width = all_pairs * LANES
    return launch(
        functools.partial(attend_kernel, spans=spans, slab=slab, put=put, pairs=PAIRS),
        "attend",
        (steps,),
        [facts],
        [
            (doc_start, full(rows, group)),
            (qkv, own(0)),
            (qkv, own(1)),
            (qkv, own(2)),
            (kv_rim, edge(0)),
            (kv_rim, edge(1)),
        ],
        [
            ((all_pairs, tokens, LANES), BF16, own(0)),
            ((width, tokens), BF16, full(width, tokens)),
        ],
        [spans.scratch(F32), spans.scratch(F32), spans.scratch(BF16)],
        us=8,
        after=after,
    )


def attend_back_kernel(facts_ref, starts_ref, q_ref, k_ref, v_ref, kr_ref, vr_ref, da_ref,
                       dqkv_ref, drim_ref,
                       bias_ref, score_ref, grad_ref, probs_ref, dscore_ref, *, spans, pairs):
    size, count = spans.size, spans.count

    @pl.when(pl.program_id(0) == 0)
    def _():
        spans.fill_bias(bias_ref, starts_ref, facts_ref)

    low = lax.broadcasted_iota(jnp.int32, (size, LANES), 1) < HEAD_DIM
    scale = HEAD_DIM ** (-0.5)

    def scaled_queries(pair, at):
        return two_heads(q_ref[pair, spans.queries(at), :] * jnp.asarray(scale, BF16), low)

    for pair in range(pairs):
        for at in range(count):
            score_ref[at] = dot(spans.keys(k_ref, kr_ref, pair, at), scaled_queries(pair, at), 1, 1)
            grads = two_heads(da_ref[pair, spans.queries(at), :], low)
            grad_ref[at] = dot(spans.keys(v_ref, vr_ref, pair, at), grads, 1, 1)
        for at in range(count):
            probs = softmax(score_ref[at] + bias_ref[at])
            probs_ref[at] = probs.astype(BF16)
            part = probs * grad_ref[at]
            dscore_ref[at] = (part - probs * jnp.sum(part, axis=0, keepdims=True)).astype(BF16)
        late = [None, None]
        for at in range(count):
            here = spans.queries(at)
            row, block = divmod(at, spans.blocks)
            dscores = dscore_ref[at]
            grads = two_heads(da_ref[pair, here, :], low)
            dk = dot(dscores, scaled_queries(pair, at))
            dv = dot(probs_ref[at], grads)
            dq = one_of_two(dot(spans.keys(k_ref, kr_ref, pair, at), dscores, 0, 0), size) * scale
            dqkv_ref[0, pair, here, :] = dq.T.astype(BF16)
            start = at * size
            for kind, grad in ((0, dk), (1, dv)):
                out_ref, rim_ref = dqkv_ref.at[kind + 1], drim_ref.at[kind]
                early = grad[:WINDOW]
                if block == 0:
                    rim_ref[pair, row * WINDOW : (row + 1) * WINDOW, :] = early.astype(BF16)
                else:
                    out_ref[pair, start - WINDOW : start, :] = (late[kind] + early).astype(BF16)
                if size > WINDOW:
                    out_ref[pair, start : start + size - WINDOW, :] = grad[WINDOW:size].astype(BF16)
                late[kind] = grad[size:]
                if block == spans.blocks - 1:
                    out_ref[pair, start + size - WINDOW : start + size, :] = late[kind].astype(BF16)


def attend_back(qkv, kv_rim, doc_start, facts, grad_att, after=()):
    rows, group = doc_start.shape
    all_pairs, tokens = qkv.shape[0] // 3, qkv.shape[1]
    rim = kv_rim.shape[1]
    spans = Spans(rows, group)
    steps = all_pairs // PAIRS
    own = lambda kind: pl.BlockSpec((PAIRS, tokens, LANES), lambda j, *_: (kind * steps + j, 0, 0))
    edge = lambda kind: pl.BlockSpec((PAIRS, rim, LANES), lambda j, *_: (kind * steps + j, 0, 0))
    return launch(
        functools.partial(attend_back_kernel, spans=spans, pairs=PAIRS),
        "attend_back",
        (steps,),
        [facts],
        [
            (doc_start, full(rows, group)),
            (qkv, own(0)),
            (qkv, own(1)),
            (qkv, own(2)),
            (kv_rim, edge(0)),
            (kv_rim, edge(1)),
            (grad_att, own(0)),
        ],
        [
            ((3, all_pairs, tokens, LANES), BF16, pl.BlockSpec((3, PAIRS, tokens, LANES), lambda j, *_: (0, j, 0, 0))),
            ((2, all_pairs, rim, LANES), BF16, pl.BlockSpec((2, PAIRS, rim, LANES), lambda j, *_: (0, j, 0, 0))),
        ],
        [spans.scratch(kind) for kind in (F32, F32, F32, BF16, BF16)],
        us=8,
        after=after,
    )


def norm_matmul_kernel(facts_ref, x_ref, gain_ref, w_ref, *refs, slab, put, step, beside):
    if beside:
        other_ref, out_ref, normedT_ref, otherT_ref, normed_ref = refs
    else:
        out_ref, normedT_ref, normed_ref = refs

    @pl.when(pl.program_id(0) == 0)
    def _():
        for at in range(0, x_ref.shape[0], step):
            x = x_ref[at : at + step, :].astype(F32)
            inv = lax.rsqrt(jnp.mean(x * x, axis=-1, keepdims=True) + epsilon)
            normed = (x * inv * gain_ref[...]).astype(BF16)
            normed_ref[at : at + step, :] = normed
            store_slabs(normedT_ref, normed.T, facts_ref, put, slab, slice(at, at + step))

    put_blocks(out_ref, dot(normed_ref[...], w_ref[...]).astype(BF16))
    if beside:
        store_slabs(otherT_ref, other_ref[...].T, facts_ref, put, slab)


def norm_matmul(x, gain, weight, first_column, facts, put, slab, beside=None, after=()):
    tokens, width = x.shape
    columns = weight.shape[1] - first_column
    tile = 1024 if beside is None else 768
    skip, wide, steps = first_column // tile, tile // LANES, columns // tile
    part = tokens // steps
    others, turned = [], []
    if beside is not None:
        others = [(beside, pl.BlockSpec((part, width), lambda j, *_: (j, 0)))]
        turned = [((width, tokens), BF16, pl.BlockSpec((width, part), lambda j, *_: (0, j)))]
    return launch(
        functools.partial(norm_matmul_kernel, slab=slab, put=put, step=min(STEP, tokens), beside=beside is not None),
        "norm_matmul",
        (steps,),
        [facts],
        [
            (x, full(tokens, width)),
            (gain[None], full(1, width)),
            (weight, pl.BlockSpec((width, tile), lambda j, *_: (0, skip + j))),
        ]
        + others,
        [
            ((columns // LANES, tokens, LANES), BF16, pl.BlockSpec((wide, tokens, LANES), lambda j, *_: (j, 0, 0))),
            ((width, tokens), BF16, full(width, tokens)),
        ]
        + turned,
        [pltpu.VMEM((tokens, width), BF16)],
        us=8,
        after=after,
    )


def out_proj_kernel(facts_ref, att_ref, w_ref, x_ref, gain_ref, resid_ref, normed_ref, normedT_ref, *, slab, put):
    resid = x_ref[...].astype(F32) + dot(side_by_side(att_ref), w_ref[...])
    resid_ref[...] = resid.astype(BF16)
    inv = lax.rsqrt(jnp.mean(resid * resid, axis=-1, keepdims=True) + epsilon)
    normed = (resid * inv * gain_ref[...]).astype(BF16)
    normed_ref[...] = normed
    store_slabs(normedT_ref, normed.T, facts_ref, put, slab)


def out_proj(att, w_out, x, gain, facts, put, slab, after=()):
    tokens, width = x.shape
    pairs = att.shape[0]
    step = 2 * STEP
    rows = pl.BlockSpec((step, width), lambda m, *_: (m, 0))
    return launch(
        functools.partial(out_proj_kernel, slab=slab, put=put),
        "out_proj",
        (tokens // step,),
        [facts],
        [
            (att, pl.BlockSpec((pairs, step, LANES), lambda m, *_: (0, m, 0))),
            (w_out, full(width, width)),
            (x, rows),
            (gain[None], full(1, width)),
        ],
        [
            ((tokens, width), BF16, rows),
            ((tokens, width), BF16, rows),
            ((width, tokens), BF16, pl.BlockSpec((width, step), lambda m, *_: (0, m))),
        ],
        us=8,
        after=after,
    )


def ff_kernel(*refs, first, given, ends):
    normed_ref, dy_ref, dyT_ref, normedT_ref, wg_ref, wu0_ref, wu1_ref, wu2_ref, wd_ref = refs[:9]
    rest = list(refs[9:])
    total_in = rest.pop(0) if given else None
    if ends:
        resid_ref, gain_ref, w_out_ref, attT_ref = rest[:4]
        rest = rest[4:]
    hidden_ref, dgu_ref, send_down, send_gate, send_up, *totals, acc_ref = rest
    tile = pl.program_id(0)
    tokens = normed_ref.shape[0]

    @pl.when(tile == 0)
    def _():
        acc_ref[...] = total_in[...] if given else jnp.zeros_like(acc_ref)

    half = FF % LANES
    w_both = jnp.concatenate([wg_ref[...], wu0_ref[:, half:], wu1_ref[...], wu2_ref[:, :half]], axis=1)
    limit = FF - (tile + first) * FF_TILE
    inside = lax.broadcasted_iota(jnp.int32, (STEP, FF_TILE), 1) < limit

    def products(at):
        here = slice(at, at + STEP)
        both = dot(normed_ref[here, :], w_both)
        return both[:, :FF_TILE], both[:, FF_TILE:], dot(dy_ref[here, :], wd_ref[...], 1, 1)

    def act(at, gate, up, back):
        here = slice(at, at + STEP)
        sigma = 1.0 / (1.0 + jnp.exp(-gate))
        silu = gate * sigma
        hidden_ref[here, :] = jnp.where(inside, silu * up, 0.0).astype(BF16)
        dgate = back * up * (sigma * (1.0 + gate * (1.0 - sigma)))
        dgu_ref[0, here, :] = jnp.where(inside, dgate, 0.0).astype(BF16)
        dgu_ref[1, here, :] = jnp.where(inside, back * silu, 0.0).astype(BF16)

    def norm_grad(at):
        here = slice(at, at + STEP)
        grads = jnp.concatenate([dgu_ref[0, here, :], dgu_ref[1, here, :]], axis=1)
        acc_ref[here, :] += dot(grads, w_both, 1, 1)

    held = products(0)
    for at in range(0, tokens, STEP):
        ahead = products(at + STEP) if at + STEP < tokens else None
        act(at, *held)
        norm_grad(at)
        held = ahead
    send_down[...] = dot(dyT_ref[...], hidden_ref[...]).astype(BF16)
    both = dot(normedT_ref[...], jnp.concatenate([dgu_ref[0], dgu_ref[1]], axis=1)).astype(BF16)
    send_gate[...] = both[:, :FF_TILE]
    send_up[...] = both[:, FF_TILE:]

    @pl.when(tile == pl.num_programs(0) - 1)
    def _():
        if not ends:
            totals[0][...] = acc_ref[...]
            return
        drb_ref, da_ref, send_out = totals
        for at in range(0, tokens, STEP):
            here = slice(at, at + STEP)
            grad = norm_back(acc_ref[here, :], resid_ref[here, :].astype(F32), gain_ref[...])
            branch = (dy_ref[here, :].astype(F32) + grad).astype(BF16)
            put_blocks(drb_ref, branch, here)
            put_blocks(da_ref, dot(branch, w_out_ref[...], 1, 1).astype(BF16), here)
        send_out[...] = dot(attT_ref[...], side_by_side(drb_ref)).astype(BF16)


def feed_forward(normed, dy, dy_turned, normed_turned, w_gate_up, w_down, first, count, total=None, end=None, after=()):
    tokens, width = normed.shape
    wide = count * FF_TILE
    last = w_gate_up.shape[1] // LANES - 1
    skip = FF // LANES + first * (FF_TILE // LANES)
    up = lambda k: pl.BlockSpec(
        (width, LANES), lambda j: (0, jnp.minimum(skip + k + j * (FF_TILE // LANES), last))
    )
    other_half = full(width // 2, tokens)
    given = [] if total is None else [(total, full(tokens, width))]
    ending, results = [], [((tokens, width), F32, full(tokens, width))]
    if end is not None:
        resid, gain, w_out, att_turned = end
        ending = [(resid, full(tokens, width)), (gain[None], full(1, width)), (w_out, full(width, width))]
        ending.append((att_turned, other_half))
        blocks = (width // LANES, tokens, LANES)
        results = [(blocks, BF16, full(*blocks))] * 2
        results.append(((width // 2, width), BF16, full(width // 2, width)))
    return launch(
        functools.partial(ff_kernel, first=first, given=len(given), ends=end is not None),
        "feed_forward",
        (count,),
        [],
        [
            (normed, full(tokens, width)),
            (dy, full(tokens, width)),
            (dy_turned, other_half),
            (normed_turned, other_half),
            (w_gate_up, pl.BlockSpec((width, FF_TILE), lambda j: (0, first + j))),
            (w_gate_up, up(0)),
            (w_gate_up, up(1)),
            (w_gate_up, up(2)),
            (w_down.T, pl.BlockSpec((FF_TILE, width), lambda j: (first + j, 0))),
        ]
        + given
        + ending,
        [
            ((tokens, wide), BF16, pl.BlockSpec((tokens, FF_TILE), lambda j: (0, j))),
            ((2, tokens, wide), BF16, pl.BlockSpec((2, tokens, FF_TILE), lambda j: (0, 0, j))),
        ]
        + [((width // 2, wide), BF16, pl.BlockSpec((width // 2, FF_TILE), lambda j: (0, j)))] * 3
        + results,
        [pltpu.VMEM((tokens, width), F32)],
        us=8,
        after=after,
    )


OUT_WIDE = 3 * LANES


def ff_grad_kernel(facts_ref, dyT_ref, normedT_ref, hidden_ref, dgu_ref, got_down, got_gate, got_up, *rest, bit, tiles):
    send_ref, keep_ref = rest[-2:]
    part = send_ref.shape[1]
    own = facts_ref[bit]
    step = pl.program_id(0)

    def put(kind, left_ref, right, got_ref, at, columns):
        for out_ref, index in ((send_ref, 1 - own), (keep_ref, own)):
            rows = pl.ds(pl.multiple_of(index * part, part), part)
            total = dot(left_ref[rows, :], right) + got_ref[rows, at : at + columns].astype(F32)
            out_ref[kind, :, :columns] = total.astype(BF16)

    @pl.when(step < tiles)
    def _():
        columns = hidden_ref.shape[1]
        put(0, dyT_ref, hidden_ref[...], got_down, 0, columns)
        put(1, normedT_ref, dgu_ref[0], got_gate, 0, columns)
        put(2, normedT_ref, dgu_ref[1], got_up, 0, columns)

    if len(rest) == 2:
        return
    attT_ref, drb_ref, got_out = rest[:3]
    for late in range(2):

        @pl.when(step == tiles + late)
        def _():
            send_ref[...] = jnp.zeros_like(send_ref)
            keep_ref[...] = jnp.zeros_like(keep_ref)
            for kind in range(3):
                blocks = range(kind * 3 + 2 * late, kind * 3 + 2 + late)
                blocks = [block for block in blocks if block < drb_ref.shape[0]]
                if blocks:
                    right = jnp.concatenate([drb_ref[block] for block in blocks], axis=1)
                    put(kind, attT_ref, right, got_out, blocks[0] * LANES, len(blocks) * LANES)


def ff_grad(facts, bit, dy_turned, normed_turned, hidden, dgu, got, out=(), after=()):
    width, tokens = dy_turned.shape
    wide = hidden.shape[1]
    tile = 512 if wide % 512 == 0 and not out else FF_TILE
    tiles = wide // tile
    own_half = pl.BlockSpec((width // 2, tokens), lambda j, *_: (1, 0))
    at = lambda j: jnp.minimum(j, tiles - 1)
    extra, columns, steps = [], wide, tiles
    if out:
        att_turned, drb = out
        extra = [(att_turned, own_half), (drb, full(*drb.shape)), (got[3], full(*got[3].shape))]
        columns, steps = wide + OUT_WIDE, tiles + 2
    part = ((3, width // 4, columns), BF16, pl.BlockSpec((3, width // 4, tile), lambda j, *_: (0, 0, j)))
    return launch(
        functools.partial(ff_grad_kernel, bit=bit, tiles=tiles),
        "ff_grad",
        (steps,),
        [facts],
        [
            (dy_turned, own_half),
            (normed_turned, own_half),
            (hidden, pl.BlockSpec((tokens, tile), lambda j, *_: (0, at(j)))),
            (dgu, pl.BlockSpec((2, tokens, tile), lambda j, *_: (0, 0, at(j)))),
        ]
        + [(value, pl.BlockSpec((width // 2, tile), lambda j, *_: (0, at(j)))) for value in got[:3]]
        + extra,
        [part, part],
        us=8,
        after=after,
    )


def norm_back(grad, values, gain):
    inv = lax.rsqrt(jnp.mean(values * values, axis=-1, keepdims=True) + epsilon)
    scaled = grad * gain
    return inv * scaled - values * (inv * inv * inv) * jnp.mean(scaled * values, axis=-1, keepdims=True)


def ff_out_kernel(*refs):
    wd_ref, resid_ref, out_ref = refs[-3:]
    total, first = resid_ref[...].astype(F32), 0
    for hidden_ref in refs[:-3]:
        count = min(hidden_ref.shape[1], FF - first)
        total += dot(hidden_ref[:, :count], wd_ref[first : first + count, :])
        first += count
    out_ref[...] = total.astype(BF16)


def ff_out(hiddens, w_down, resid, us, after=()):
    tokens, width = resid.shape
    rows = lambda columns: pl.BlockSpec((STEP, columns), lambda m: (m, 0))
    return launch(
        ff_out_kernel,
        "ff_out",
        (tokens // STEP,),
        [],
        [(hidden, rows(hidden.shape[1])) for hidden in hiddens]
        + [(w_down.T, full(FF, width)), (resid, rows(width))],
        [((tokens, width), BF16, rows(width))],
        us=us,
        after=after,
    )[0]


def att_grad_kernel(facts_ref, *refs, bit):
    split = bit is not None
    oneT_ref, rimT_ref, dqkv_ref, drim_ref = refs[:4]
    kind = pl.program_id(0)

    def put(total):
        if split:
            got_ref, send_ref, keep_ref = refs[-3:]
            part = send_ref.shape[0]
            own = facts_ref[bit]
            for out_ref, half in ((send_ref, 1 - own), (keep_ref, own)):
                rows = pl.ds(pl.multiple_of(half * part, part), part)
                out_ref[...] = (total(rows) + got_ref[rows, :].astype(F32)).astype(BF16)
        else:
            refs[-1][...] = total(slice(None)).astype(BF16)

    @pl.when(kind == 0)
    def _():
        right = side_by_side(dqkv_ref)
        put(lambda rows: dot(oneT_ref[rows, :], right))

    @pl.when(kind > 0)
    def _():
        right, rim = side_by_side(dqkv_ref), side_by_side(drim_ref)
        put(lambda rows: dot(oneT_ref[rows, :], right) + dot(rimT_ref[rows, :], rim))


def att_grad(facts, one_turned, rim_turned, dqkv, drim, bit=None, got=None, us=8, after=()):
    width, tokens = one_turned.shape
    rim = rim_turned.shape[1]
    split = got is not None
    half = 1 if split else 0
    inputs = [
        (turned, pl.BlockSpec((width // 2, turned.shape[1]), lambda j, *_: (half, 0)))
        for turned in (one_turned, rim_turned)
    ]
    blocks = width // LANES
    inputs += [
        (dqkv, pl.BlockSpec((None, blocks, tokens, LANES), lambda j, *_: (j, 0, 0, 0))),
        (drim, pl.BlockSpec((None, blocks, rim, LANES), lambda j, *_: (jnp.maximum(j - 1, 0), 0, 0, 0))),
    ]
    columns = 3 * width
    tile = pl.BlockSpec((width // 2, width), lambda j, *_: (0, j))
    if split:
        inputs.append((got, tile))
        part = ((width // 4, columns), BF16, pl.BlockSpec((width // 4, width), lambda j, *_: (0, j)))
        outputs = [part, part]
    else:
        outputs = [((width // 2, columns), BF16, tile)]
    return launch(
        functools.partial(att_grad_kernel, bit=bit),
        "att_grad",
        (3,),
        [facts],
        inputs,
        outputs,
        us=us,
        after=after,
    )


def input_grad_kernel(dqkv_ref, w_ref, x_ref, gain_ref, drb_ref, back_ref, out_ref, *, tails):
    step = out_ref.shape[0]
    grads = jnp.concatenate([side_by_side(dqkv_ref.at[kind]) for kind in range(3)], axis=1)
    grad = norm_back(dot(grads, w_ref[...], 1, 1), x_ref[...].astype(F32), gain_ref[...])
    out_ref[...] = grad + side_by_side(drb_ref).astype(F32)
    for row, end in enumerate(tails):
        block, last = divmod(end - WINDOW, step)

        @pl.when(pl.program_id(0) == block)
        def _():
            out_ref[last : last + WINDOW, :] += back_ref[row * WINDOW : (row + 1) * WINDOW, :].astype(F32)


def input_grad(dqkv, w_qkv, x, gain, drb, back, tails, us, after=()):
    tokens, width = x.shape
    blocks = width // LANES
    rows = pl.BlockSpec((STEP, width), lambda m: (m, 0))
    return launch(
        functools.partial(input_grad_kernel, tails=tails),
        "input_grad",
        (tokens // STEP,),
        [],
        [
            (dqkv, pl.BlockSpec((3, blocks, STEP, LANES), lambda m: (0, 0, m, 0))),
            (w_qkv, full(*w_qkv.shape)),
            (x, rows),
            (gain[None], full(1, width)),
            (drb, pl.BlockSpec((blocks, STEP, LANES), lambda m: (0, m, 0))),
            (back, full(*back.shape)),
        ],
        [((tokens, width), F32, rows)],
        us=us,
        after=after,
    )[0]


def rim_grad_kernel(drim_ref, wk_ref, wv_ref, x_ref, gain_ref, out_ref):
    grad = dot(side_by_side(drim_ref.at[0]), wk_ref[...], 1, 1)
    grad += dot(side_by_side(drim_ref.at[1]), wv_ref[...], 1, 1)
    out_ref[...] = norm_back(grad, x_ref[...].astype(F32), gain_ref[...]).astype(BF16)


def rim_grad(drim, w_qkv, x, gain, after=()):
    rim, width = x.shape
    part = lambda k: pl.BlockSpec((width, width), lambda j: (0, k))
    return launch(
        rim_grad_kernel,
        "rim_grad",
        (1,),
        [],
        [
            (drim, full(*drim.shape)),
            (w_qkv, part(1)),
            (w_qkv, part(2)),
            (x, full(rim, width)),
            (gain[None], full(1, width)),
        ],
        [((rim, width), BF16, full(rim, width))],
        us=8,
        after=after,
    )[0]


def half_of(columns):
    return -(-columns // (2 * LANES)) * LANES


def add_kernel(facts_ref, *refs, bits):
    count = len(bits)
    for k, bit in enumerate(bits):
        keep_ref, got_ref = refs[2 * k : 2 * k + 2]
        outs = refs[2 * count + 2 * k : 2 * count + 2 * k + 2]
        for out_ref, index in zip(outs, (1 - facts_ref[bit], facts_ref[bit])):
            out_ref[...] = (keep_ref[:, index].astype(F32) + got_ref[:, index].astype(F32)).astype(BF16)


def add_and_cut(facts, items, us, after=()):
    inputs, outputs = [], []
    for keep, got, _ in items:
        kinds, rows, columns = keep.shape
        cut = lambda value: value.reshape(kinds, 2, rows // 2, columns)
        spec = pl.BlockSpec((kinds, 2, rows // 2, half_of(columns)), lambda j, *_: (0, 0, 0, j))
        part = pl.BlockSpec((kinds, rows // 2, half_of(columns)), lambda j, *_: (0, 0, j))
        inputs += [(cut(keep), spec), (cut(got), spec)]
        outputs += [((kinds, rows // 2, columns), BF16, part)] * 2
    kernel = functools.partial(add_kernel, bits=[bit for _, _, bit in items])
    parts = launch(kernel, "add_and_cut", (2,), [facts], inputs, outputs, us=us, after=after)
    return [(parts[2 * k], parts[2 * k + 1]) for k in range(len(items))]


def merge_kernel(facts_ref, *refs, bit):
    *parts, send_ref, keep_ref = refs
    for out_ref, index in ((send_ref, 1 - facts_ref[bit]), (keep_ref, facts_ref[bit])):
        first = 0
        for keep, got in zip(parts[::2], parts[1::2]):
            columns = keep.shape[3]
            total = keep[:, index].astype(F32) + got[:, index].astype(F32)
            out_ref[:, :, first : first + columns] = total.astype(BF16)
            first += columns


def merge_and_cut(facts, pieces, bit, us, after=()):
    inputs = []
    for keep, got in pieces:
        kinds, rows, columns = keep.shape
        spec = pl.BlockSpec((1, 2, rows // 2, columns), lambda j, *_: (j, 0, 0, 0))
        inputs += [(value.reshape(kinds, 2, rows // 2, columns), spec) for value in (keep, got)]
    columns = sum(keep.shape[2] for keep, _ in pieces)
    part = ((kinds, rows // 2, columns), BF16, pl.BlockSpec((1, rows // 2, columns), lambda j, *_: (j, 0, 0)))
    kernel = functools.partial(merge_kernel, bit=bit)
    return launch(kernel, "merge_and_cut", (kinds,), [facts], inputs, [part, part], us=us, after=after)


def log2(count):
    return count.bit_length() - 1


def stage_orders(n_dp, n_seq, flavour):
    dp = [("dp", bit) for bit in range(1, log2(n_dp))]
    if flavour:
        dp = dp[::-1]
    seq = [("seq", bit) for bit in range(log2(n_seq))]
    return dp + seq, seq[:1] + dp + seq[1:]


def row_bits(n_dp, n_seq):
    return [("seq", bit) for bit in reversed(range(log2(n_seq)))] + [
        ("dp", bit) for bit in reversed(range(log2(n_dp)))
    ]


def block_places(n_dp, n_seq, flavour):
    bits, orders = row_bits(n_dp, n_seq), stage_orders(n_dp, n_seq, flavour)
    count = n_dp * n_seq
    tables = []
    for core in range(2):
        table = []
        for block in range(count):
            value = {step: (block >> (len(bits) - 1 - k)) & 1 for k, step in enumerate(bits)}
            owner = value[("dp", 0)]
            place = 0
            for step in orders[owner]:
                place = place * 2 + value[step]
            table.append(place + (count // 2 if owner == core else 0))
        tables.append(np.array(table, np.int32))
    return tables


def swap_pairs(n_dp, n_seq, steps):
    pairs = []
    for d in range(n_dp):
        for s in range(n_seq):
            axis, bit = steps[d % 2]
            there = (d ^ (1 << bit), s) if axis == "dp" else (d, s ^ (1 << bit))
            pairs.append((d * n_seq + s, there[0] * n_seq + there[1]))
    return pairs


def swap(value, steps):
    n_dp, n_seq = lax.axis_size("dp"), lax.axis_size("seq")
    return lax.ppermute(value, ("dp", "seq"), swap_pairs(n_dp, n_seq, steps))


def gather_steps(n_dp):
    dims = [("dp", bit) for bit in range(1, log2(n_dp))]
    return list(zip(dims[::-1], dims))


def stage_fact(n_dp, n_seq, flavour, stage):
    return 3 + flavour * (log2(n_dp * n_seq) - 1) + stage


def gather_fact(n_dp, n_seq, step):
    return 3 + 2 * (log2(n_dp * n_seq) - 1) + step


def places_fact(n_dp, n_seq, flavour, count):
    return gather_fact(n_dp, n_seq, log2(n_dp)) + flavour * count


def facts_table(n_dp, n_seq, group, places):
    table = []
    for d in range(n_dp):
        for s in range(n_seq):
            core = d & 1
            bit = lambda steps: ((d if steps[core][0] == "dp" else s) >> steps[core][1]) & 1
            row = [core, s, s * group]
            for flavour in range(2):
                row += [bit(steps) for steps in zip(*stage_orders(n_dp, n_seq, flavour))]
            row += [bit(steps) for steps in gather_steps(n_dp)] + [0]
            assert len(row) == places_fact(n_dp, n_seq, 0, 0)
            for flavour in range(2):
                row += list(places[flavour][core])
            table.append(row)
    return np.array(table, np.int32)


CORE = (("dp", 0), ("dp", 0))


class Chunk:
    def __init__(self, flavour):
        self.sizes = lax.axis_size("dp"), lax.axis_size("seq")
        self.flavour = flavour
        self.stages = list(zip(*stage_orders(*self.sizes, flavour)))
        self.done = 0

    def bit(self):
        return stage_fact(*self.sizes, self.flavour, self.done)

    def between_cores(self, *parts):
        self.got = [swap(part, CORE) for part in parts]

    def go(self, send, keep):
        self.keep = keep
        self.got = swap(send, self.stages[self.done])
        self.done += 1

    @property
    def last(self):
        return self.done == len(self.stages)


def advance(facts, *chunks, us=8, after=()):
    parts = add_and_cut(facts, [(chunk.keep, chunk.got, chunk.bit()) for chunk in chunks], us, after)
    for chunk, (send, keep) in zip(chunks, parts):
        chunk.go(send, keep)
    return parts[0][0]


def merge(facts, *chunks, us, after=()):
    whole = Chunk(chunks[0].flavour)
    whole.done = chunks[0].done
    pieces = [(chunk.keep, chunk.got) for chunk in chunks]
    whole.go(*merge_and_cut(facts, pieces, whole.bit(), us, after))
    return whole


def finish_kernel(*refs):
    out_ref, first = refs[-1], 0
    for keep_ref, got_ref in zip(refs[:-1:2], refs[1:-1:2]):
        columns = keep_ref.shape[2]
        total = keep_ref[...].astype(F32) + got_ref[...].astype(F32)
        out_ref[:, :, first : first + columns] = total.astype(BF16)
        first += columns


def finish(*chunks, us=8, after=()):
    kinds, part, _ = chunks[0].keep.shape
    inputs = [(array, full(*array.shape)) for chunk in chunks for array in (chunk.keep, chunk.got)]
    shape = (kinds, part, sum(chunk.keep.shape[2] for chunk in chunks))
    return launch(finish_kernel, "finish", (1,), [], inputs, [(shape, BF16, full(*shape))], us=us, after=after)[0]


def join_kernel(facts_ref, value_ref, got_ref, out_ref, *, bit):
    count = value_ref.shape[1]
    first = facts_ref[bit] * count
    out_ref[:, pl.ds(first, count)] = value_ref[...]
    out_ref[:, pl.ds(count - first, count)] = got_ref[...]


class Gather:
    def __init__(self, facts, value):
        self.facts = facts
        n_dp = lax.axis_size("dp")
        self.dims = [("dp", bit) for bit in range(1, log2(n_dp))]
        self.steps = gather_steps(n_dp)
        self.kinds, self.part, self.columns = value.shape
        self.value = value[:, None]
        self.done = 0
        self.send()

    @property
    def last(self):
        return self.done == len(self.steps)

    def send(self):
        self.got = swap(self.value, CORE if self.last else self.steps[self.done])

    def step(self, us=8, after=()):
        bit = gather_fact(lax.axis_size("dp"), lax.axis_size("seq"), self.done)
        kinds, count, part, columns = self.value.shape
        spec = lambda count: pl.BlockSpec((kinds, count, part, half_of(columns)), lambda j, *_: (0, 0, 0, j))
        (self.value,) = launch(
            functools.partial(join_kernel, bit=bit),
            "join",
            (2,),
            [self.facts],
            [(self.value, spec(count)), (self.got, spec(count))],
            [((kinds, 2 * count, part, columns), BF16, spec(2 * count))],
            us=us,
            after=after,
        )
        self.done += 1
        self.send()
        return self.value

    def whole(self):
        dims = self.dims
        core = lax.axis_index("dp") & 1
        halves = []
        for which, order in enumerate((dims[::-1], dims)):
            half = jnp.where(core == which, self.value, self.got)
            half = half.reshape((self.kinds,) + (2,) * len(dims) + (self.part, self.columns))
            wanted = [1 + order[::-1].index(step) for step in dims[::-1]]
            halves.append(half.transpose([0] + wanted + [len(dims) + 1, len(dims) + 2]))
        whole = jnp.stack(halves, axis=len(dims) + 1)
        return whole.reshape(self.kinds, lax.axis_size("dp") * self.part, self.columns)


def natural_rows(facts_ref, own_ref, got_ref, kind, step, columns):
    pieces = []
    for x in range(2):
        for which in range(2):
            index = x * 2 + step if which == 0 else step * 2 + x
            own, got = own_ref[kind, index, :, columns], got_ref[kind, index, :, columns]
            pieces.append(jnp.where(facts_ref[CORE_INDEX] == which, own, got))
    return jnp.concatenate(pieces, axis=0).astype(F32)


def row_sums(value):
    total = jnp.sum(value, axis=1, keepdims=True)
    return jnp.broadcast_to(total, (total.shape[0], LANES)).T[:1, :]


def put_ff_kernel(facts_ref, own_ref, got_ref, w_ref, gain_ref, gate_up_ref, down_ref, out_ref, dgain_ref):
    step = pl.program_id(0)
    rows = lambda kind: natural_rows(facts_ref, own_ref, got_ref, kind, step, slice(0, FF))
    wide = out_ref.shape[1]
    for kind in range(3):
        count = min(OUT_WIDE, wide - kind * OUT_WIDE)
        columns = slice(FF_WIDE, FF_WIDE + count)
        part = natural_rows(facts_ref, own_ref, got_ref, kind, step, columns)
        out_ref[:, kind * OUT_WIDE : kind * OUT_WIDE + count] = part
    down_ref[...] = rows(0).T
    gate, up = rows(1), rows(2)
    gate_up_ref[:, :FF] = gate
    gate_up_ref[:, FF:] = up
    weight = w_ref[...].astype(F32)
    total = row_sums(gate * weight[:, :FF]) + row_sums(up * weight[:, FF:])
    dgain_ref[...] = total / gain_ref[...]


def put_ff(gather, w_gate_up, gain, after=()):
    kept, width = 8 * gather.part, gain.shape[0]
    half = kept // 2
    whole = full(*gather.value.shape)
    return launch(
        put_ff_kernel,
        "put_ff",
        (2,),
        [gather.facts],
        [
            (gather.value, whole),
            (gather.got, whole),
            (w_gate_up, pl.BlockSpec((half, 2 * FF), lambda j, facts: (2 * facts[SEQ_INDEX] + j, 0))),
            (gain[None], pl.BlockSpec((1, half), lambda j, facts: (0, 2 * facts[SEQ_INDEX] + j))),
        ],
        [
            ((kept, 2 * FF), F32, pl.BlockSpec((half, 2 * FF), lambda j, *_: (j, 0))),
            ((FF, kept), F32, pl.BlockSpec((FF, half), lambda j, *_: (0, j))),
            ((kept, width), F32, pl.BlockSpec((half, width), lambda j, *_: (j, 0))),
            ((1, kept), F32, pl.BlockSpec((1, half), lambda j, *_: (0, j))),
        ],
        us=8,
        after=after,
    )


def put_att_kernel(facts_ref, own_ref, got_ref, w_ref, gain_ref, qkv_ref, dgain_ref):
    qkv = natural_rows(facts_ref, own_ref, got_ref, 0, pl.program_id(0), slice(0, qkv_ref.shape[1]))
    qkv_ref[...] = qkv
    dgain_ref[...] = row_sums(qkv * w_ref[...].astype(F32)) / gain_ref[...]


def put_att(gather, w_qkv, gain, after=()):
    kept, columns = 8 * gather.part, gather.columns
    half = kept // 2
    whole = full(*gather.value.shape)
    return launch(
        put_att_kernel,
        "put_att",
        (2,),
        [gather.facts],
        [
            (gather.value, whole),
            (gather.got, whole),
            (w_qkv, pl.BlockSpec((half, columns), lambda j, facts: (2 * facts[SEQ_INDEX] + j, 0))),
            (gain[None], pl.BlockSpec((1, half), lambda j, facts: (0, 2 * facts[SEQ_INDEX] + j))),
        ],
        [
            ((kept, columns), F32, pl.BlockSpec((half, columns), lambda j, *_: (j, 0))),
            ((1, kept), F32, pl.BlockSpec((1, half), lambda j, *_: (0, j))),
        ],
        us=8,
        after=after,
    )


def place_rows(turned, places):
    count = places.shape[0]
    blocks = turned.reshape((count, turned.shape[0] // count) + turned.shape[1:])
    return jnp.zeros_like(blocks).at[places].set(blocks).reshape(turned.shape)


def shifted(value, axis, steps):
    count = lax.axis_size(axis)
    leading, last = (max(0, -steps), min(count, count - steps))
    return lax.ppermute(value, axis, [(source, source + steps) for source in range(leading, last)])


def per_device(inputs, w_qkv, w_out, w_gate_up, w_down, gain_attn, gain_mlp, doc_start, cotangent):
    n_dp, n_seq = lax.axis_size("dp"), lax.axis_size("seq")
    rows, group, width = inputs.shape
    tokens = rows * group
    slab = width // (n_dp * n_seq)
    places = [block_places(n_dp, n_seq, flavour) for flavour in range(2)]
    ordered = slab % 16 == 0
    if not ordered:
        slab = 32
    blocks = width // slab
    listed = places if ordered else [[np.arange(blocks)] * 2] * 2
    table = facts_table(n_dp, n_seq, group, listed)
    device = lax.axis_index("dp") * n_seq + lax.axis_index("seq")
    facts = lax.dynamic_index_in_dim(jnp.asarray(table), device, axis=0, keepdims=False)
    put = [places_fact(n_dp, n_seq, flavour, blocks) for flavour in range(2)]
    core = lax.axis_index("dp") & 1

    def in_order(turned, flavour):
        if ordered:
            return turned
        return place_rows(turned, jnp.where(core == 0, *places[flavour]))

    x = inputs.reshape(tokens, width)
    dy = cotangent.reshape(tokens, width)

    tails = [(row + 1) * group for row in range(rows)]
    x_rim = shifted(inputs[:, group - WINDOW :], "seq", 1).reshape(rows * WINDOW, width)
    qkv, one_turned, dy_turned = norm_matmul(x, gain_attn, w_qkv, 0, facts, put[1], slab, dy)
    kv_rim, rim_turned = norm_matmul(x_rim, gain_attn, w_qkv, width, facts, put[1], slab, after=[qkv])
    att, att_turned = attend(qkv, kv_rim, doc_start, facts, put[1], slab)
    resid, normed_two, two_turned = out_proj(att, w_out, x, gain_mlp, facts, put[1], slab)
    one_turned, rim_turned, att_turned = [in_order(turned, 1) for turned in (one_turned, rim_turned, att_turned)]
    two_turned, dy_turned = [in_order(turned, 1) for turned in (two_turned, dy_turned)]

    def feed(first, count, total=None, end=None, after=()):
        hidden, dgu, *rest = feed_forward(
            normed_two, dy, dy_turned, two_turned, w_gate_up, w_down, first, count, total, end, after
        )
        chunk = Chunk(1)
        drb_da, sends = ([], rest[:3]) if end is None else (rest[3:5], rest[:3] + rest[5:])
        chunk.between_cores(*sends)
        return hidden, dgu, chunk, drb_da or rest[3:]

    def keep_ff(chunk, hidden, dgu, out=(), after=()):
        send, keep = ff_grad(facts, chunk.bit(), dy_turned, two_turned, hidden, dgu, chunk.got, out, after)
        chunk.go(send, keep)
        return send

    count = FF_CHUNKS[0]
    hidden_one, dgu_one, one, (total,) = feed(0, count)
    token = keep_ff(one, hidden_one, dgu_one)
    hidden_two, dgu_two, two, (drb, da) = feed(count, FF_CHUNKS[1], total, (resid, gain_mlp, w_out, att_turned), after=[token])
    token = advance(facts, one, after=[da])
    token = keep_ff(two, hidden_two, dgu_two, (att_turned, drb), after=[token])
    dqkv, drim = attend_back(qkv, kv_rim, doc_start, facts, da, after=[token])
    att = Chunk(1)
    grads = (facts, one_turned, rim_turned, dqkv, drim)
    (send,) = att_grad(*grads, us=20, after=[one.got])
    att.between_cores(send)
    token = advance(facts, one, two, us=30, after=[send])
    back = rim_grad(drim, w_qkv, x_rim, gain_attn, after=[token])
    back_got = shifted(back, "seq", -1)
    send, keep = att_grad(*grads, att.bit(), att.got[0], after=[back])
    att.go(send[None], keep[None])
    token = advance(facts, one, two, us=1, after=[send])
    grad_inputs = input_grad(dqkv, w_qkv, x, gain_attn, drb, back_got, tails, us=15, after=[token])
    token = advance(facts, att, two, after=[grad_inputs, one.got])
    while not (one.last and two.last):
        token = advance(facts, *(chunk for chunk in (one, two) if not chunk.last), after=[token])
    outputs = ff_out([hidden_one, hidden_two], w_down, resid, us=8, after=[token])
    token = advance(facts, att, after=[outputs])
    gather_ff = Gather(facts, finish(one, two, after=[token]))
    token = gather_ff.value
    while not att.last:
        token = advance(facts, att, after=[token])
    token = gather_ff.step(after=[token])
    gather = Gather(facts, finish(att, after=[token]))
    if ordered and n_dp == 8:
        token = gather.step(us=1, after=[gather.value])
        token = gather_ff.step(after=[token])
        token = gather.step(us=24, after=[token])
        total_gate_up, turned_down, total_out, gain_two = put_ff(gather_ff, w_gate_up, gain_mlp, after=[token])
        total_down = turned_down.T
        total_qkv, gain_one = put_att(gather, w_qkv, gain_attn, after=[total_gate_up])
        gain_one, gain_two = gain_one[0], gain_two[0]
    else:
        for both in (gather_ff, gather):
            while not both.last:
                both.step()
        total_ff = gather_ff.whole()
        total_qkv = gather.whole()[0].astype(F32)
        total_down, total_gate, total_up = [total_ff[kind, :, :FF] for kind in range(3)]
        total_down = total_down.astype(F32)
        total_gate_up = jnp.concatenate([total_gate, total_up], axis=1).astype(F32)
        outs = [total_ff[kind, :, FF_WIDE:] for kind in range(3)]
        total_out = jnp.concatenate(outs, axis=1)[:, :width].astype(F32)
        kept = total_qkv.shape[0]
        first_row = lax.axis_index("seq") * kept

        def gain_total(total, weight, gain):
            mine = lax.dynamic_slice_in_dim(weight, first_row, kept, axis=0).astype(F32)
            return jnp.sum(total * mine, axis=1) / lax.dynamic_slice_in_dim(gain, first_row, kept)

        gain_one = gain_total(total_qkv, w_qkv, gain_attn)
        gain_two = gain_total(total_gate_up, w_gate_up, gain_mlp)

    return (
        outputs.reshape(rows, group, width),
        grad_inputs.reshape(rows, group, width),
        total_qkv,
        total_out,
        total_gate_up,
        total_down,
        gain_one,
        gain_two,
    )


def solution(mesh):
    in_specs = (
        P("dp", "seq", None),
        P(),
        P(),
        P(),
        P(),
        P(),
        P(),
        P("dp", "seq"),
        P("dp", "seq", None),
    )
    out_specs = (
        P("dp", "seq", None),
        P("dp", "seq", None),
        P("seq", None),
        P("seq", None),
        P("seq", None),
        P("seq", None),
        P("seq"),
        P("seq"),
    )
    return jax.shard_map(
        per_device, mesh=mesh, in_specs=in_specs, out_specs=out_specs, check_vma=False
    )
```

```python
import functools
import math

import jax
import jax.numpy as jnp
import numpy as np
from jax import lax
from jax.experimental import pallas as pl
from jax.experimental.pallas import tpu as pltpu
from jax.sharding import PartitionSpec as P

HEADS = 16
HEAD_DIM = 64
FF = 2752
WINDOW = 64
LANES = 128
PAIRS = 2
FF_TILE = 256
FF_TILES = -(-FF // FF_TILE)
FF_CHUNKS = (7, 4)
FF_WIDE = FF_TILES * FF_TILE
STEP = 256
epsilon = 1e-05
masked_value = -1e30
F32 = jnp.float32
BF16 = jnp.bfloat16
VMEM_LIMIT = 64 * 1024 * 1024 - 64 * 1024
PER_US = 1.1e9


def dot(left, right, left_dim=1, right_dim=0):
    return lax.dot_general(
        left, right, (((left_dim,), (right_dim,)), ((), ())), preferred_element_type=F32
    )


def launch(kernel, name, grid, scalars, inputs, outputs, scratch=(), us=8, after=()):
    known = len(scalars) + len(inputs)

    def body(*refs):
        kernel(*refs[:known], *refs[known + len(after) :])

    specs = [spec for _, spec in inputs] + [pl.BlockSpec(memory_space=pl.ANY)] * len(after)
    shapes = [pltpu.HBM(shape, kind) for shape, kind, _ in outputs]
    moved = sum(array.size * array.dtype.itemsize for array, _ in inputs)
    moved += sum(math.prod(shape) * np.dtype(kind).itemsize for shape, kind, _ in outputs)
    return pl.pallas_call(
        body,
        grid_spec=pltpu.PrefetchScalarGridSpec(
            num_scalar_prefetch=len(scalars),
            grid=grid,
            in_specs=specs,
            out_specs=[spec for _, _, spec in outputs],
            scratch_shapes=list(scratch),
        ),
        out_shape=shapes,
        compiler_params=pltpu.CompilerParams(vmem_limit_bytes=VMEM_LIMIT),
        cost_estimate=pl.CostEstimate(flops=int(us * PER_US), bytes_accessed=int(moved / 100), transcendentals=0),
        name=name,
    )(*scalars, *[array for array, _ in inputs], *after)


def full(*shape):
    return pl.BlockSpec(shape, lambda *_: (0,) * len(shape))


CORE_INDEX, SEQ_INDEX, POSITION = range(3)


def store_slabs(out_ref, value, facts_ref, first, slab, columns=slice(None)):
    for k in range(value.shape[0] // slab):
        row = pl.multiple_of(facts_ref[first + k] * slab, slab)
        out_ref[pl.ds(row, slab), columns] = value[k * slab : (k + 1) * slab]


def side_by_side(ref):
    return jnp.concatenate([ref[k] for k in range(ref.shape[0])], axis=1)


def put_blocks(ref, value, rows=slice(None)):
    for k in range(ref.shape[0]):
        ref[k, rows, :] = value[:, k * LANES : (k + 1) * LANES]

def two_heads(value, low):
    zero = jnp.zeros_like(value)
    return jnp.concatenate([jnp.where(low, value, zero), jnp.where(low, zero, value)], axis=0)


def one_of_two(value, size):
    feature = lax.broadcasted_iota(jnp.int32, (LANES, size), 0)
    return jnp.where(feature < HEAD_DIM, value[:, :size], value[:, size:])


class Spans:
    def __init__(self, rows, group):
        self.rows, self.group = rows, group
        self.size = min(128, group)
        self.blocks = group // self.size
        self.count = rows * self.blocks
        self.window = self.size + WINDOW

    def queries(self, at):
        return slice(at * self.size, (at + 1) * self.size)

    def keys(self, own_ref, rim_ref, pair, at):
        row, block = divmod(at, self.blocks)
        start = at * self.size
        if block == 0:
            rim = rim_ref[pair, row * WINDOW : (row + 1) * WINDOW, :]
            return jnp.concatenate([rim, own_ref[pair, start : start + self.size, :]], axis=0)
        return own_ref[pair, start - WINDOW : start + self.size, :]

    def fill_bias(self, bias_ref, starts_ref, facts_ref):
        size = self.size
        key = lax.broadcasted_iota(jnp.int32, (self.window, size), 0) - WINDOW
        query = lax.broadcasted_iota(jnp.int32, (self.window, size), 1)
        near = (key <= query) & (query - key <= WINDOW)
        for at in range(self.count):
            row, block = divmod(at, self.blocks)
            begin = starts_ref[row : row + 1, block * size : (block + 1) * size]
            begin = begin - facts_ref[POSITION] - block * size
            bias = jnp.where(near & (key >= begin), 0.0, masked_value).astype(F32)
            bias_ref[at, :, :size] = bias
            bias_ref[at, :, size:] = bias

    def scratch(self, kind):
        return pltpu.VMEM((self.count, self.window, 2 * self.size), kind)


def softmax(scores):
    weights = jnp.exp(scores - jnp.max(scores, axis=0, keepdims=True))
    return weights * (1.0 / jnp.sum(weights, axis=0, keepdims=True))


def attend_kernel(facts_ref, starts_ref, q_ref, k_ref, v_ref, kr_ref, vr_ref,
                  att_ref, attT_ref, bias_ref, score_ref, probs_ref, *, spans, slab, put, pairs):
    step = pl.program_id(0)
    size, count = spans.size, spans.count

    @pl.when(step == 0)
    def _():
        spans.fill_bias(bias_ref, starts_ref, facts_ref)

    low = lax.broadcasted_iota(jnp.int32, (size, LANES), 1) < HEAD_DIM
    for pair in range(pairs):
        for at in range(count):
            queries = q_ref[pair, spans.queries(at), :] * jnp.asarray(HEAD_DIM ** (-0.5), BF16)
            keys = spans.keys(k_ref, kr_ref, pair, at)
            score_ref[at] = dot(keys, two_heads(queries, low), 1, 1)
        for at in range(count):
            probs_ref[at] = softmax(score_ref[at] + bias_ref[at]).astype(BF16)
        for at in range(count):
            values = spans.keys(v_ref, vr_ref, pair, at)
            mixed = one_of_two(dot(values, probs_ref[at], 0, 0), size)
            att_ref[pair, spans.queries(at), :] = mixed.T.astype(BF16)
            first = put + (step * pairs + pair) * (LANES // slab)
            store_slabs(attT_ref, mixed.astype(BF16), facts_ref, first, slab, spans.queries(at))


def attend(qkv, kv_rim, doc_start, facts, put, slab, after=()):
    rows, group = doc_start.shape
    all_pairs, tokens = qkv.shape[0] // 3, qkv.shape[1]
    rim = kv_rim.shape[1]
    spans = Spans(rows, group)
    steps = all_pairs // PAIRS
    own = lambda kind: pl.BlockSpec((PAIRS, tokens, LANES), lambda j, *_: (kind * steps + j, 0, 0))
    edge = lambda kind: pl.BlockSpec((PAIRS, rim, LANES), lambda j, *_: (kind * steps + j, 0, 0))
    width = all_pairs * LANES
    return launch(
        functools.partial(attend_kernel, spans=spans, slab=slab, put=put, pairs=PAIRS),
        "attend",
        (steps,),
        [facts],
        [
            (doc_start, full(rows, group)),
            (qkv, own(0)),
            (qkv, own(1)),
            (qkv, own(2)),
            (kv_rim, edge(0)),
            (kv_rim, edge(1)),
        ],
        [
            ((all_pairs, tokens, LANES), BF16, own(0)),
            ((width, tokens), BF16, full(width, tokens)),
        ],
        [spans.scratch(F32), spans.scratch(F32), spans.scratch(BF16)],
        us=8,
        after=after,
    )


def attend_back_kernel(facts_ref, starts_ref, q_ref, k_ref, v_ref, kr_ref, vr_ref, da_ref,
                       dqkv_ref, drim_ref,
                       bias_ref, score_ref, grad_ref, probs_ref, dscore_ref, *, spans, pairs):
    size, count = spans.size, spans.count

    @pl.when(pl.program_id(0) == 0)
    def _():
        spans.fill_bias(bias_ref, starts_ref, facts_ref)

    low = lax.broadcasted_iota(jnp.int32, (size, LANES), 1) < HEAD_DIM
    scale = HEAD_DIM ** (-0.5)

    def scaled_queries(pair, at):
        return two_heads(q_ref[pair, spans.queries(at), :] * jnp.asarray(scale, BF16), low)

    for pair in range(pairs):
        for at in range(count):
            score_ref[at] = dot(spans.keys(k_ref, kr_ref, pair, at), scaled_queries(pair, at), 1, 1)
            grads = two_heads(da_ref[pair, spans.queries(at), :], low)
            grad_ref[at] = dot(spans.keys(v_ref, vr_ref, pair, at), grads, 1, 1)
        for at in range(count):
            probs = softmax(score_ref[at] + bias_ref[at])
            probs_ref[at] = probs.astype(BF16)
            part = probs * grad_ref[at]
            dscore_ref[at] = (part - probs * jnp.sum(part, axis=0, keepdims=True)).astype(BF16)
        late = [None, None]
        for at in range(count):
            here = spans.queries(at)
            row, block = divmod(at, spans.blocks)
            dscores = dscore_ref[at]
            grads = two_heads(da_ref[pair, here, :], low)
            dk = dot(dscores, scaled_queries(pair, at))
            dv = dot(probs_ref[at], grads)
            dq = one_of_two(dot(spans.keys(k_ref, kr_ref, pair, at), dscores, 0, 0), size) * scale
            dqkv_ref[0, pair, here, :] = dq.T.astype(BF16)
            start = at * size
            for kind, grad in ((0, dk), (1, dv)):
                out_ref, rim_ref = dqkv_ref.at[kind + 1], drim_ref.at[kind]
                early = grad[:WINDOW]
                if block == 0:
                    rim_ref[pair, row * WINDOW : (row + 1) * WINDOW, :] = early.astype(BF16)
                else:
                    out_ref[pair, start - WINDOW : start, :] = (late[kind] + early).astype(BF16)
                if size > WINDOW:
                    out_ref[pair, start : start + size - WINDOW, :] = grad[WINDOW:size].astype(BF16)
                late[kind] = grad[size:]
                if block == spans.blocks - 1:
                    out_ref[pair, start + size - WINDOW : start + size, :] = late[kind].astype(BF16)


def attend_back(qkv, kv_rim, doc_start, facts, grad_att, after=()):
    rows, group = doc_start.shape
    all_pairs, tokens = qkv.shape[0] // 3, qkv.shape[1]
    rim = kv_rim.shape[1]
    spans = Spans(rows, group)
    steps = all_pairs // PAIRS
    own = lambda kind: pl.BlockSpec((PAIRS, tokens, LANES), lambda j, *_: (kind * steps + j, 0, 0))
    edge = lambda kind: pl.BlockSpec((PAIRS, rim, LANES), lambda j, *_: (kind * steps + j, 0, 0))
    return launch(
        functools.partial(attend_back_kernel, spans=spans, pairs=PAIRS),
        "attend_back",
        (steps,),
        [facts],
        [
            (doc_start, full(rows, group)),
            (qkv, own(0)),
            (qkv, own(1)),
            (qkv, own(2)),
            (kv_rim, edge(0)),
            (kv_rim, edge(1)),
            (grad_att, own(0)),
        ],
        [
            ((3, all_pairs, tokens, LANES), BF16, pl.BlockSpec((3, PAIRS, tokens, LANES), lambda j, *_: (0, j, 0, 0))),
            ((2, all_pairs, rim, LANES), BF16, pl.BlockSpec((2, PAIRS, rim, LANES), lambda j, *_: (0, j, 0, 0))),
        ],
        [spans.scratch(kind) for kind in (F32, F32, F32, BF16, BF16)],
        us=8,
        after=after,
    )


def norm_matmul_kernel(facts_ref, x_ref, gain_ref, w_ref, *refs, slab, put, step, beside):
    if beside:
        other_ref, out_ref, normedT_ref, otherT_ref, normed_ref = refs
    else:
        out_ref, normedT_ref, normed_ref = refs

    @pl.when(pl.program_id(0) == 0)
    def _():
        for at in range(0, x_ref.shape[0], step):
            x = x_ref[at : at + step, :].astype(F32)
            inv = lax.rsqrt(jnp.mean(x * x, axis=-1, keepdims=True) + epsilon)
            normed = (x * inv * gain_ref[...]).astype(BF16)
            normed_ref[at : at + step, :] = normed
            store_slabs(normedT_ref, normed.T, facts_ref, put, slab, slice(at, at + step))

    put_blocks(out_ref, dot(normed_ref[...], w_ref[...]).astype(BF16))
    if beside:
        store_slabs(otherT_ref, other_ref[...].T, facts_ref, put, slab)


def norm_matmul(x, gain, weight, first_column, facts, put, slab, beside=None, after=()):
    tokens, width = x.shape
    columns = weight.shape[1] - first_column
    tile = 1024 if beside is None else 768
    skip, wide, steps = first_column // tile, tile // LANES, columns // tile
    part = tokens // steps
    others, turned = [], []
    if beside is not None:
        others = [(beside, pl.BlockSpec((part, width), lambda j, *_: (j, 0)))]
        turned = [((width, tokens), BF16, pl.BlockSpec((width, part), lambda j, *_: (0, j)))]
    return launch(
        functools.partial(norm_matmul_kernel, slab=slab, put=put, step=min(STEP, tokens), beside=beside is not None),
        "norm_matmul",
        (steps,),
        [facts],
        [
            (x, full(tokens, width)),
            (gain[None], full(1, width)),
            (weight, pl.BlockSpec((width, tile), lambda j, *_: (0, skip + j))),
        ]
        + others,
        [
            ((columns // LANES, tokens, LANES), BF16, pl.BlockSpec((wide, tokens, LANES), lambda j, *_: (j, 0, 0))),
            ((width, tokens), BF16, full(width, tokens)),
        ]
        + turned,
        [pltpu.VMEM((tokens, width), BF16)],
        us=8,
        after=after,
    )


def out_proj_kernel(facts_ref, att_ref, w_ref, x_ref, gain_ref, resid_ref, normed_ref, normedT_ref, *, slab, put):
    resid = x_ref[...].astype(F32) + dot(side_by_side(att_ref), w_ref[...])
    resid_ref[...] = resid.astype(BF16)
    inv = lax.rsqrt(jnp.mean(resid * resid, axis=-1, keepdims=True) + epsilon)
    normed = (resid * inv * gain_ref[...]).astype(BF16)
    normed_ref[...] = normed
    store_slabs(normedT_ref, normed.T, facts_ref, put, slab)


def out_proj(att, w_out, x, gain, facts, put, slab, after=()):
    tokens, width = x.shape
    pairs = att.shape[0]
    step = 2 * STEP
    rows = pl.BlockSpec((step, width), lambda m, *_: (m, 0))
    return launch(
        functools.partial(out_proj_kernel, slab=slab, put=put),
        "out_proj",
        (tokens // step,),
        [facts],
        [
            (att, pl.BlockSpec((pairs, step, LANES), lambda m, *_: (0, m, 0))),
            (w_out, full(width, width)),
            (x, rows),
            (gain[None], full(1, width)),
        ],
        [
            ((tokens, width), BF16, rows),
            ((tokens, width), BF16, rows),
            ((width, tokens), BF16, pl.BlockSpec((width, step), lambda m, *_: (0, m))),
        ],
        us=8,
        after=after,
    )


def ff_kernel(*refs, first, given, ends):
    normed_ref, dy_ref, dyT_ref, normedT_ref, wg_ref, wu0_ref, wu1_ref, wu2_ref, wd_ref = refs[:9]
    rest = list(refs[9:])
    total_in = rest.pop(0) if given else None
    if ends:
        resid_ref, gain_ref, w_out_ref, attT_ref = rest[:4]
        rest = rest[4:]
    hidden_ref, dgu_ref, send_down, send_gate, send_up, *totals, acc_ref = rest
    tile = pl.program_id(0)
    tokens = normed_ref.shape[0]

    @pl.when(tile == 0)
    def _():
        acc_ref[...] = total_in[...] if given else jnp.zeros_like(acc_ref)

    half = FF % LANES
    w_both = jnp.concatenate([wg_ref[...], wu0_ref[:, half:], wu1_ref[...], wu2_ref[:, :half]], axis=1)
    limit = FF - (tile + first) * FF_TILE
    inside = lax.broadcasted_iota(jnp.int32, (STEP, FF_TILE), 1) < limit

    def products(at):
        here = slice(at, at + STEP)
        both = dot(normed_ref[here, :], w_both)
        return both[:, :FF_TILE], both[:, FF_TILE:], dot(dy_ref[here, :], wd_ref[...], 1, 1)

    def act(at, gate, up, back):
        here = slice(at, at + STEP)
        sigma = 1.0 / (1.0 + jnp.exp(-gate))
        silu = gate * sigma
        hidden_ref[here, :] = jnp.where(inside, silu * up, 0.0).astype(BF16)
        dgate = back * up * (sigma * (1.0 + gate * (1.0 - sigma)))
        dgu_ref[0, here, :] = jnp.where(inside, dgate, 0.0).astype(BF16)
        dgu_ref[1, here, :] = jnp.where(inside, back * silu, 0.0).astype(BF16)

    def norm_grad(at):
        here = slice(at, at + STEP)
        grads = jnp.concatenate([dgu_ref[0, here, :], dgu_ref[1, here, :]], axis=1)
        acc_ref[here, :] += dot(grads, w_both, 1, 1)

    held = products(0)
    for at in range(0, tokens, STEP):
        ahead = products(at + STEP) if at + STEP < tokens else None
        act(at, *held)
        norm_grad(at)
        held = ahead
    send_down[...] = dot(dyT_ref[...], hidden_ref[...]).astype(BF16)
    both = dot(normedT_ref[...], jnp.concatenate([dgu_ref[0], dgu_ref[1]], axis=1)).astype(BF16)
    send_gate[...] = both[:, :FF_TILE]
    send_up[...] = both[:, FF_TILE:]

    @pl.when(tile == pl.num_programs(0) - 1)
    def _():
        if not ends:
            totals[0][...] = acc_ref[...]
            return
        drb_ref, da_ref, send_out = totals
        for at in range(0, tokens, STEP):
            here = slice(at, at + STEP)
            grad = norm_back(acc_ref[here, :], resid_ref[here, :].astype(F32), gain_ref[...])
            branch = (dy_ref[here, :].astype(F32) + grad).astype(BF16)
            put_blocks(drb_ref, branch, here)
            put_blocks(da_ref, dot(branch, w_out_ref[...], 1, 1).astype(BF16), here)
        send_out[...] = dot(attT_ref[...], side_by_side(drb_ref)).astype(BF16)


def feed_forward(normed, dy, dy_turned, normed_turned, w_gate_up, w_down, first, count, total=None, end=None, after=()):
    tokens, width = normed.shape
    wide = count * FF_TILE
    last = w_gate_up.shape[1] // LANES - 1
    skip = FF // LANES + first * (FF_TILE // LANES)
    up = lambda k: pl.BlockSpec(
        (width, LANES), lambda j: (0, jnp.minimum(skip + k + j * (FF_TILE // LANES), last))
    )
    other_half = full(width // 2, tokens)
    given = [] if total is None else [(total, full(tokens, width))]
    ending, results = [], [((tokens, width), F32, full(tokens, width))]
    if end is not None:
        resid, gain, w_out, att_turned = end
        ending = [(resid, full(tokens, width)), (gain[None], full(1, width)), (w_out, full(width, width))]
        ending.append((att_turned, other_half))
        blocks = (width // LANES, tokens, LANES)
        results = [(blocks, BF16, full(*blocks))] * 2
        results.append(((width // 2, width), BF16, full(width // 2, width)))
    return launch(
        functools.partial(ff_kernel, first=first, given=len(given), ends=end is not None),
        "feed_forward",
        (count,),
        [],
        [
            (normed, full(tokens, width)),
            (dy, full(tokens, width)),
            (dy_turned, other_half),
            (normed_turned, other_half),
            (w_gate_up, pl.BlockSpec((width, FF_TILE), lambda j: (0, first + j))),
            (w_gate_up, up(0)),
            (w_gate_up, up(1)),
            (w_gate_up, up(2)),
            (w_down.T, pl.BlockSpec((FF_TILE, width), lambda j: (first + j, 0))),
        ]
        + given
        + ending,
        [
            ((tokens, wide), BF16, pl.BlockSpec((tokens, FF_TILE), lambda j: (0, j))),
            ((2, tokens, wide), BF16, pl.BlockSpec((2, tokens, FF_TILE), lambda j: (0, 0, j))),
        ]
        + [((width // 2, wide), BF16, pl.BlockSpec((width // 2, FF_TILE), lambda j: (0, j)))] * 3
        + results,
        [pltpu.VMEM((tokens, width), F32)],
        us=8,
        after=after,
    )


OUT_WIDE = 3 * LANES


def ff_grad_kernel(facts_ref, dyT_ref, normedT_ref, hidden_ref, dgu_ref, got_down, got_gate, got_up, *rest, bit, tiles):
    send_ref, keep_ref = rest[-2:]
    part = send_ref.shape[1]
    own = facts_ref[bit]
    step = pl.program_id(0)

    def put(kind, left_ref, right, got_ref, at, columns):
        for out_ref, index in ((send_ref, 1 - own), (keep_ref, own)):
            rows = pl.ds(pl.multiple_of(index * part, part), part)
            total = dot(left_ref[rows, :], right) + got_ref[rows, at : at + columns].astype(F32)
            out_ref[kind, :, :columns] = total.astype(BF16)

    @pl.when(step < tiles)
    def _():
        columns = hidden_ref.shape[1]
        put(0, dyT_ref, hidden_ref[...], got_down, 0, columns)
        put(1, normedT_ref, dgu_ref[0], got_gate, 0, columns)
        put(2, normedT_ref, dgu_ref[1], got_up, 0, columns)

    if len(rest) == 2:
        return
    attT_ref, drb_ref, got_out = rest[:3]
    each = hidden_ref.shape[1] // LANES
    for late in range(-(-OUT_WIDE // (each * LANES))):

        @pl.when(step == tiles + late)
        def _():
            send_ref[...] = jnp.zeros_like(send_ref)
            keep_ref[...] = jnp.zeros_like(keep_ref)
            for kind in range(3):
                blocks = range(kind * 3 + each * late, kind * 3 + min(3, each * (late + 1)))
                blocks = [block for block in blocks if block < drb_ref.shape[0]]
                if blocks:
                    right = jnp.concatenate([drb_ref[block] for block in blocks], axis=1)
                    put(kind, attT_ref, right, got_out, blocks[0] * LANES, len(blocks) * LANES)


def ff_grad(facts, bit, dy_turned, normed_turned, hidden, dgu, got, out=(), after=()):
    width, tokens = dy_turned.shape
    wide = hidden.shape[1]
    tile = 512 if wide % 512 == 0 else FF_TILE
    tiles = wide // tile
    own_half = pl.BlockSpec((width // 2, tokens), lambda j, *_: (1, 0))
    at = lambda j: jnp.minimum(j, tiles - 1)
    extra, columns, steps = [], wide, tiles
    if out:
        att_turned, drb = out
        extra = [(att_turned, own_half), (drb, full(*drb.shape)), (got[3], full(*got[3].shape))]
        columns, steps = wide + OUT_WIDE, tiles + -(-OUT_WIDE // tile)
    part = ((3, width // 4, columns), BF16, pl.BlockSpec((3, width // 4, tile), lambda j, *_: (0, 0, j)))
    return launch(
        functools.partial(ff_grad_kernel, bit=bit, tiles=tiles),
        "ff_grad",
        (steps,),
        [facts],
        [
            (dy_turned, own_half),
            (normed_turned, own_half),
            (hidden, pl.BlockSpec((tokens, tile), lambda j, *_: (0, at(j)))),
            (dgu, pl.BlockSpec((2, tokens, tile), lambda j, *_: (0, 0, at(j)))),
        ]
        + [(value, pl.BlockSpec((width // 2, tile), lambda j, *_: (0, at(j)))) for value in got[:3]]
        + extra,
        [part, part],
        us=8,
        after=after,
    )


def norm_back(grad, values, gain):
    inv = lax.rsqrt(jnp.mean(values * values, axis=-1, keepdims=True) + epsilon)
    scaled = grad * gain
    return inv * scaled - values * (inv * inv * inv) * jnp.mean(scaled * values, axis=-1, keepdims=True)


def ff_out_kernel(*refs):
    wd_ref, resid_ref, out_ref = refs[-3:]
    total, first = resid_ref[...].astype(F32), 0
    for hidden_ref in refs[:-3]:
        count = min(hidden_ref.shape[1], FF - first)
        total += dot(hidden_ref[:, :count], wd_ref[first : first + count, :])
        first += count
    out_ref[...] = total.astype(BF16)


def ff_out(hiddens, w_down, resid, us, after=()):
    tokens, width = resid.shape
    rows = lambda columns: pl.BlockSpec((STEP, columns), lambda m: (m, 0))
    return launch(
        ff_out_kernel,
        "ff_out",
        (tokens // STEP,),
        [],
        [(hidden, rows(hidden.shape[1])) for hidden in hiddens]
        + [(w_down.T, full(FF, width)), (resid, rows(width))],
        [((tokens, width), BF16, rows(width))],
        us=us,
        after=after,
    )[0]


def att_grad_kernel(facts_ref, *refs, bit):
    split = bit is not None
    oneT_ref, rimT_ref, dqkv_ref, drim_ref = refs[:4]
    kind = pl.program_id(0)

    def put(total):
        if split:
            got_ref, send_ref, keep_ref = refs[-3:]
            part = send_ref.shape[0]
            own = facts_ref[bit]
            for out_ref, half in ((send_ref, 1 - own), (keep_ref, own)):
                rows = pl.ds(pl.multiple_of(half * part, part), part)
                out_ref[...] = (total(rows) + got_ref[rows, :].astype(F32)).astype(BF16)
        else:
            refs[-1][...] = total(slice(None)).astype(BF16)

    @pl.when(kind == 0)
    def _():
        right = side_by_side(dqkv_ref)
        put(lambda rows: dot(oneT_ref[rows, :], right))

    @pl.when(kind > 0)
    def _():
        right, rim = side_by_side(dqkv_ref), side_by_side(drim_ref)
        put(lambda rows: dot(oneT_ref[rows, :], right) + dot(rimT_ref[rows, :], rim))


def att_grad(facts, one_turned, rim_turned, dqkv, drim, bit=None, got=None, us=8, after=()):
    width, tokens = one_turned.shape
    rim = rim_turned.shape[1]
    split = got is not None
    half = 1 if split else 0
    inputs = [
        (turned, pl.BlockSpec((width // 2, turned.shape[1]), lambda j, *_: (half, 0)))
        for turned in (one_turned, rim_turned)
    ]
    blocks = width // LANES
    inputs += [
        (dqkv, pl.BlockSpec((None, blocks, tokens, LANES), lambda j, *_: (j, 0, 0, 0))),
        (drim, pl.BlockSpec((None, blocks, rim, LANES), lambda j, *_: (jnp.maximum(j - 1, 0), 0, 0, 0))),
    ]
    columns = 3 * width
    tile = pl.BlockSpec((width // 2, width), lambda j, *_: (0, j))
    if split:
        inputs.append((got, tile))
        part = ((width // 4, columns), BF16, pl.BlockSpec((width // 4, width), lambda j, *_: (0, j)))
        outputs = [part, part]
    else:
        outputs = [((width // 2, columns), BF16, tile)]
    return launch(
        functools.partial(att_grad_kernel, bit=bit),
        "att_grad",
        (3,),
        [facts],
        inputs,
        outputs,
        us=us,
        after=after,
    )


def input_grad_kernel(dqkv_ref, w_ref, x_ref, gain_ref, drb_ref, back_ref, out_ref, *, tails):
    step = out_ref.shape[0]
    grads = jnp.concatenate([side_by_side(dqkv_ref.at[kind]) for kind in range(3)], axis=1)
    grad = norm_back(dot(grads, w_ref[...], 1, 1), x_ref[...].astype(F32), gain_ref[...])
    out_ref[...] = grad + side_by_side(drb_ref).astype(F32)
    for row, end in enumerate(tails):
        block, last = divmod(end - WINDOW, step)

        @pl.when(pl.program_id(0) == block)
        def _():
            out_ref[last : last + WINDOW, :] += back_ref[row * WINDOW : (row + 1) * WINDOW, :].astype(F32)


def input_grad(dqkv, w_qkv, x, gain, drb, back, tails, us, after=()):
    tokens, width = x.shape
    blocks = width // LANES
    rows = pl.BlockSpec((STEP, width), lambda m: (m, 0))
    return launch(
        functools.partial(input_grad_kernel, tails=tails),
        "input_grad",
        (tokens // STEP,),
        [],
        [
            (dqkv, pl.BlockSpec((3, blocks, STEP, LANES), lambda m: (0, 0, m, 0))),
            (w_qkv, full(*w_qkv.shape)),
            (x, rows),
            (gain[None], full(1, width)),
            (drb, pl.BlockSpec((blocks, STEP, LANES), lambda m: (0, m, 0))),
            (back, full(*back.shape)),
        ],
        [((tokens, width), F32, rows)],
        us=us,
        after=after,
    )[0]


def rim_grad_kernel(drim_ref, wk_ref, wv_ref, x_ref, gain_ref, out_ref):
    grad = dot(side_by_side(drim_ref.at[0]), wk_ref[...], 1, 1)
    grad += dot(side_by_side(drim_ref.at[1]), wv_ref[...], 1, 1)
    out_ref[...] = norm_back(grad, x_ref[...].astype(F32), gain_ref[...]).astype(BF16)


def rim_grad(drim, w_qkv, x, gain, after=()):
    rim, width = x.shape
    part = lambda k: pl.BlockSpec((width, width), lambda j: (0, k))
    return launch(
        rim_grad_kernel,
        "rim_grad",
        (1,),
        [],
        [
            (drim, full(*drim.shape)),
            (w_qkv, part(1)),
            (w_qkv, part(2)),
            (x, full(rim, width)),
            (gain[None], full(1, width)),
        ],
        [((rim, width), BF16, full(rim, width))],
        us=8,
        after=after,
    )[0]


def half_of(columns):
    return -(-columns // (2 * LANES)) * LANES


def add_kernel(facts_ref, *refs, bits):
    count = len(bits)
    for k, bit in enumerate(bits):
        keep_ref, got_ref = refs[2 * k : 2 * k + 2]
        outs = refs[2 * count + 2 * k : 2 * count + 2 * k + 2]
        for out_ref, index in zip(outs, (1 - facts_ref[bit], facts_ref[bit])):
            out_ref[...] = (keep_ref[:, index].astype(F32) + got_ref[:, index].astype(F32)).astype(BF16)


def add_and_cut(facts, items, us, after=()):
    inputs, outputs = [], []
    for keep, got, _ in items:
        kinds, rows, columns = keep.shape
        cut = lambda value: value.reshape(kinds, 2, rows // 2, columns)
        spec = pl.BlockSpec((kinds, 2, rows // 2, half_of(columns)), lambda j, *_: (0, 0, 0, j))
        part = pl.BlockSpec((kinds, rows // 2, half_of(columns)), lambda j, *_: (0, 0, j))
        inputs += [(cut(keep), spec), (cut(got), spec)]
        outputs += [((kinds, rows // 2, columns), BF16, part)] * 2
    kernel = functools.partial(add_kernel, bits=[bit for _, _, bit in items])
    parts = launch(kernel, "add_and_cut", (2,), [facts], inputs, outputs, us=us, after=after)
    return [(parts[2 * k], parts[2 * k + 1]) for k in range(len(items))]


def merge_kernel(facts_ref, *refs, bit):
    *parts, send_ref, keep_ref = refs
    for out_ref, index in ((send_ref, 1 - facts_ref[bit]), (keep_ref, facts_ref[bit])):
        first = 0
        for keep, got in zip(parts[::2], parts[1::2]):
            columns = keep.shape[3]
            total = keep[:, index].astype(F32) + got[:, index].astype(F32)
            out_ref[:, :, first : first + columns] = total.astype(BF16)
            first += columns


def merge_and_cut(facts, pieces, bit, us, after=()):
    inputs = []
    for keep, got in pieces:
        kinds, rows, columns = keep.shape
        spec = pl.BlockSpec((1, 2, rows // 2, columns), lambda j, *_: (j, 0, 0, 0))
        inputs += [(value.reshape(kinds, 2, rows // 2, columns), spec) for value in (keep, got)]
    columns = sum(keep.shape[2] for keep, _ in pieces)
    part = ((kinds, rows // 2, columns), BF16, pl.BlockSpec((1, rows // 2, columns), lambda j, *_: (j, 0, 0)))
    kernel = functools.partial(merge_kernel, bit=bit)
    return launch(kernel, "merge_and_cut", (kinds,), [facts], inputs, [part, part], us=us, after=after)


def log2(count):
    return count.bit_length() - 1


def stage_orders(n_dp, n_seq, flavour):
    dp = [("dp", bit) for bit in range(1, log2(n_dp))]
    if flavour:
        dp = dp[::-1]
    seq = [("seq", bit) for bit in range(log2(n_seq))]
    return dp + seq, seq[:1] + dp + seq[1:]


def row_bits(n_dp, n_seq):
    return [("seq", bit) for bit in reversed(range(log2(n_seq)))] + [
        ("dp", bit) for bit in reversed(range(log2(n_dp)))
    ]


def block_places(n_dp, n_seq, flavour):
    bits, orders = row_bits(n_dp, n_seq), stage_orders(n_dp, n_seq, flavour)
    count = n_dp * n_seq
    tables = []
    for core in range(2):
        table = []
        for block in range(count):
            value = {step: (block >> (len(bits) - 1 - k)) & 1 for k, step in enumerate(bits)}
            owner = value[("dp", 0)]
            place = 0
            for step in orders[owner]:
                place = place * 2 + value[step]
            table.append(place + (count // 2 if owner == core else 0))
        tables.append(np.array(table, np.int32))
    return tables


def swap_pairs(n_dp, n_seq, steps):
    pairs = []
    for d in range(n_dp):
        for s in range(n_seq):
            axis, bit = steps[d % 2]
            there = (d ^ (1 << bit), s) if axis == "dp" else (d, s ^ (1 << bit))
            pairs.append((d * n_seq + s, there[0] * n_seq + there[1]))
    return pairs


def swap(value, steps):
    n_dp, n_seq = lax.axis_size("dp"), lax.axis_size("seq")
    return lax.ppermute(value, ("dp", "seq"), swap_pairs(n_dp, n_seq, steps))


def gather_steps(n_dp):
    dims = [("dp", bit) for bit in range(1, log2(n_dp))]
    return list(zip(dims[::-1], dims))


def stage_fact(n_dp, n_seq, flavour, stage):
    return 3 + flavour * (log2(n_dp * n_seq) - 1) + stage


def gather_fact(n_dp, n_seq, step):
    return 3 + 2 * (log2(n_dp * n_seq) - 1) + step


def places_fact(n_dp, n_seq, flavour, count):
    return gather_fact(n_dp, n_seq, log2(n_dp)) + flavour * count


def facts_table(n_dp, n_seq, group, places):
    table = []
    for d in range(n_dp):
        for s in range(n_seq):
            core = d & 1
            bit = lambda steps: ((d if steps[core][0] == "dp" else s) >> steps[core][1]) & 1
            row = [core, s, s * group]
            for flavour in range(2):
                row += [bit(steps) for steps in zip(*stage_orders(n_dp, n_seq, flavour))]
            row += [bit(steps) for steps in gather_steps(n_dp)] + [0]
            assert len(row) == places_fact(n_dp, n_seq, 0, 0)
            for flavour in range(2):
                row += list(places[flavour][core])
            table.append(row)
    return np.array(table, np.int32)


CORE = (("dp", 0), ("dp", 0))


class Chunk:
    def __init__(self, flavour):
        self.sizes = lax.axis_size("dp"), lax.axis_size("seq")
        self.flavour = flavour
        self.stages = list(zip(*stage_orders(*self.sizes, flavour)))
        self.done = 0

    def bit(self):
        return stage_fact(*self.sizes, self.flavour, self.done)

    def between_cores(self, *parts):
        self.got = [swap(part, CORE) for part in parts]

    def go(self, send, keep):
        self.keep = keep
        self.got = swap(send, self.stages[self.done])
        self.done += 1

    @property
    def last(self):
        return self.done == len(self.stages)


def advance(facts, *chunks, us=8, after=()):
    parts = add_and_cut(facts, [(chunk.keep, chunk.got, chunk.bit()) for chunk in chunks], us, after)
    for chunk, (send, keep) in zip(chunks, parts):
        chunk.go(send, keep)
    return parts[0][0]


def merge(facts, *chunks, us, after=()):
    whole = Chunk(chunks[0].flavour)
    whole.done = chunks[0].done
    pieces = [(chunk.keep, chunk.got) for chunk in chunks]
    whole.go(*merge_and_cut(facts, pieces, whole.bit(), us, after))
    return whole


def finish_kernel(*refs):
    out_ref, first = refs[-1], 0
    for keep_ref, got_ref in zip(refs[:-1:2], refs[1:-1:2]):
        columns = keep_ref.shape[2]
        total = keep_ref[...].astype(F32) + got_ref[...].astype(F32)
        out_ref[:, :, first : first + columns] = total.astype(BF16)
        first += columns


def finish(*chunks, us=8, after=()):
    kinds, part, _ = chunks[0].keep.shape
    inputs = [(array, full(*array.shape)) for chunk in chunks for array in (chunk.keep, chunk.got)]
    shape = (kinds, part, sum(chunk.keep.shape[2] for chunk in chunks))
    return launch(finish_kernel, "finish", (1,), [], inputs, [(shape, BF16, full(*shape))], us=us, after=after)[0]


def join_kernel(facts_ref, value_ref, got_ref, out_ref, *, bit):
    count = value_ref.shape[1]
    first = facts_ref[bit] * count
    out_ref[:, pl.ds(first, count)] = value_ref[...]
    out_ref[:, pl.ds(count - first, count)] = got_ref[...]


class Gather:
    def __init__(self, facts, value):
        self.facts = facts
        n_dp = lax.axis_size("dp")
        self.dims = [("dp", bit) for bit in range(1, log2(n_dp))]
        self.steps = gather_steps(n_dp)
        self.kinds, self.part, self.columns = value.shape
        self.value = value[:, None]
        self.done = 0
        self.send()

    @property
    def last(self):
        return self.done == len(self.steps)

    def send(self):
        self.got = swap(self.value, CORE if self.last else self.steps[self.done])

    def step(self, us=8, after=()):
        bit = gather_fact(lax.axis_size("dp"), lax.axis_size("seq"), self.done)
        kinds, count, part, columns = self.value.shape
        spec = lambda count: pl.BlockSpec((kinds, count, part, half_of(columns)), lambda j, *_: (0, 0, 0, j))
        (self.value,) = launch(
            functools.partial(join_kernel, bit=bit),
            "join",
            (2,),
            [self.facts],
            [(self.value, spec(count)), (self.got, spec(count))],
            [((kinds, 2 * count, part, columns), BF16, spec(2 * count))],
            us=us,
            after=after,
        )
        self.done += 1
        self.send()
        return self.value

    def whole(self):
        dims = self.dims
        core = lax.axis_index("dp") & 1
        halves = []
        for which, order in enumerate((dims[::-1], dims)):
            half = jnp.where(core == which, self.value, self.got)
            half = half.reshape((self.kinds,) + (2,) * len(dims) + (self.part, self.columns))
            wanted = [1 + order[::-1].index(step) for step in dims[::-1]]
            halves.append(half.transpose([0] + wanted + [len(dims) + 1, len(dims) + 2]))
        whole = jnp.stack(halves, axis=len(dims) + 1)
        return whole.reshape(self.kinds, lax.axis_size("dp") * self.part, self.columns)


def natural_rows(facts_ref, own_ref, got_ref, kind, step, columns):
    pieces = []
    for x in range(2):
        for which in range(2):
            index = x * 2 + step if which == 0 else step * 2 + x
            own, got = own_ref[kind, index, :, columns], got_ref[kind, index, :, columns]
            pieces.append(jnp.where(facts_ref[CORE_INDEX] == which, own, got))
    return jnp.concatenate(pieces, axis=0).astype(F32)


def row_sums(value):
    total = jnp.sum(value, axis=1, keepdims=True)
    return jnp.broadcast_to(total, (total.shape[0], LANES)).T[:1, :]


def put_ff_kernel(facts_ref, own_ref, got_ref, w_ref, gain_ref, gate_up_ref, down_ref, out_ref, dgain_ref):
    step = pl.program_id(0)
    rows = lambda kind: natural_rows(facts_ref, own_ref, got_ref, kind, step, slice(0, FF))
    wide = out_ref.shape[1]
    for kind in range(3):
        count = min(OUT_WIDE, wide - kind * OUT_WIDE)
        columns = slice(FF_WIDE, FF_WIDE + count)
        part = natural_rows(facts_ref, own_ref, got_ref, kind, step, columns)
        out_ref[:, kind * OUT_WIDE : kind * OUT_WIDE + count] = part
    down_ref[...] = rows(0).T
    gate, up = rows(1), rows(2)
    gate_up_ref[:, :FF] = gate
    gate_up_ref[:, FF:] = up
    weight = w_ref[...].astype(F32)
    total = row_sums(gate * weight[:, :FF]) + row_sums(up * weight[:, FF:])
    dgain_ref[...] = total / gain_ref[...]


def put_ff(gather, w_gate_up, gain, after=()):
    kept, width = 8 * gather.part, gain.shape[0]
    half = kept // 2
    whole = full(*gather.value.shape)
    return launch(
        put_ff_kernel,
        "put_ff",
        (2,),
        [gather.facts],
        [
            (gather.value, whole),
            (gather.got, whole),
            (w_gate_up, pl.BlockSpec((half, 2 * FF), lambda j, facts: (2 * facts[SEQ_INDEX] + j, 0))),
            (gain[None], pl.BlockSpec((1, half), lambda j, facts: (0, 2 * facts[SEQ_INDEX] + j))),
        ],
        [
            ((kept, 2 * FF), F32, pl.BlockSpec((half, 2 * FF), lambda j, *_: (j, 0))),
            ((FF, kept), F32, pl.BlockSpec((FF, half), lambda j, *_: (0, j))),
            ((kept, width), F32, pl.BlockSpec((half, width), lambda j, *_: (j, 0))),
            ((1, kept), F32, pl.BlockSpec((1, half), lambda j, *_: (0, j))),
        ],
        us=8,
        after=after,
    )


def put_att_kernel(facts_ref, own_ref, got_ref, w_ref, gain_ref, qkv_ref, dgain_ref):
    qkv = natural_rows(facts_ref, own_ref, got_ref, 0, pl.program_id(0), slice(0, qkv_ref.shape[1]))
    qkv_ref[...] = qkv
    dgain_ref[...] = row_sums(qkv * w_ref[...].astype(F32)) / gain_ref[...]


def put_att(gather, w_qkv, gain, after=()):
    kept, columns = 8 * gather.part, gather.columns
    half = kept // 2
    whole = full(*gather.value.shape)
    return launch(
        put_att_kernel,
        "put_att",
        (2,),
        [gather.facts],
        [
            (gather.value, whole),
            (gather.got, whole),
            (w_qkv, pl.BlockSpec((half, columns), lambda j, facts: (2 * facts[SEQ_INDEX] + j, 0))),
            (gain[None], pl.BlockSpec((1, half), lambda j, facts: (0, 2 * facts[SEQ_INDEX] + j))),
        ],
        [
            ((kept, columns), F32, pl.BlockSpec((half, columns), lambda j, *_: (j, 0))),
            ((1, kept), F32, pl.BlockSpec((1, half), lambda j, *_: (0, j))),
        ],
        us=8,
        after=after,
    )


def place_rows(turned, places):
    count = places.shape[0]
    blocks = turned.reshape((count, turned.shape[0] // count) + turned.shape[1:])
    return jnp.zeros_like(blocks).at[places].set(blocks).reshape(turned.shape)


def shifted(value, axis, steps):
    count = lax.axis_size(axis)
    leading, last = (max(0, -steps), min(count, count - steps))
    return lax.ppermute(value, axis, [(source, source + steps) for source in range(leading, last)])


def per_device(inputs, w_qkv, w_out, w_gate_up, w_down, gain_attn, gain_mlp, doc_start, cotangent):
    n_dp, n_seq = lax.axis_size("dp"), lax.axis_size("seq")
    rows, group, width = inputs.shape
    tokens = rows * group
    slab = width // (n_dp * n_seq)
    places = [block_places(n_dp, n_seq, flavour) for flavour in range(2)]
    ordered = slab % 16 == 0
    if not ordered:
        slab = 32
    blocks = width // slab
    listed = places if ordered else [[np.arange(blocks)] * 2] * 2
    table = facts_table(n_dp, n_seq, group, listed)
    device = lax.axis_index("dp") * n_seq + lax.axis_index("seq")
    facts = lax.dynamic_index_in_dim(jnp.asarray(table), device, axis=0, keepdims=False)
    put = [places_fact(n_dp, n_seq, flavour, blocks) for flavour in range(2)]
    core = lax.axis_index("dp") & 1

    def in_order(turned, flavour):
        if ordered:
            return turned
        return place_rows(turned, jnp.where(core == 0, *places[flavour]))

    x = inputs.reshape(tokens, width)
    dy = cotangent.reshape(tokens, width)

    tails = [(row + 1) * group for row in range(rows)]
    x_rim = shifted(inputs[:, group - WINDOW :], "seq", 1).reshape(rows * WINDOW, width)
    qkv, one_turned, dy_turned = norm_matmul(x, gain_attn, w_qkv, 0, facts, put[1], slab, dy)
    kv_rim, rim_turned = norm_matmul(x_rim, gain_attn, w_qkv, width, facts, put[1], slab, after=[qkv])
    att, att_turned = attend(qkv, kv_rim, doc_start, facts, put[1], slab)
    resid, normed_two, two_turned = out_proj(att, w_out, x, gain_mlp, facts, put[1], slab)
    one_turned, rim_turned, att_turned = [in_order(turned, 1) for turned in (one_turned, rim_turned, att_turned)]
    two_turned, dy_turned = [in_order(turned, 1) for turned in (two_turned, dy_turned)]

    def feed(first, count, total=None, end=None, after=()):
        hidden, dgu, *rest = feed_forward(
            normed_two, dy, dy_turned, two_turned, w_gate_up, w_down, first, count, total, end, after
        )
        chunk = Chunk(1)
        drb_da, sends = ([], rest[:3]) if end is None else (rest[3:5], rest[:3] + rest[5:])
        chunk.between_cores(*sends)
        return hidden, dgu, chunk, drb_da or rest[3:]

    def keep_ff(chunk, hidden, dgu, out=(), after=()):
        send, keep = ff_grad(facts, chunk.bit(), dy_turned, two_turned, hidden, dgu, chunk.got, out, after)
        chunk.go(send, keep)
        return send

    count = FF_CHUNKS[0]
    hidden_one, dgu_one, one, (total,) = feed(0, count)
    token = keep_ff(one, hidden_one, dgu_one)
    hidden_two, dgu_two, two, (drb, da) = feed(count, FF_CHUNKS[1], total, (resid, gain_mlp, w_out, att_turned), after=[token])
    token = advance(facts, one, after=[da])
    token = keep_ff(two, hidden_two, dgu_two, (att_turned, drb), after=[token])
    dqkv, drim = attend_back(qkv, kv_rim, doc_start, facts, da, after=[token])
    att = Chunk(1)
    grads = (facts, one_turned, rim_turned, dqkv, drim)
    (send,) = att_grad(*grads, us=20, after=[one.got])
    att.between_cores(send)
    token = advance(facts, one, two, us=30, after=[send])
    back = rim_grad(drim, w_qkv, x_rim, gain_attn, after=[token])
    back_got = shifted(back, "seq", -1)
    send, keep = att_grad(*grads, att.bit(), att.got[0], after=[back])
    att.go(send[None], keep[None])
    token = advance(facts, one, two, us=1, after=[send])
    grad_inputs = input_grad(dqkv, w_qkv, x, gain_attn, drb, back_got, tails, us=15, after=[token])
    token = advance(facts, att, two, after=[grad_inputs, one.got])
    while not (one.last and two.last):
        token = advance(facts, *(chunk for chunk in (one, two) if not chunk.last), after=[token])
    outputs = ff_out([hidden_one, hidden_two], w_down, resid, us=8, after=[token])
    token = advance(facts, att, after=[outputs])
    gather_ff = Gather(facts, finish(one, two, after=[token]))
    token = gather_ff.value
    while not att.last:
        token = advance(facts, att, after=[token])
    token = gather_ff.step(after=[token])
    gather = Gather(facts, finish(att, after=[token]))
    if ordered and n_dp == 8:
        token = gather.step(us=1, after=[gather.value])
        token = gather_ff.step(after=[token])
        token = gather.step(us=24, after=[token])
        total_gate_up, turned_down, total_out, gain_two = put_ff(gather_ff, w_gate_up, gain_mlp, after=[token])
        total_down = turned_down.T
        total_qkv, gain_one = put_att(gather, w_qkv, gain_attn, after=[total_gate_up])
        gain_one, gain_two = gain_one[0], gain_two[0]
    else:
        for both in (gather_ff, gather):
            while not both.last:
                both.step()
        total_ff = gather_ff.whole()
        total_qkv = gather.whole()[0].astype(F32)
        total_down, total_gate, total_up = [total_ff[kind, :, :FF] for kind in range(3)]
        total_down = total_down.astype(F32)
        total_gate_up = jnp.concatenate([total_gate, total_up], axis=1).astype(F32)
        outs = [total_ff[kind, :, FF_WIDE:] for kind in range(3)]
        total_out = jnp.concatenate(outs, axis=1)[:, :width].astype(F32)
        kept = total_qkv.shape[0]
        first_row = lax.axis_index("seq") * kept

        def gain_total(total, weight, gain):
            mine = lax.dynamic_slice_in_dim(weight, first_row, kept, axis=0).astype(F32)
            return jnp.sum(total * mine, axis=1) / lax.dynamic_slice_in_dim(gain, first_row, kept)

        gain_one = gain_total(total_qkv, w_qkv, gain_attn)
        gain_two = gain_total(total_gate_up, w_gate_up, gain_mlp)

    return (
        outputs.reshape(rows, group, width),
        grad_inputs.reshape(rows, group, width),
        total_qkv,
        total_out,
        total_gate_up,
        total_down,
        gain_one,
        gain_two,
    )


def solution(mesh):
    in_specs = (
        P("dp", "seq", None),
        P(),
        P(),
        P(),
        P(),
        P(),
        P(),
        P("dp", "seq"),
        P("dp", "seq", None),
    )
    out_specs = (
        P("dp", "seq", None),
        P("dp", "seq", None),
        P("seq", None),
        P("seq", None),
        P("seq", None),
        P("seq", None),
        P("seq"),
        P("seq"),
    )
    return jax.shard_map(
        per_device, mesh=mesh, in_specs=in_specs, out_specs=out_specs, check_vma=False
    )
```

```python
import functools
import math

import jax
import jax.numpy as jnp
import numpy as np
from jax import lax
from jax.experimental import pallas as pl
from jax.experimental.pallas import tpu as pltpu
from jax.sharding import PartitionSpec as P

HEADS = 16
HEAD_DIM = 64
FF = 2752
WINDOW = 64
LANES = 128
PAIRS = 2
FF_TILE = 256
FF_TILES = -(-FF // FF_TILE)
FF_CHUNKS = (7, 4)
FF_WIDE = FF_TILES * FF_TILE
STEP = 256
epsilon = 1e-05
masked_value = -1e30
F32 = jnp.float32
BF16 = jnp.bfloat16
VMEM_LIMIT = 64 * 1024 * 1024 - 64 * 1024
PER_US = 1.1e9


def dot(left, right, left_dim=1, right_dim=0):
    return lax.dot_general(
        left, right, (((left_dim,), (right_dim,)), ((), ())), preferred_element_type=F32
    )


def launch(kernel, name, grid, scalars, inputs, outputs, scratch=(), us=8, after=()):
    known = len(scalars) + len(inputs)

    def body(*refs):
        kernel(*refs[:known], *refs[known + len(after) :])

    specs = [spec for _, spec in inputs] + [pl.BlockSpec(memory_space=pl.ANY)] * len(after)
    shapes = [pltpu.HBM(shape, kind) for shape, kind, _ in outputs]
    moved = sum(array.size * array.dtype.itemsize for array, _ in inputs)
    moved += sum(math.prod(shape) * np.dtype(kind).itemsize for shape, kind, _ in outputs)
    return pl.pallas_call(
        body,
        grid_spec=pltpu.PrefetchScalarGridSpec(
            num_scalar_prefetch=len(scalars),
            grid=grid,
            in_specs=specs,
            out_specs=[spec for _, _, spec in outputs],
            scratch_shapes=list(scratch),
        ),
        out_shape=shapes,
        compiler_params=pltpu.CompilerParams(vmem_limit_bytes=VMEM_LIMIT),
        cost_estimate=pl.CostEstimate(flops=int(us * PER_US), bytes_accessed=int(moved / 100), transcendentals=0),
        name=name,
    )(*scalars, *[array for array, _ in inputs], *after)


def full(*shape):
    return pl.BlockSpec(shape, lambda *_: (0,) * len(shape))


CORE_INDEX, SEQ_INDEX, POSITION = range(3)


def store_slabs(out_ref, value, facts_ref, first, slab, columns=slice(None)):
    for k in range(value.shape[0] // slab):
        row = pl.multiple_of(facts_ref[first + k] * slab, slab)
        out_ref[pl.ds(row, slab), columns] = value[k * slab : (k + 1) * slab]


def side_by_side(ref):
    return jnp.concatenate([ref[k] for k in range(ref.shape[0])], axis=1)


def put_blocks(ref, value, rows=slice(None)):
    for k in range(ref.shape[0]):
        ref[k, rows, :] = value[:, k * LANES : (k + 1) * LANES]

def two_heads(value, low):
    zero = jnp.zeros_like(value)
    return jnp.concatenate([jnp.where(low, value, zero), jnp.where(low, zero, value)], axis=0)


def one_of_two(value, size):
    feature = lax.broadcasted_iota(jnp.int32, (LANES, size), 0)
    return jnp.where(feature < HEAD_DIM, value[:, :size], value[:, size:])


class Spans:
    def __init__(self, rows, group):
        self.rows, self.group = rows, group
        self.size = min(128, group)
        self.blocks = group // self.size
        self.count = rows * self.blocks
        self.window = self.size + WINDOW

    def queries(self, at):
        return slice(at * self.size, (at + 1) * self.size)

    def keys(self, own_ref, rim_ref, pair, at):
        row, block = divmod(at, self.blocks)
        start = at * self.size
        if block == 0:
            rim = rim_ref[pair, row * WINDOW : (row + 1) * WINDOW, :]
            return jnp.concatenate([rim, own_ref[pair, start : start + self.size, :]], axis=0)
        return own_ref[pair, start - WINDOW : start + self.size, :]

    def fill_bias(self, bias_ref, starts_ref, facts_ref):
        size = self.size
        key = lax.broadcasted_iota(jnp.int32, (self.window, size), 0) - WINDOW
        query = lax.broadcasted_iota(jnp.int32, (self.window, size), 1)
        near = (key <= query) & (query - key <= WINDOW)
        for at in range(self.count):
            row, block = divmod(at, self.blocks)
            begin = starts_ref[row : row + 1, block * size : (block + 1) * size]
            begin = begin - facts_ref[POSITION] - block * size
            bias = jnp.where(near & (key >= begin), 0.0, masked_value).astype(F32)
            bias_ref[at, :, :size] = bias
            bias_ref[at, :, size:] = bias

    def scratch(self, kind):
        return pltpu.VMEM((self.count, self.window, 2 * self.size), kind)


def softmax(scores):
    weights = jnp.exp(scores - jnp.max(scores, axis=0, keepdims=True))
    return weights * (1.0 / jnp.sum(weights, axis=0, keepdims=True))


def attend_kernel(facts_ref, starts_ref, q_ref, k_ref, v_ref, kr_ref, vr_ref,
                  att_ref, attT_ref, bias_ref, score_ref, probs_ref, *, spans, slab, put, pairs):
    step = pl.program_id(0)
    size, count = spans.size, spans.count

    @pl.when(step == 0)
    def _():
        spans.fill_bias(bias_ref, starts_ref, facts_ref)

    low = lax.broadcasted_iota(jnp.int32, (size, LANES), 1) < HEAD_DIM
    for pair in range(pairs):
        for at in range(count):
            queries = q_ref[pair, spans.queries(at), :] * jnp.asarray(HEAD_DIM ** (-0.5), BF16)
            keys = spans.keys(k_ref, kr_ref, pair, at)
            score_ref[at] = dot(keys, two_heads(queries, low), 1, 1)
        for at in range(count):
            probs_ref[at] = softmax(score_ref[at] + bias_ref[at]).astype(BF16)
        for at in range(count):
            values = spans.keys(v_ref, vr_ref, pair, at)
            mixed = one_of_two(dot(values, probs_ref[at], 0, 0), size)
            att_ref[pair, spans.queries(at), :] = mixed.T.astype(BF16)
            first = put + (step * pairs + pair) * (LANES // slab)
            store_slabs(attT_ref, mixed.astype(BF16), facts_ref, first, slab, spans.queries(at))


def attend(qkv, kv_rim, doc_start, facts, put, slab, after=()):
    rows, group = doc_start.shape
    all_pairs, tokens = qkv.shape[0] // 3, qkv.shape[1]
    rim = kv_rim.shape[1]
    spans = Spans(rows, group)
    steps = all_pairs // PAIRS
    own = lambda kind: pl.BlockSpec((PAIRS, tokens, LANES), lambda j, *_: (kind * steps + j, 0, 0))
    edge = lambda kind: pl.BlockSpec((PAIRS, rim, LANES), lambda j, *_: (kind * steps + j, 0, 0))
    width = all_pairs * LANES
    return launch(
        functools.partial(attend_kernel, spans=spans, slab=slab, put=put, pairs=PAIRS),
        "attend",
        (steps,),
        [facts],
        [
            (doc_start, full(rows, group)),
            (qkv, own(0)),
            (qkv, own(1)),
            (qkv, own(2)),
            (kv_rim, edge(0)),
            (kv_rim, edge(1)),
        ],
        [
            ((all_pairs, tokens, LANES), BF16, own(0)),
            ((width, tokens), BF16, full(width, tokens)),
        ],
        [spans.scratch(F32), spans.scratch(F32), spans.scratch(BF16)],
        us=8,
        after=after,
    )


def attend_back_kernel(facts_ref, starts_ref, q_ref, k_ref, v_ref, kr_ref, vr_ref, da_ref,
                       dqkv_ref, drim_ref,
                       bias_ref, score_ref, grad_ref, probs_ref, dscore_ref, *, spans, pairs):
    size, count = spans.size, spans.count

    @pl.when(pl.program_id(0) == 0)
    def _():
        spans.fill_bias(bias_ref, starts_ref, facts_ref)

    low = lax.broadcasted_iota(jnp.int32, (size, LANES), 1) < HEAD_DIM
    scale = HEAD_DIM ** (-0.5)

    def scaled_queries(pair, at):
        return two_heads(q_ref[pair, spans.queries(at), :] * jnp.asarray(scale, BF16), low)

    for pair in range(pairs):
        for at in range(count):
            score_ref[at] = dot(spans.keys(k_ref, kr_ref, pair, at), scaled_queries(pair, at), 1, 1)
            grads = two_heads(da_ref[pair, spans.queries(at), :], low)
            grad_ref[at] = dot(spans.keys(v_ref, vr_ref, pair, at), grads, 1, 1)
        for at in range(count):
            probs = softmax(score_ref[at] + bias_ref[at])
            probs_ref[at] = probs.astype(BF16)
            part = probs * grad_ref[at]
            dscore_ref[at] = (part - probs * jnp.sum(part, axis=0, keepdims=True)).astype(BF16)
        late = [None, None]
        for at in range(count):
            here = spans.queries(at)
            row, block = divmod(at, spans.blocks)
            dscores = dscore_ref[at]
            grads = two_heads(da_ref[pair, here, :], low)
            dk = dot(dscores, scaled_queries(pair, at))
            dv = dot(probs_ref[at], grads)
            dq = one_of_two(dot(spans.keys(k_ref, kr_ref, pair, at), dscores, 0, 0), size) * scale
            dqkv_ref[0, pair, here, :] = dq.T.astype(BF16)
            start = at * size
            for kind, grad in ((0, dk), (1, dv)):
                out_ref, rim_ref = dqkv_ref.at[kind + 1], drim_ref.at[kind]
                early = grad[:WINDOW]
                if block == 0:
                    rim_ref[pair, row * WINDOW : (row + 1) * WINDOW, :] = early.astype(BF16)
                else:
                    out_ref[pair, start - WINDOW : start, :] = (late[kind] + early).astype(BF16)
                if size > WINDOW:
                    out_ref[pair, start : start + size - WINDOW, :] = grad[WINDOW:size].astype(BF16)
                late[kind] = grad[size:]
                if block == spans.blocks - 1:
                    out_ref[pair, start + size - WINDOW : start + size, :] = late[kind].astype(BF16)


def attend_back(qkv, kv_rim, doc_start, facts, grad_att, after=()):
    rows, group = doc_start.shape
    all_pairs, tokens = qkv.shape[0] // 3, qkv.shape[1]
    rim = kv_rim.shape[1]
    spans = Spans(rows, group)
    steps = all_pairs // PAIRS
    own = lambda kind: pl.BlockSpec((PAIRS, tokens, LANES), lambda j, *_: (kind * steps + j, 0, 0))
    edge = lambda kind: pl.BlockSpec((PAIRS, rim, LANES), lambda j, *_: (kind * steps + j, 0, 0))
    return launch(
        functools.partial(attend_back_kernel, spans=spans, pairs=PAIRS),
        "attend_back",
        (steps,),
        [facts],
        [
            (doc_start, full(rows, group)),
            (qkv, own(0)),
            (qkv, own(1)),
            (qkv, own(2)),
            (kv_rim, edge(0)),
            (kv_rim, edge(1)),
            (grad_att, own(0)),
        ],
        [
            ((3, all_pairs, tokens, LANES), BF16, pl.BlockSpec((3, PAIRS, tokens, LANES), lambda j, *_: (0, j, 0, 0))),
            ((2, all_pairs, rim, LANES), BF16, pl.BlockSpec((2, PAIRS, rim, LANES), lambda j, *_: (0, j, 0, 0))),
        ],
        [spans.scratch(kind) for kind in (F32, F32, F32, BF16, BF16)],
        us=8,
        after=after,
    )


def norm_matmul_kernel(facts_ref, x_ref, gain_ref, w_ref, *refs, slab, put, step, beside):
    if beside:
        other_ref, out_ref, normedT_ref, otherT_ref, normed_ref = refs
    else:
        out_ref, normedT_ref, normed_ref = refs

    @pl.when(pl.program_id(0) == 0)
    def _():
        for at in range(0, x_ref.shape[0], step):
            x = x_ref[at : at + step, :].astype(F32)
            inv = lax.rsqrt(jnp.mean(x * x, axis=-1, keepdims=True) + epsilon)
            normed = (x * inv * gain_ref[...]).astype(BF16)
            normed_ref[at : at + step, :] = normed
            store_slabs(normedT_ref, normed.T, facts_ref, put, slab, slice(at, at + step))

    put_blocks(out_ref, dot(normed_ref[...], w_ref[...]).astype(BF16))
    if beside:
        store_slabs(otherT_ref, other_ref[...].T, facts_ref, put, slab)


def norm_matmul(x, gain, weight, first_column, facts, put, slab, beside=None, after=()):
    tokens, width = x.shape
    columns = weight.shape[1] - first_column
    tile = 1024 if beside is None else 768
    skip, wide, steps = first_column // tile, tile // LANES, columns // tile
    part = tokens // steps
    others, turned = [], []
    if beside is not None:
        others = [(beside, pl.BlockSpec((part, width), lambda j, *_: (j, 0)))]
        turned = [((width, tokens), BF16, pl.BlockSpec((width, part), lambda j, *_: (0, j)))]
    return launch(
        functools.partial(norm_matmul_kernel, slab=slab, put=put, step=min(STEP, tokens), beside=beside is not None),
        "norm_matmul",
        (steps,),
        [facts],
        [
            (x, full(tokens, width)),
            (gain[None], full(1, width)),
            (weight, pl.BlockSpec((width, tile), lambda j, *_: (0, skip + j))),
        ]
        + others,
        [
            ((columns // LANES, tokens, LANES), BF16, pl.BlockSpec((wide, tokens, LANES), lambda j, *_: (j, 0, 0))),
            ((width, tokens), BF16, full(width, tokens)),
        ]
        + turned,
        [pltpu.VMEM((tokens, width), BF16)],
        us=8,
        after=after,
    )


def out_proj_kernel(facts_ref, att_ref, w_ref, x_ref, gain_ref, resid_ref, normed_ref, normedT_ref, *, slab, put):
    resid = x_ref[...].astype(F32) + dot(side_by_side(att_ref), w_ref[...])
    resid_ref[...] = resid.astype(BF16)
    inv = lax.rsqrt(jnp.mean(resid * resid, axis=-1, keepdims=True) + epsilon)
    normed = (resid * inv * gain_ref[...]).astype(BF16)
    normed_ref[...] = normed
    store_slabs(normedT_ref, normed.T, facts_ref, put, slab)


def out_proj(att, w_out, x, gain, facts, put, slab, after=()):
    tokens, width = x.shape
    pairs = att.shape[0]
    step = 2 * STEP
    rows = pl.BlockSpec((step, width), lambda m, *_: (m, 0))
    return launch(
        functools.partial(out_proj_kernel, slab=slab, put=put),
        "out_proj",
        (tokens // step,),
        [facts],
        [
            (att, pl.BlockSpec((pairs, step, LANES), lambda m, *_: (0, m, 0))),
            (w_out, full(width, width)),
            (x, rows),
            (gain[None], full(1, width)),
        ],
        [
            ((tokens, width), BF16, rows),
            ((tokens, width), BF16, rows),
            ((width, tokens), BF16, pl.BlockSpec((width, step), lambda m, *_: (0, m))),
        ],
        us=8,
        after=after,
    )


def ff_kernel(*refs, first, given, ends):
    normed_ref, dy_ref, dyT_ref, normedT_ref, wg_ref, wu0_ref, wu1_ref, wu2_ref, wd_ref = refs[:9]
    rest = list(refs[9:])
    total_in = rest.pop(0) if given else None
    if ends:
        resid_ref, gain_ref, w_out_ref, attT_ref = rest[:4]
        rest = rest[4:]
    hidden_ref, dgu_ref, send_down, send_gate, send_up, *totals, acc_ref = rest
    tile = pl.program_id(0)
    tokens = normed_ref.shape[0]

    @pl.when(tile == 0)
    def _():
        acc_ref[...] = total_in[...] if given else jnp.zeros_like(acc_ref)

    half = FF % LANES
    w_both = jnp.concatenate([wg_ref[...], wu0_ref[:, half:], wu1_ref[...], wu2_ref[:, :half]], axis=1)
    limit = FF - (tile + first) * FF_TILE
    inside = lax.broadcasted_iota(jnp.int32, (STEP, FF_TILE), 1) < limit

    def products(at):
        here = slice(at, at + STEP)
        both = dot(normed_ref[here, :], w_both)
        return both[:, :FF_TILE], both[:, FF_TILE:], dot(dy_ref[here, :], wd_ref[...], 1, 1)

    def act(at, gate, up, back):
        here = slice(at, at + STEP)
        sigma = 1.0 / (1.0 + jnp.exp(-gate))
        silu = gate * sigma
        hidden_ref[here, :] = jnp.where(inside, silu * up, 0.0).astype(BF16)
        dgate = back * up * (sigma * (1.0 + gate * (1.0 - sigma)))
        dgu_ref[0, here, :] = jnp.where(inside, dgate, 0.0).astype(BF16)
        dgu_ref[1, here, :] = jnp.where(inside, back * silu, 0.0).astype(BF16)

    def norm_grad(at):
        here = slice(at, at + STEP)
        grads = jnp.concatenate([dgu_ref[0, here, :], dgu_ref[1, here, :]], axis=1)
        acc_ref[here, :] += dot(grads, w_both, 1, 1)

    held = products(0)
    for at in range(0, tokens, STEP):
        ahead = products(at + STEP) if at + STEP < tokens else None
        act(at, *held)
        norm_grad(at)
        held = ahead
    send_down[...] = dot(dyT_ref[...], hidden_ref[...]).astype(BF16)
    both = dot(normedT_ref[...], jnp.concatenate([dgu_ref[0], dgu_ref[1]], axis=1)).astype(BF16)
    send_gate[...] = both[:, :FF_TILE]
    send_up[...] = both[:, FF_TILE:]

    @pl.when(tile == pl.num_programs(0) - 1)
    def _():
        if not ends:
            totals[0][...] = acc_ref[...]
            return
        drb_ref, da_ref, send_out = totals
        for at in range(0, tokens, STEP):
            here = slice(at, at + STEP)
            grad = norm_back(acc_ref[here, :], resid_ref[here, :].astype(F32), gain_ref[...])
            branch = (dy_ref[here, :].astype(F32) + grad).astype(BF16)
            put_blocks(drb_ref, branch, here)
            put_blocks(da_ref, dot(branch, w_out_ref[...], 1, 1).astype(BF16), here)
        send_out[...] = dot(attT_ref[...], side_by_side(drb_ref)).astype(BF16)


def feed_forward(normed, dy, dy_turned, normed_turned, w_gate_up, w_down, first, count, total=None, end=None, after=()):
    tokens, width = normed.shape
    wide = count * FF_TILE
    last = w_gate_up.shape[1] // LANES - 1
    skip = FF // LANES + first * (FF_TILE // LANES)
    up = lambda k: pl.BlockSpec(
        (width, LANES), lambda j: (0, jnp.minimum(skip + k + j * (FF_TILE // LANES), last))
    )
    other_half = full(width // 2, tokens)
    given = [] if total is None else [(total, full(tokens, width))]
    ending, results = [], [((tokens, width), F32, full(tokens, width))]
    if end is not None:
        resid, gain, w_out, att_turned = end
        ending = [(resid, full(tokens, width)), (gain[None], full(1, width)), (w_out, full(width, width))]
        ending.append((att_turned, other_half))
        blocks = (width // LANES, tokens, LANES)
        results = [(blocks, BF16, full(*blocks))] * 2
        results.append(((width // 2, width), BF16, full(width // 2, width)))
    return launch(
        functools.partial(ff_kernel, first=first, given=len(given), ends=end is not None),
        "feed_forward",
        (count,),
        [],
        [
            (normed, full(tokens, width)),
            (dy, full(tokens, width)),
            (dy_turned, other_half),
            (normed_turned, other_half),
            (w_gate_up, pl.BlockSpec((width, FF_TILE), lambda j: (0, first + j))),
            (w_gate_up, up(0)),
            (w_gate_up, up(1)),
            (w_gate_up, up(2)),
            (w_down.T, pl.BlockSpec((FF_TILE, width), lambda j: (first + j, 0))),
        ]
        + given
        + ending,
        [
            ((tokens, wide), BF16, pl.BlockSpec((tokens, FF_TILE), lambda j: (0, j))),
            ((2, tokens, wide), BF16, pl.BlockSpec((2, tokens, FF_TILE), lambda j: (0, 0, j))),
        ]
        + [((width // 2, wide), BF16, pl.BlockSpec((width // 2, FF_TILE), lambda j: (0, j)))] * 3
        + results,
        [pltpu.VMEM((tokens, width), F32)],
        us=8,
        after=after,
    )


OUT_WIDE = 3 * LANES


def ff_grad_kernel(facts_ref, dyT_ref, normedT_ref, hidden_ref, dgu_ref, got_down, got_gate, got_up, *rest, bit, tiles):
    send_ref, keep_ref = rest[-2:]
    part = send_ref.shape[1]
    own = facts_ref[bit]
    step = pl.program_id(0)

    def put(kind, left_ref, right, got_ref, at, columns):
        for out_ref, index in ((send_ref, 1 - own), (keep_ref, own)):
            rows = pl.ds(pl.multiple_of(index * part, part), part)
            total = dot(left_ref[rows, :], right) + got_ref[rows, at : at + columns].astype(F32)
            out_ref[kind, :, :columns] = total.astype(BF16)

    @pl.when(step < tiles)
    def _():
        columns = hidden_ref.shape[1]
        put(0, dyT_ref, hidden_ref[...], got_down, 0, columns)
        put(1, normedT_ref, dgu_ref[0], got_gate, 0, columns)
        put(2, normedT_ref, dgu_ref[1], got_up, 0, columns)

    if len(rest) == 2:
        return
    attT_ref, drb_ref, got_out = rest[:3]
    each = hidden_ref.shape[1] // LANES
    for late in range(-(-OUT_WIDE // (each * LANES))):

        @pl.when(step == tiles + late)
        def _():
            send_ref[...] = jnp.zeros_like(send_ref)
            keep_ref[...] = jnp.zeros_like(keep_ref)
            for kind in range(3):
                blocks = range(kind * 3 + each * late, kind * 3 + min(3, each * (late + 1)))
                blocks = [block for block in blocks if block < drb_ref.shape[0]]
                if blocks:
                    right = jnp.concatenate([drb_ref[block] for block in blocks], axis=1)
                    put(kind, attT_ref, right, got_out, blocks[0] * LANES, len(blocks) * LANES)


def ff_grad(facts, bit, dy_turned, normed_turned, hidden, dgu, got, out=(), after=()):
    width, tokens = dy_turned.shape
    wide = hidden.shape[1]
    tile = 512 if wide % 512 == 0 else FF_TILE
    tiles = wide // tile
    own_half = pl.BlockSpec((width // 2, tokens), lambda j, *_: (1, 0))
    at = lambda j: jnp.minimum(j, tiles - 1)
    extra, columns, steps = [], wide, tiles
    if out:
        att_turned, drb = out
        extra = [(att_turned, own_half), (drb, full(*drb.shape)), (got[3], full(*got[3].shape))]
        columns, steps = wide + OUT_WIDE, tiles + -(-OUT_WIDE // tile)
    part = ((3, width // 4, columns), BF16, pl.BlockSpec((3, width // 4, tile), lambda j, *_: (0, 0, j)))
    return launch(
        functools.partial(ff_grad_kernel, bit=bit, tiles=tiles),
        "ff_grad",
        (steps,),
        [facts],
        [
            (dy_turned, own_half),
            (normed_turned, own_half),
            (hidden, pl.BlockSpec((tokens, tile), lambda j, *_: (0, at(j)))),
            (dgu, pl.BlockSpec((2, tokens, tile), lambda j, *_: (0, 0, at(j)))),
        ]
        + [(value, pl.BlockSpec((width // 2, tile), lambda j, *_: (0, at(j)))) for value in got[:3]]
        + extra,
        [part, part],
        us=8,
        after=after,
    )


def norm_back(grad, values, gain):
    inv = lax.rsqrt(jnp.mean(values * values, axis=-1, keepdims=True) + epsilon)
    scaled = grad * gain
    return inv * scaled - values * (inv * inv * inv) * jnp.mean(scaled * values, axis=-1, keepdims=True)


def ff_out_kernel(*refs):
    wd_ref, resid_ref, out_ref = refs[-3:]
    total, first = resid_ref[...].astype(F32), 0
    for hidden_ref in refs[:-3]:
        count = min(hidden_ref.shape[1], FF - first)
        total += dot(hidden_ref[:, :count], wd_ref[first : first + count, :])
        first += count
    out_ref[...] = total.astype(BF16)


def ff_out(hiddens, w_down, resid, us, after=()):
    tokens, width = resid.shape
    rows = lambda columns: pl.BlockSpec((STEP, columns), lambda m: (m, 0))
    return launch(
        ff_out_kernel,
        "ff_out",
        (tokens // STEP,),
        [],
        [(hidden, rows(hidden.shape[1])) for hidden in hiddens]
        + [(w_down.T, full(FF, width)), (resid, rows(width))],
        [((tokens, width), BF16, rows(width))],
        us=us,
        after=after,
    )[0]


def att_grad_kernel(facts_ref, *refs, bit):
    split = bit is not None
    oneT_ref, rimT_ref, dqkv_ref, drim_ref = refs[:4]
    kind = pl.program_id(0)

    def put(total):
        if split:
            got_ref, send_ref, keep_ref = refs[-3:]
            part = send_ref.shape[0]
            own = facts_ref[bit]
            for out_ref, half in ((send_ref, 1 - own), (keep_ref, own)):
                rows = pl.ds(pl.multiple_of(half * part, part), part)
                out_ref[...] = (total(rows) + got_ref[rows, :].astype(F32)).astype(BF16)
        else:
            refs[-1][...] = total(slice(None)).astype(BF16)

    @pl.when(kind == 0)
    def _():
        right = side_by_side(dqkv_ref)
        put(lambda rows: dot(oneT_ref[rows, :], right))

    @pl.when(kind > 0)
    def _():
        right, rim = side_by_side(dqkv_ref), side_by_side(drim_ref)
        put(lambda rows: dot(oneT_ref[rows, :], right) + dot(rimT_ref[rows, :], rim))


def att_grad(facts, one_turned, rim_turned, dqkv, drim, bit=None, got=None, us=8, after=()):
    width, tokens = one_turned.shape
    rim = rim_turned.shape[1]
    split = got is not None
    half = 1 if split else 0
    inputs = [
        (turned, pl.BlockSpec((width // 2, turned.shape[1]), lambda j, *_: (half, 0)))
        for turned in (one_turned, rim_turned)
    ]
    blocks = width // LANES
    inputs += [
        (dqkv, pl.BlockSpec((None, blocks, tokens, LANES), lambda j, *_: (j, 0, 0, 0))),
        (drim, pl.BlockSpec((None, blocks, rim, LANES), lambda j, *_: (jnp.maximum(j - 1, 0), 0, 0, 0))),
    ]
    columns = 3 * width
    tile = pl.BlockSpec((width // 2, width), lambda j, *_: (0, j))
    if split:
        inputs.append((got, tile))
        part = ((width // 4, columns), BF16, pl.BlockSpec((width // 4, width), lambda j, *_: (0, j)))
        outputs = [part, part]
    else:
        outputs = [((width // 2, columns), BF16, tile)]
    return launch(
        functools.partial(att_grad_kernel, bit=bit),
        "att_grad",
        (3,),
        [facts],
        inputs,
        outputs,
        us=us,
        after=after,
    )


def input_grad_kernel(dqkv_ref, w_ref, x_ref, gain_ref, drb_ref, back_ref, out_ref, *, tails):
    step = out_ref.shape[0]
    grads = jnp.concatenate([side_by_side(dqkv_ref.at[kind]) for kind in range(3)], axis=1)
    grad = norm_back(dot(grads, w_ref[...], 1, 1), x_ref[...].astype(F32), gain_ref[...])
    out_ref[...] = grad + side_by_side(drb_ref).astype(F32)
    for row, end in enumerate(tails):
        block, last = divmod(end - WINDOW, step)

        @pl.when(pl.program_id(0) == block)
        def _():
            out_ref[last : last + WINDOW, :] += back_ref[row * WINDOW : (row + 1) * WINDOW, :].astype(F32)


def input_grad(dqkv, w_qkv, x, gain, drb, back, tails, us, after=()):
    tokens, width = x.shape
    blocks = width // LANES
    rows = pl.BlockSpec((STEP, width), lambda m: (m, 0))
    return launch(
        functools.partial(input_grad_kernel, tails=tails),
        "input_grad",
        (tokens // STEP,),
        [],
        [
            (dqkv, pl.BlockSpec((3, blocks, STEP, LANES), lambda m: (0, 0, m, 0))),
            (w_qkv, full(*w_qkv.shape)),
            (x, rows),
            (gain[None], full(1, width)),
            (drb, pl.BlockSpec((blocks, STEP, LANES), lambda m: (0, m, 0))),
            (back, full(*back.shape)),
        ],
        [((tokens, width), F32, rows)],
        us=us,
        after=after,
    )[0]


def rim_grad_kernel(drim_ref, wk_ref, wv_ref, x_ref, gain_ref, out_ref):
    grad = dot(side_by_side(drim_ref.at[0]), wk_ref[...], 1, 1)
    grad += dot(side_by_side(drim_ref.at[1]), wv_ref[...], 1, 1)
    out_ref[...] = norm_back(grad, x_ref[...].astype(F32), gain_ref[...]).astype(BF16)


def rim_grad(drim, w_qkv, x, gain, after=()):
    rim, width = x.shape
    part = lambda k: pl.BlockSpec((width, width), lambda j: (0, k))
    return launch(
        rim_grad_kernel,
        "rim_grad",
        (1,),
        [],
        [
            (drim, full(*drim.shape)),
            (w_qkv, part(1)),
            (w_qkv, part(2)),
            (x, full(rim, width)),
            (gain[None], full(1, width)),
        ],
        [((rim, width), BF16, full(rim, width))],
        us=8,
        after=after,
    )[0]


def half_of(columns):
    return -(-columns // (2 * LANES)) * LANES


def add_kernel(facts_ref, *refs, bits):
    count = len(bits)
    for k, bit in enumerate(bits):
        keep_ref, got_ref = refs[2 * k : 2 * k + 2]
        outs = refs[2 * count + 2 * k : 2 * count + 2 * k + 2]
        for out_ref, index in zip(outs, (1 - facts_ref[bit], facts_ref[bit])):
            out_ref[...] = (keep_ref[:, index].astype(F32) + got_ref[:, index].astype(F32)).astype(BF16)


def add_and_cut(facts, items, us, after=()):
    inputs, outputs = [], []
    for keep, got, _ in items:
        kinds, rows, columns = keep.shape
        cut = lambda value: value.reshape(kinds, 2, rows // 2, columns)
        spec = pl.BlockSpec((kinds, 2, rows // 2, half_of(columns)), lambda j, *_: (0, 0, 0, j))
        part = pl.BlockSpec((kinds, rows // 2, half_of(columns)), lambda j, *_: (0, 0, j))
        inputs += [(cut(keep), spec), (cut(got), spec)]
        outputs += [((kinds, rows // 2, columns), BF16, part)] * 2
    kernel = functools.partial(add_kernel, bits=[bit for _, _, bit in items])
    parts = launch(kernel, "add_and_cut", (2,), [facts], inputs, outputs, us=us, after=after)
    return [(parts[2 * k], parts[2 * k + 1]) for k in range(len(items))]


def merge_kernel(facts_ref, *refs, bit):
    *parts, send_ref, keep_ref = refs
    for out_ref, index in ((send_ref, 1 - facts_ref[bit]), (keep_ref, facts_ref[bit])):
        first = 0
        for keep, got in zip(parts[::2], parts[1::2]):
            columns = keep.shape[3]
            total = keep[:, index].astype(F32) + got[:, index].astype(F32)
            out_ref[:, :, first : first + columns] = total.astype(BF16)
            first += columns


def merge_and_cut(facts, pieces, bit, us, after=()):
    inputs = []
    for keep, got in pieces:
        kinds, rows, columns = keep.shape
        spec = pl.BlockSpec((1, 2, rows // 2, columns), lambda j, *_: (j, 0, 0, 0))
        inputs += [(value.reshape(kinds, 2, rows // 2, columns), spec) for value in (keep, got)]
    columns = sum(keep.shape[2] for keep, _ in pieces)
    part = ((kinds, rows // 2, columns), BF16, pl.BlockSpec((1, rows // 2, columns), lambda j, *_: (j, 0, 0)))
    kernel = functools.partial(merge_kernel, bit=bit)
    return launch(kernel, "merge_and_cut", (kinds,), [facts], inputs, [part, part], us=us, after=after)


def log2(count):
    return count.bit_length() - 1


def stage_orders(n_dp, n_seq, flavour):
    dp = [("dp", bit) for bit in range(1, log2(n_dp))]
    if flavour:
        dp = dp[::-1]
    seq = [("seq", bit) for bit in range(log2(n_seq))]
    return dp + seq, seq[:1] + dp + seq[1:]


def row_bits(n_dp, n_seq):
    return [("seq", bit) for bit in reversed(range(log2(n_seq)))] + [
        ("dp", bit) for bit in reversed(range(log2(n_dp)))
    ]


def block_places(n_dp, n_seq, flavour):
    bits, orders = row_bits(n_dp, n_seq), stage_orders(n_dp, n_seq, flavour)
    count = n_dp * n_seq
    tables = []
    for core in range(2):
        table = []
        for block in range(count):
            value = {step: (block >> (len(bits) - 1 - k)) & 1 for k, step in enumerate(bits)}
            owner = value[("dp", 0)]
            place = 0
            for step in orders[owner]:
                place = place * 2 + value[step]
            table.append(place + (count // 2 if owner == core else 0))
        tables.append(np.array(table, np.int32))
    return tables


def swap_pairs(n_dp, n_seq, steps):
    pairs = []
    for d in range(n_dp):
        for s in range(n_seq):
            axis, bit = steps[d % 2]
            there = (d ^ (1 << bit), s) if axis == "dp" else (d, s ^ (1 << bit))
            pairs.append((d * n_seq + s, there[0] * n_seq + there[1]))
    return pairs


def swap(value, steps):
    n_dp, n_seq = lax.axis_size("dp"), lax.axis_size("seq")
    return lax.ppermute(value, ("dp", "seq"), swap_pairs(n_dp, n_seq, steps))


def gather_steps(n_dp):
    dims = [("dp", bit) for bit in range(1, log2(n_dp))]
    return list(zip(dims[::-1], dims))


def stage_fact(n_dp, n_seq, flavour, stage):
    return 3 + flavour * (log2(n_dp * n_seq) - 1) + stage


def gather_fact(n_dp, n_seq, step):
    return 3 + 2 * (log2(n_dp * n_seq) - 1) + step


def places_fact(n_dp, n_seq, flavour, count):
    return gather_fact(n_dp, n_seq, log2(n_dp)) + flavour * count


def facts_table(n_dp, n_seq, group, places):
    table = []
    for d in range(n_dp):
        for s in range(n_seq):
            core = d & 1
            bit = lambda steps: ((d if steps[core][0] == "dp" else s) >> steps[core][1]) & 1
            row = [core, s, s * group]
            for flavour in range(2):
                row += [bit(steps) for steps in zip(*stage_orders(n_dp, n_seq, flavour))]
            row += [bit(steps) for steps in gather_steps(n_dp)] + [0]
            assert len(row) == places_fact(n_dp, n_seq, 0, 0)
            for flavour in range(2):
                row += list(places[flavour][core])
            table.append(row)
    return np.array(table, np.int32)


CORE = (("dp", 0), ("dp", 0))


class Chunk:
    def __init__(self, flavour):
        self.sizes = lax.axis_size("dp"), lax.axis_size("seq")
        self.flavour = flavour
        self.stages = list(zip(*stage_orders(*self.sizes, flavour)))
        self.done = 0

    def bit(self):
        return stage_fact(*self.sizes, self.flavour, self.done)

    def between_cores(self, *parts):
        self.got = [swap(part, CORE) for part in parts]

    def go(self, send, keep):
        self.keep = keep
        self.got = swap(send, self.stages[self.done])
        self.done += 1

    @property
    def last(self):
        return self.done == len(self.stages)


def advance(facts, *chunks, us=8, after=()):
    parts = add_and_cut(facts, [(chunk.keep, chunk.got, chunk.bit()) for chunk in chunks], us, after)
    for chunk, (send, keep) in zip(chunks, parts):
        chunk.go(send, keep)
    return parts[0][0]


def merge(facts, *chunks, us, after=()):
    whole = Chunk(chunks[0].flavour)
    whole.done = chunks[0].done
    pieces = [(chunk.keep, chunk.got) for chunk in chunks]
    whole.go(*merge_and_cut(facts, pieces, whole.bit(), us, after))
    return whole


def finish_kernel(*refs):
    out_ref, first = refs[-1], 0
    for keep_ref, got_ref in zip(refs[:-1:2], refs[1:-1:2]):
        columns = keep_ref.shape[2]
        total = keep_ref[...].astype(F32) + got_ref[...].astype(F32)
        out_ref[:, :, first : first + columns] = total.astype(BF16)
        first += columns


def finish(*chunks, us=8, after=()):
    kinds, part, _ = chunks[0].keep.shape
    inputs = [(array, full(*array.shape)) for chunk in chunks for array in (chunk.keep, chunk.got)]
    shape = (kinds, part, sum(chunk.keep.shape[2] for chunk in chunks))
    return launch(finish_kernel, "finish", (1,), [], inputs, [(shape, BF16, full(*shape))], us=us, after=after)[0]


def join_kernel(facts_ref, value_ref, got_ref, out_ref, *, bit):
    count = value_ref.shape[1]
    first = facts_ref[bit] * count
    out_ref[:, pl.ds(first, count)] = value_ref[...]
    out_ref[:, pl.ds(count - first, count)] = got_ref[...]


class Gather:
    def __init__(self, facts, value):
        self.facts = facts
        n_dp = lax.axis_size("dp")
        self.dims = [("dp", bit) for bit in range(1, log2(n_dp))]
        self.steps = gather_steps(n_dp)
        self.kinds, self.part, self.columns = value.shape
        self.value = value[:, None]
        self.done = 0
        self.send()

    @property
    def last(self):
        return self.done == len(self.steps)

    def send(self):
        self.got = swap(self.value, CORE if self.last else self.steps[self.done])

    def step(self, us=8, after=()):
        bit = gather_fact(lax.axis_size("dp"), lax.axis_size("seq"), self.done)
        kinds, count, part, columns = self.value.shape
        spec = lambda count: pl.BlockSpec((kinds, count, part, half_of(columns)), lambda j, *_: (0, 0, 0, j))
        (self.value,) = launch(
            functools.partial(join_kernel, bit=bit),
            "join",
            (2,),
            [self.facts],
            [(self.value, spec(count)), (self.got, spec(count))],
            [((kinds, 2 * count, part, columns), BF16, spec(2 * count))],
            us=us,
            after=after,
        )
        self.done += 1
        self.send()
        return self.value

    def whole(self):
        dims = self.dims
        core = lax.axis_index("dp") & 1
        halves = []
        for which, order in enumerate((dims[::-1], dims)):
            half = jnp.where(core == which, self.value, self.got)
            half = half.reshape((self.kinds,) + (2,) * len(dims) + (self.part, self.columns))
            wanted = [1 + order[::-1].index(step) for step in dims[::-1]]
            halves.append(half.transpose([0] + wanted + [len(dims) + 1, len(dims) + 2]))
        whole = jnp.stack(halves, axis=len(dims) + 1)
        return whole.reshape(self.kinds, lax.axis_size("dp") * self.part, self.columns)


def natural_rows(facts_ref, own_ref, got_ref, kind, step, columns):
    pieces = []
    for x in range(2):
        for which in range(2):
            index = x * 2 + step if which == 0 else step * 2 + x
            own, got = own_ref[kind, index, :, columns], got_ref[kind, index, :, columns]
            pieces.append(jnp.where(facts_ref[CORE_INDEX] == which, own, got))
    return jnp.concatenate(pieces, axis=0).astype(F32)


def row_sums(value):
    total = jnp.sum(value, axis=1, keepdims=True)
    return jnp.broadcast_to(total, (total.shape[0], LANES)).T[:1, :]


def put_ff_kernel(facts_ref, own_ref, got_ref, w_ref, gain_ref, gate_up_ref, down_ref, out_ref, dgain_ref):
    step = pl.program_id(0)
    rows = lambda kind: natural_rows(facts_ref, own_ref, got_ref, kind, step, slice(0, FF))
    wide = out_ref.shape[1]
    for kind in range(3):
        count = min(OUT_WIDE, wide - kind * OUT_WIDE)
        columns = slice(FF_WIDE, FF_WIDE + count)
        part = natural_rows(facts_ref, own_ref, got_ref, kind, step, columns)
        out_ref[:, kind * OUT_WIDE : kind * OUT_WIDE + count] = part
    down_ref[...] = rows(0).T
    gate, up = rows(1), rows(2)
    gate_up_ref[:, :FF] = gate
    gate_up_ref[:, FF:] = up
    weight = w_ref[...].astype(F32)
    total = row_sums(gate * weight[:, :FF]) + row_sums(up * weight[:, FF:])
    dgain_ref[...] = total / gain_ref[...]


def put_ff(gather, w_gate_up, gain, after=()):
    kept, width = 8 * gather.part, gain.shape[0]
    half = kept // 2
    whole = full(*gather.value.shape)
    return launch(
        put_ff_kernel,
        "put_ff",
        (2,),
        [gather.facts],
        [
            (gather.value, whole),
            (gather.got, whole),
            (w_gate_up, pl.BlockSpec((half, 2 * FF), lambda j, facts: (2 * facts[SEQ_INDEX] + j, 0))),
            (gain[None], pl.BlockSpec((1, half), lambda j, facts: (0, 2 * facts[SEQ_INDEX] + j))),
        ],
        [
            ((kept, 2 * FF), F32, pl.BlockSpec((half, 2 * FF), lambda j, *_: (j, 0))),
            ((FF, kept), F32, pl.BlockSpec((FF, half), lambda j, *_: (0, j))),
            ((kept, width), F32, pl.BlockSpec((half, width), lambda j, *_: (j, 0))),
            ((1, kept), F32, pl.BlockSpec((1, half), lambda j, *_: (0, j))),
        ],
        us=8,
        after=after,
    )


def put_att_kernel(facts_ref, own_ref, got_ref, w_ref, gain_ref, qkv_ref, dgain_ref):
    qkv = natural_rows(facts_ref, own_ref, got_ref, 0, pl.program_id(0), slice(0, qkv_ref.shape[1]))
    qkv_ref[...] = qkv
    dgain_ref[...] = row_sums(qkv * w_ref[...].astype(F32)) / gain_ref[...]


def put_att(gather, w_qkv, gain, after=()):
    kept, columns = 8 * gather.part, gather.columns
    half = kept // 2
    whole = full(*gather.value.shape)
    return launch(
        put_att_kernel,
        "put_att",
        (2,),
        [gather.facts],
        [
            (gather.value, whole),
            (gather.got, whole),
            (w_qkv, pl.BlockSpec((half, columns), lambda j, facts: (2 * facts[SEQ_INDEX] + j, 0))),
            (gain[None], pl.BlockSpec((1, half), lambda j, facts: (0, 2 * facts[SEQ_INDEX] + j))),
        ],
        [
            ((kept, columns), F32, pl.BlockSpec((half, columns), lambda j, *_: (j, 0))),
            ((1, kept), F32, pl.BlockSpec((1, half), lambda j, *_: (0, j))),
        ],
        us=8,
        after=after,
    )


def place_rows(turned, places):
    count = places.shape[0]
    blocks = turned.reshape((count, turned.shape[0] // count) + turned.shape[1:])
    return jnp.zeros_like(blocks).at[places].set(blocks).reshape(turned.shape)


def shifted(value, axis, steps):
    count = lax.axis_size(axis)
    leading, last = (max(0, -steps), min(count, count - steps))
    return lax.ppermute(value, axis, [(source, source + steps) for source in range(leading, last)])


def per_device(inputs, w_qkv, w_out, w_gate_up, w_down, gain_attn, gain_mlp, doc_start, cotangent):
    n_dp, n_seq = lax.axis_size("dp"), lax.axis_size("seq")
    rows, group, width = inputs.shape
    tokens = rows * group
    slab = width // (n_dp * n_seq)
    places = [block_places(n_dp, n_seq, flavour) for flavour in range(2)]
    ordered = slab % 16 == 0
    if not ordered:
        slab = 32
    blocks = width // slab
    listed = places if ordered else [[np.arange(blocks)] * 2] * 2
    table = facts_table(n_dp, n_seq, group, listed)
    device = lax.axis_index("dp") * n_seq + lax.axis_index("seq")
    facts = lax.dynamic_index_in_dim(jnp.asarray(table), device, axis=0, keepdims=False)
    put = [places_fact(n_dp, n_seq, flavour, blocks) for flavour in range(2)]
    core = lax.axis_index("dp") & 1

    def in_order(turned, flavour):
        if ordered:
            return turned
        return place_rows(turned, jnp.where(core == 0, *places[flavour]))

    x = inputs.reshape(tokens, width)
    dy = cotangent.reshape(tokens, width)

    tails = [(row + 1) * group for row in range(rows)]
    x_rim = shifted(inputs[:, group - WINDOW :], "seq", 1).reshape(rows * WINDOW, width)
    qkv, one_turned, dy_turned = norm_matmul(x, gain_attn, w_qkv, 0, facts, put[1], slab, dy)
    kv_rim, rim_turned = norm_matmul(x_rim, gain_attn, w_qkv, width, facts, put[1], slab, after=[qkv])
    att, att_turned = attend(qkv, kv_rim, doc_start, facts, put[1], slab)
    resid, normed_two, two_turned = out_proj(att, w_out, x, gain_mlp, facts, put[1], slab)
    one_turned, rim_turned, att_turned = [in_order(turned, 1) for turned in (one_turned, rim_turned, att_turned)]
    two_turned, dy_turned = [in_order(turned, 1) for turned in (two_turned, dy_turned)]

    def feed(first, count, total=None, end=None, after=()):
        hidden, dgu, *rest = feed_forward(
            normed_two, dy, dy_turned, two_turned, w_gate_up, w_down, first, count, total, end, after
        )
        chunk = Chunk(1)
        drb_da, sends = ([], rest[:3]) if end is None else (rest[3:5], rest[:3] + rest[5:])
        chunk.between_cores(*sends)
        return hidden, dgu, chunk, drb_da or rest[3:]

    def keep_ff(chunk, hidden, dgu, out=(), after=()):
        send, keep = ff_grad(facts, chunk.bit(), dy_turned, two_turned, hidden, dgu, chunk.got, out, after)
        chunk.go(send, keep)
        return send

    count = FF_CHUNKS[0]
    hidden_one, dgu_one, one, (total,) = feed(0, count)
    token = keep_ff(one, hidden_one, dgu_one)
    hidden_two, dgu_two, two, (drb, da) = feed(count, FF_CHUNKS[1], total, (resid, gain_mlp, w_out, att_turned), after=[token])
    token = advance(facts, one, after=[da])
    token = keep_ff(two, hidden_two, dgu_two, (att_turned, drb), after=[token])
    dqkv, drim = attend_back(qkv, kv_rim, doc_start, facts, da, after=[token])
    att = Chunk(1)
    grads = (facts, one_turned, rim_turned, dqkv, drim)
    (send,) = att_grad(*grads, us=20, after=[one.got])
    att.between_cores(send)
    token = advance(facts, one, two, us=30, after=[send])
    back = rim_grad(drim, w_qkv, x_rim, gain_attn, after=[token])
    back_got = shifted(back, "seq", -1)
    send, keep = att_grad(*grads, att.bit(), att.got[0], us=4, after=[back])
    att.go(send[None], keep[None])
    token = advance(facts, one, two, us=1, after=[send])
    grad_inputs = input_grad(dqkv, w_qkv, x, gain_attn, drb, back_got, tails, us=15, after=[token])
    token = advance(facts, att, two, after=[grad_inputs])
    while not (one.last and two.last):
        token = advance(facts, *(chunk for chunk in (one, two) if not chunk.last), after=[token])
    outputs = ff_out([hidden_one, hidden_two], w_down, resid, us=8, after=[token])
    token = advance(facts, att, after=[outputs])
    gather_ff = Gather(facts, finish(one, two, after=[token]))
    token = gather_ff.value
    while not att.last:
        token = advance(facts, att, after=[token])
    token = gather_ff.step(after=[token])
    gather = Gather(facts, finish(att, after=[token]))
    if ordered and n_dp == 8:
        token = gather.step(us=1, after=[gather.value])
        token = gather_ff.step(after=[token])
        token = gather.step(us=24, after=[token])
        total_gate_up, turned_down, total_out, gain_two = put_ff(gather_ff, w_gate_up, gain_mlp, after=[token])
        total_down = turned_down.T
        total_qkv, gain_one = put_att(gather, w_qkv, gain_attn, after=[total_gate_up])
        gain_one, gain_two = gain_one[0], gain_two[0]
    else:
        for both in (gather_ff, gather):
            while not both.last:
                both.step()
        total_ff = gather_ff.whole()
        total_qkv = gather.whole()[0].astype(F32)
        total_down, total_gate, total_up = [total_ff[kind, :, :FF] for kind in range(3)]
        total_down = total_down.astype(F32)
        total_gate_up = jnp.concatenate([total_gate, total_up], axis=1).astype(F32)
        outs = [total_ff[kind, :, FF_WIDE:] for kind in range(3)]
        total_out = jnp.concatenate(outs, axis=1)[:, :width].astype(F32)
        kept = total_qkv.shape[0]
        first_row = lax.axis_index("seq") * kept

        def gain_total(total, weight, gain):
            mine = lax.dynamic_slice_in_dim(weight, first_row, kept, axis=0).astype(F32)
            return jnp.sum(total * mine, axis=1) / lax.dynamic_slice_in_dim(gain, first_row, kept)

        gain_one = gain_total(total_qkv, w_qkv, gain_attn)
        gain_two = gain_total(total_gate_up, w_gate_up, gain_mlp)

    return (
        outputs.reshape(rows, group, width),
        grad_inputs.reshape(rows, group, width),
        total_qkv,
        total_out,
        total_gate_up,
        total_down,
        gain_one,
        gain_two,
    )


def solution(mesh):
    in_specs = (
        P("dp", "seq", None),
        P(),
        P(),
        P(),
        P(),
        P(),
        P(),
        P("dp", "seq"),
        P("dp", "seq", None),
    )
    out_specs = (
        P("dp", "seq", None),
        P("dp", "seq", None),
        P("seq", None),
        P("seq", None),
        P("seq", None),
        P("seq", None),
        P("seq"),
        P("seq"),
    )
    return jax.shard_map(
        per_device, mesh=mesh, in_specs=in_specs, out_specs=out_specs, check_vma=False
    )
```
